128 devices in a mesh: row: 8 (over x, core), col: 16 (over z, y).
Axes of the slice: x: 4, y: 4, z: 4, core: 2. Of those that a mesh axis runs over, the one named last changes fastest.
Arguments:
- density: bfloat16 [4096, 3, 256], P(('row', 'col')), may hold values from -6 to 6
- coords: bfloat16 [4096, 3, 256], P(('row', 'col')), may hold values from 0 to 1
- basis: bfloat16 [4096, 32, 768], P(('row', 'col')), may hold values from -0.21875 to 0.21875
- transfer: float32 [4096, 32, 32], P(('row', 'col')), may hold values from -1 to 1
- parent: int32 [4096], replicated, may hold values from 0 to 1023
- near_pairs: int32 [2, 16384], P(None, ('row', 'col')), may hold values from 0 to 4095, as said below
- near_count: int32 [128], P(('row', 'col')), may hold values from 16 to 128, as said below
- far_pairs: int32 [2, 8192], P(None, ('row', 'col')), may hold values from 0 to 1023
- coupling: float32 [8192, 32, 32], P(('row', 'col')), may hold values from -1 to 1
Outputs:
- velocity: float32 [4096, 3, 256], P(('row', 'col'))
The draws below stay inside these ranges and needn't reach their ends.
Inputs may be any that keep to these rules, and one draw needn't show every extreme that they name: `near_pairs`: let i = j % 128 for slot j of device (r, c), owners in row-major order with 32 clusters each. The first cluster is owned by device (r, i // (128 // 16)) and the second by device (i // (128 // 8), c); the two may be equal. Slots past a device's live count hold valid but unused pairs. `near_count`: the largest live count equals 128 in every draw.
All inputs are finite; a program needn't handle non-finite values.
Results may differ from the reference program's by a relative error of at most 0.0026.
Values may be sent and summed in bfloat16 or wider, within the bound.
No kernel may reach another device: no remote copies, remote signals or barrier semaphores. Data moves between devices by JAX's collectives and lax.ppermute only.
A program may use at most 64 MiB of HBM per device.

```python
import math
import jax
import jax.numpy as jnp
from jax import lax

CL = 256
R = 32
CPD = 32
NC = 4096
NPAR = 1024
NP_DEV = 128
NF = 8192
N_ROW = 8
N_COL = 16


def draw_near_pairs(key, part):
    key = jax.random.fold_in(key, 7)
    devices = N_ROW * N_COL
    row_span = CPD * N_COL
    slots = jnp.arange(devices * NP_DEV, dtype=jnp.int32)
    owner = slots // NP_DEV
    within_dev = slots % NP_DEV
    owner_row = owner // N_COL
    owner_col = owner % N_COL
    dest_col = within_dev // (NP_DEV // N_COL)
    dest_row = within_dev // (NP_DEV // N_ROW)
    key_first, key_inner = jax.random.split(key, 2)
    first_ids = owner_row * row_span + dest_col * CPD + jax.random.randint(key_first, slots.shape, 0, CPD, dtype=jnp.int32)
    second_ids = dest_row * row_span + owner_col * CPD + jax.random.randint(key_inner, slots.shape, 0, CPD, dtype=jnp.int32)
    return jnp.stack([first_ids, second_ids]).astype(jnp.int32)


def draw_near_count(key, part):
    key = jax.random.fold_in(key, 11)
    devices = N_ROW * N_COL
    key_counts, key_full = jax.random.split(key)
    counts = jax.random.randint(key_counts, (devices,), NP_DEV // 8, NP_DEV // 2 + 1, dtype=jnp.int32)
    fullest = jax.random.randint(key_full, (), 0, devices, dtype=jnp.int32)
    return jnp.where(jnp.arange(devices, dtype=jnp.int32) == fullest, NP_DEV, counts).astype(jnp.int32)


def plant(values, own_key, smallest, high):
    spot = [jax.random.randint(jax.random.fold_in(own_key, axis), (), 0, length) for axis, length in enumerate(values.shape)]
    widest = values.shape.index(max(values.shape))
    next_to = spot[:widest] + [(spot[widest] + 1) % values.shape[widest]] + spot[widest + 1:]
    return values.at[tuple(spot)].set(smallest).at[tuple(next_to)].set(high)


def steps_of(stream_key, extent, cuts, least, top_value):
    gain, own = 1.0, jax.random.fold_in(stream_key, 6)
    for position, shards_of in cuts:
        draws = jnp.exp(jax.random.uniform(jax.random.fold_in(own, position), (shards_of,), jnp.float32, least / len(cuts), top_value / len(cuts)))
        gain = gain * jnp.repeat(draws, extent[position] // shards_of).reshape([-1 if axis == position else 1 for axis in range(len(extent))])
    return gain


def bell_draw(key, extent, scale, reach, pieces=(), kind=jnp.bfloat16):
    factor_of = steps_of(key, extent, pieces, -0.22, 0.18) if pieces else 1.0
    result = jax.random.normal(key, extent, jnp.float32) * scale * factor_of
    return jnp.minimum(jnp.maximum(result, -reach), reach).astype(kind)


def setup_inputs(seed: int = 0) -> dict:
    keys = jax.random.split(jax.random.key(seed), 10)
    return {
        "density": bell_draw(keys[0], (NC, 3, CL), 1.0, 6.0, ((0, 128),)),
        "coords": jnp.clip(1.0 * jax.random.uniform(keys[1], (NC, 3, CL), jnp.float32) ** steps_of(keys[1], (NC, 3, CL), ((0, 128),), -0.2, 0.2), 0.0, 1.0).astype(jnp.bfloat16),
        "basis": bell_draw(keys[2], (NC, R, 3 * CL), (3 * CL) ** -0.5, 0.21875, ((0, 128),)),
        "transfer": bell_draw(keys[3], (NC, R, R), R ** -0.5, 1.0, ((0, 128),), jnp.float32),
        "parent": plant(jax.random.randint(keys[4], (NC,), 0, NPAR), jax.random.fold_in(keys[4], 1), 0, NPAR - 1).astype(jnp.int32),
        "near_pairs": draw_near_pairs(jax.random.fold_in(keys[9], 71), 0),
        "near_count": draw_near_count(jax.random.fold_in(keys[9], 71), 0),
        "far_pairs": plant(jax.random.randint(keys[7], (2, NF), 0, NPAR), jax.random.fold_in(keys[7], 1), 0, NPAR - 1).astype(jnp.int32),
        "coupling": bell_draw(keys[8], (NF, R, R), R ** -0.5, 1.0, ((0, 128),), jnp.float32),
    }


REG_EPS = 0.02
STOKES_SCALE = 1.0 / (8.0 * math.pi)

def stokeslet(near_x, far_x):
    offset = near_x[:, :, :, None] - far_x[:, :, None, :]
    dist_sq = lax.optimization_barrier(jnp.sum(offset * offset, axis=1))
    inv_dist = lax.rsqrt(dist_sq + REG_EPS * REG_EPS)
    inv_cube = inv_dist * inv_dist * inv_dist
    isotropic = (dist_sq + 2.0 * REG_EPS * REG_EPS) * inv_cube
    dyadic = offset[:, :, None] * offset[:, None, :] * inv_cube[:, None, None]
    identity = jnp.eye(3, dtype=jnp.float32)
    return (dyadic + identity[None, :, :, None, None] * isotropic[:, None, None]) * STOKES_SCALE

def near_field(density, coords, near_pairs, near_count):
    accumulated = jnp.zeros((NC, 3, CL), jnp.float32)

    def per_device(accumulated, device):
        live_pairs = near_count[device]

        def per_block(slot_block, accumulated):
            first_slot = (device * NP_DEV + slot_block * 4).astype(jnp.int32)
            glob_a = lax.dynamic_slice_in_dim(near_pairs[0], first_slot, 4)
            glob_b = lax.dynamic_slice_in_dim(near_pairs[1], first_slot, 4)
            within = slot_block * 4 + jnp.arange(4, dtype=jnp.int32) < live_pairs
            row_keep = within.astype(jnp.float32)
            col_keep = (within & (glob_a != glob_b)).astype(jnp.float32)
            kernel_tile = stokeslet(coords[glob_a].astype(jnp.float32), coords[glob_b].astype(jnp.float32))
            kernel_tile = lax.optimization_barrier(kernel_tile.astype(jnp.bfloat16)).astype(jnp.float32)
            source_a = density[glob_a].astype(jnp.float32)
            source_b = density[glob_b].astype(jnp.float32)
            to_first = jnp.einsum('pijxy,pjy->pix', kernel_tile, source_b) * row_keep[:, None, None]
            to_second = jnp.einsum('pijxy,pix->pjy', kernel_tile, source_a) * col_keep[:, None, None]
            return accumulated.at[glob_a].add(to_first).at[glob_b].add(to_second)
        return (lax.fori_loop(0, (live_pairs + 3) // 4, per_block, accumulated), None)
    accumulated, unused = lax.scan(per_device, accumulated, jnp.arange(N_ROW * N_COL, dtype=jnp.int32))
    return accumulated

def far_field(density, basis, transfer, parent, far_pairs, coupling):
    highest = lax.Precision.HIGHEST
    basis_wide = basis.astype(jnp.float32)
    moments = jnp.einsum('crk,ck->cr', basis_wide, density.reshape(NC, 3 * CL).astype(jnp.float32), precision=highest)
    lifted = jnp.einsum('crs,cs->cr', transfer, moments, precision=highest)
    parent_moments = jnp.zeros((NPAR, R), jnp.float32).at[parent].add(lifted)
    to_first = jnp.einsum('krs,ks->kr', coupling, parent_moments[far_pairs[1]], precision=highest)
    to_second = jnp.einsum('ksr,ks->kr', coupling, parent_moments[far_pairs[0]], precision=highest)
    parent_locals = jnp.zeros((NPAR, R), jnp.float32).at[far_pairs[0]].add(to_first).at[far_pairs[1]].add(to_second)
    local_coef = jnp.einsum('csr,cs->cr', transfer, parent_locals[parent], precision=highest)
    return jnp.einsum('crk,cr->ck', basis_wide, local_coef, precision=highest).reshape(NC, 3, CL)

def reference(density, coords, basis, transfer, parent, near_pairs, near_count, far_pairs, coupling):
    near = near_field(density, coords, near_pairs, near_count)
    return near + far_field(density, basis, transfer, parent, far_pairs, coupling)
```

```python
import functools
import math

import jax
import jax.numpy as jnp
from jax import lax
from jax.experimental import pallas as pl
from jax.experimental.pallas import tpu as pltpu
from jax.sharding import PartitionSpec as P

REG_EPS = 0.02
EPS_SQ = REG_EPS * REG_EPS
STOKES_SCALE = 1.0 / (8.0 * math.pi)
BOTH = ("row", "col")
GROUP = 16
PANELS = 256
FIELD_ROWS = 40
POINT_ROWS = 16
f32, bf16 = jnp.float32, jnp.bfloat16


def pieces(value, count):
    out = []
    for _ in range(count):
        head = value.astype(bf16).astype(f32)
        out.append(head)
        value = value - head
    return out


def put(ref, row, value):
    for half in range(2):
        ref[half, row * GROUP : (row + 1) * GROUP, :] = value[:, half * 128 : (half + 1) * 128]


def get(ref, row):
    return jnp.concatenate([ref[half, row * GROUP : (row + 1) * GROUP, :] for half in range(2)], 1)


def split_parts(block):
    parts = [block[:, k * PANELS : (k + 1) * PANELS] for k in range(6)]
    return parts[:3], parts[3:]


def prepare(block, field, left, right):
    q, y = split_parts(block)
    one, zero = jnp.ones_like(q[0]), jnp.zeros_like(q[0])
    norm = pieces(y[0] * y[0] + y[1] * y[1] + y[2] * y[2] + EPS_SQ / 2, 3)
    along = y[0] * q[0] + y[1] * q[1] + y[2] * q[2]
    rows = list(q) + pieces(along, 3)
    for i in range(3):
        for j in range(3):
            rows += pieces(y[i] * q[j], 2)
    for i in range(3):
        rows += pieces(y[i] * along, 3)
    rows += [zero] * (FIELD_ROWS - len(rows))
    for k, value in enumerate(rows):
        put(field, k, value)
    for k, value in enumerate([-2 * v for v in y] + norm + [one] * 3 + [zero] * 7):
        put(left, k, value)
    for k, value in enumerate(y + [one] * 3 + norm + [zero] * 7):
        put(right, k, value)


def finish(block, sums, point_sums):
    _, x = split_parts(block)
    mom = [get(sums, i) for i in range(3)]
    dot = x[0] * mom[0] + x[1] * mom[1] + x[2] * mom[2] - (get(sums, 3) + get(sums, 4) + get(sums, 5))
    out = []
    for i in range(3):
        cross = sum(x[j] * (get(sums, 6 + 2 * (3 * i + j)) + get(sums, 7 + 2 * (3 * i + j))) for j in range(3))
        tail = get(sums, 24 + 3 * i) + get(sums, 25 + 3 * i) + get(sums, 26 + 3 * i)
        total = get(point_sums, i) + EPS_SQ * mom[i] + ((x[i] * dot - cross) + tail)
        out.append(total * STOKES_SCALE)
    return out


def near_kernel(a_ref, b_ref, to_a, to_b, fa, la, ra, fb, lb, rb, sum_a, pt_a, sum_b, pt_b):
    def group(g, carry):
        rows = pl.ds(pl.multiple_of(g * GROUP, GROUP), GROUP)
        block_a, block_b = a_ref[rows, :].astype(f32), b_ref[rows, :].astype(f32)
        prepare(block_a, fa, la, ra)
        prepare(block_b, fb, lb, rb)

        def slot(s, carry):
            def load(ref, count):
                return jnp.concatenate(
                    [ref[half, pl.ds(s, count, stride=GROUP), :] for half in range(2)], 1
                ).astype(bf16)

            def store(ref, count, value):
                for half in range(2):
                    ref[half, pl.ds(s, count, stride=GROUP), :] = value[:, half * 128 : (half + 1) * 128]

            def one_way(field, left, right, sums, point_sums):
                shifted = lax.dot_general(
                    load(left, POINT_ROWS),
                    load(right, POINT_ROWS),
                    (((0,), (0,)), ((), ())),
                    preferred_element_type=f32,
                )
                inv = lax.rsqrt(shifted)
                cube = inv * inv * inv
                source = load(field, FIELD_ROWS)
                store(sums, FIELD_ROWS, jnp.dot(source, cube.astype(bf16), preferred_element_type=f32))
                store(point_sums, 8, jnp.dot(source[:8], inv.astype(bf16), preferred_element_type=f32))

            one_way(fa, la, rb, sum_b, pt_b)
            one_way(fb, lb, ra, sum_a, pt_a)
            return carry

        lax.fori_loop(0, GROUP, slot, 0, unroll=4)
        for out, block, sums, point_sums in ((to_a, block_a, sum_a, pt_a), (to_b, block_b, sum_b, pt_b)):
            for i, value in enumerate(finish(block, sums, point_sums)):
                out[rows, i * PANELS : (i + 1) * PANELS] = value
        return carry

    lax.fori_loop(0, a_ref.shape[0] // GROUP, group, 0)


def near_products(first, second):
    slots = first.shape[0]
    vmem = pl.BlockSpec(memory_space=pltpu.VMEM)

    def rows(count):
        return pltpu.VMEM((2, count * GROUP, 128), f32)

    return pl.pallas_call(
        near_kernel,
        out_shape=[jax.ShapeDtypeStruct((slots, 3 * PANELS), f32)] * 2,
        in_specs=[vmem] * 2,
        out_specs=[vmem] * 2,
        scratch_shapes=[rows(FIELD_ROWS), rows(POINT_ROWS), rows(POINT_ROWS)] * 2
        + [rows(FIELD_ROWS), rows(8)] * 2,
        compiler_params=pltpu.CompilerParams(vmem_limit_bytes=32 << 20),
        cost_estimate=pl.CostEstimate(
            flops=slots * 2 * 2 * 64 * PANELS * PANELS, bytes_accessed=slots * 9216, transcendentals=0
        ),
    )(first, second)


def one_hot(ids, count):
    return (ids[:, None] == jnp.arange(count, dtype=ids.dtype)[None, :]).astype(f32)


def shards(density, coords, basis, transfer, parent, near_pairs, near_count, far_pairs, coupling):
    highest = lax.Precision.HIGHEST
    own, _, panels = density.shape
    rank = basis.shape[1]
    rows, cols = lax.axis_size("row"), lax.axis_size("col")
    devices, half = rows * cols, cols // rows
    my_row, my_col = lax.axis_index("row"), lax.axis_index("col")
    slots = near_pairs.shape[1]
    per_pair = slots // cols

    swap = [
        (r * cols + half * p + h, p * cols + half * r + h)
        for r in range(rows)
        for p in range(rows)
        for h in range(half)
    ]
    flat = density.reshape(own, 3 * panels)
    data = jnp.concatenate([flat, coords.reshape(own, 3 * panels)], axis=1)
    first_data = lax.ppermute(data, BOTH, swap)

    moments = jnp.einsum("crk,ck->cr", basis, flat, preferred_element_type=f32)
    lifted = jnp.einsum("crs,cs->cr", transfer, moments, precision=highest)
    ids = (near_pairs % own).astype(f32)
    live = jnp.arange(slots) < near_count[0]
    message = jnp.concatenate(
        [lifted.reshape(-1, 128), jnp.where(live, ids[0], -1.0)[None], ids[1][None]], axis=0
    )
    lift_rows = message.shape[0] - 2
    everyone = lax.all_to_all(
        jnp.broadcast_to(message[None], (devices,) + message.shape), BOTH, 0, 0, tiled=True
    )

    table = everyone[:, lift_rows:, :].reshape(rows, cols, 2, rows, half * per_pair)
    mine = lax.dynamic_index_in_dim(table, my_col, 1, keepdims=False)
    mine = lax.dynamic_index_in_dim(mine, my_row, 2, keepdims=False)
    own_first, own_second = mine[:, 0].reshape(-1), mine[:, 1].reshape(-1)
    same_place = (jnp.arange(rows)[:, None] == my_row) & (
        half * my_row + jnp.arange(half * per_pair)[None, :] // per_pair == my_col
    )
    back_ids = jnp.where(
        (own_first < 0) | (same_place.reshape(-1) & (own_first == own_second)), -1.0, own_second
    )
    picked = jnp.dot(
        one_hot(own_second, own).astype(bf16), data, preferred_element_type=f32
    ).astype(bf16)
    second = lax.all_to_all(picked, "col", 0, 0, tiled=True)

    held = lax.dynamic_index_in_dim(table, my_col // half, 0, keepdims=False)
    held = lax.dynamic_index_in_dim(held, my_row, 2, keepdims=False)[:, 0]
    held = lax.dynamic_slice_in_dim(held, my_col % half * per_pair, per_pair, 1).reshape(-1)
    first_hot = one_hot(held, own)
    first = jnp.dot(first_hot.astype(bf16), first_data, preferred_element_type=f32).astype(bf16)
    to_first, to_second = near_products(first, second)
    near_first = lax.ppermute(
        jnp.einsum("sc,sk->ck", first_hot, to_first, precision=highest), BOTH, swap
    )
    returned = lax.all_to_all(to_second, "col", 0, 0, tiled=True)
    near_second = jnp.einsum("sc,sk->ck", one_hot(back_ids, own), returned, precision=highest)

    per_lane = 128 // rank
    all_lifted = everyone[:, :lift_rows, :].reshape(-1, 128)
    parents = parent.reshape(-1, per_lane)
    ends = far_pairs.reshape(-1)
    hits = (parents.T[:, None, :] == ends[None, :, None]).astype(f32)
    found = jnp.einsum("mkn,nl->mkl", hits, all_lifted, precision=highest)
    at_ends = sum(found[m, :, m * rank : (m + 1) * rank] for m in range(per_lane))
    count = far_pairs.shape[1]
    sent_first = jnp.einsum("krs,ks->kr", coupling, at_ends[count:], precision=highest)
    sent_second = jnp.einsum("ksr,ks->kr", coupling, at_ends[:count], precision=highest)
    sent = jnp.concatenate([sent_first, sent_second], axis=0)
    partial = jnp.concatenate(
        [jnp.einsum("kn,kr->nr", hits[m], sent, precision=highest) for m in range(per_lane)], axis=1
    )
    gathered = lax.all_to_all(partial.reshape(devices, lift_rows, 128), BOTH, 0, 0, tiled=True)
    parent_locals = jnp.sum(gathered, axis=0).reshape(own, rank)
    local_coef = jnp.einsum("csr,cs->cr", transfer, parent_locals, precision=highest)
    far_part = jnp.einsum("crk,cr->ck", basis.astype(f32), local_coef, precision=highest)
    return (near_first + near_second + far_part).reshape(own, 3, panels)


def solution(mesh):
    placed = (
        P(BOTH, None, None),
        P(BOTH, None, None),
        P(BOTH, None, None),
        P(BOTH, None, None),
        P(),
        P(None, BOTH),
        P(BOTH),
        P(None, BOTH),
        P(BOTH, None, None),
    )
    return jax.shard_map(
        shards, mesh=mesh, in_specs=placed, out_specs=P(BOTH, None, None), check_vma=False
    )
```

```python
import functools
import math

import jax
import jax.numpy as jnp
from jax import lax
from jax.experimental import pallas as pl
from jax.experimental.pallas import tpu as pltpu
from jax.sharding import PartitionSpec as P

REG_EPS = 0.02
EPS_SQ = REG_EPS * REG_EPS
STOKES_SCALE = 1.0 / (8.0 * math.pi)
BOTH = ("row", "col")
GROUP = 16
PANELS = 256
FIELD_ROWS = 40
POINT_ROWS = 16
f32, bf16 = jnp.float32, jnp.bfloat16


def pieces(value, count):
    out = []
    for _ in range(count):
        head = value.astype(bf16).astype(f32)
        out.append(head)
        value = value - head
    return out


def put(ref, row, value):
    for half in range(2):
        ref[half, row * GROUP : (row + 1) * GROUP, :] = value[:, half * 128 : (half + 1) * 128]


def get(ref, row):
    return jnp.concatenate([ref[half, row * GROUP : (row + 1) * GROUP, :] for half in range(2)], 1)


def split_parts(block):
    parts = [block[:, k * PANELS : (k + 1) * PANELS] for k in range(6)]
    return parts[:3], parts[3:]


def prepare(block, field, left, right):
    q, y = split_parts(block)
    one, zero = jnp.ones_like(q[0]), jnp.zeros_like(q[0])
    norm = pieces(y[0] * y[0] + y[1] * y[1] + y[2] * y[2] + EPS_SQ / 2, 3)
    along = y[0] * q[0] + y[1] * q[1] + y[2] * q[2]
    rows = list(q) + pieces(along, 3)
    for i in range(3):
        for j in range(3):
            rows += pieces(y[i] * q[j], 2)
    for i in range(3):
        rows += pieces(y[i] * along, 3)
    rows += [zero] * (FIELD_ROWS - len(rows))
    for k, value in enumerate(rows):
        put(field, k, value)
    for k, value in enumerate([-2 * v for v in y] + norm + [one] * 3 + [zero] * 7):
        put(left, k, value)
    for k, value in enumerate(y + [one] * 3 + norm + [zero] * 7):
        put(right, k, value)


def finish(block, sums, point_sums):
    _, x = split_parts(block)
    mom = [get(sums, i) for i in range(3)]
    dot = x[0] * mom[0] + x[1] * mom[1] + x[2] * mom[2] - (get(sums, 3) + get(sums, 4) + get(sums, 5))
    out = []
    for i in range(3):
        cross = sum(x[j] * (get(sums, 6 + 2 * (3 * i + j)) + get(sums, 7 + 2 * (3 * i + j))) for j in range(3))
        tail = get(sums, 24 + 3 * i) + get(sums, 25 + 3 * i) + get(sums, 26 + 3 * i)
        total = get(point_sums, i) + EPS_SQ * mom[i] + ((x[i] * dot - cross) + tail)
        out.append(total * STOKES_SCALE)
    return out


def near_kernel(ids_lane, first_ref, second_ref, near_first, to_second, fa, la, ra, fb, lb, rb, sum_a, pt_a, sum_b, pt_b):
    own = first_ref.shape[0]
    near_first[...] = jnp.zeros_like(near_first)

    def group(g, carry):
        rows = pl.ds(pl.multiple_of(g * GROUP, GROUP), GROUP)
        ids = second_ref[rows, ids_lane : ids_lane + 128].astype(f32)[:, :own]
        chosen = (ids == lax.broadcasted_iota(jnp.int32, (GROUP, own), 1).astype(f32)).astype(bf16)
        block_a = jnp.dot(chosen, first_ref[...], preferred_element_type=f32)
        block_b = second_ref[rows, : 6 * PANELS].astype(f32)
        prepare(block_a, fa, la, ra)
        prepare(block_b, fb, lb, rb)

        def slot(s, carry):
            def load(ref, count):
                return jnp.concatenate(
                    [ref[half, pl.ds(s, count, stride=GROUP), :] for half in range(2)], 1
                ).astype(bf16)

            def store(ref, count, value):
                for half in range(2):
                    ref[half, pl.ds(s, count, stride=GROUP), :] = value[:, half * 128 : (half + 1) * 128]

            def one_way(field, left, right, sums, point_sums):
                shifted = lax.dot_general(
                    load(left, POINT_ROWS),
                    load(right, POINT_ROWS),
                    (((0,), (0,)), ((), ())),
                    preferred_element_type=f32,
                )
                inv = lax.rsqrt(shifted)
                cube = inv * inv * inv
                source = load(field, FIELD_ROWS)
                store(sums, FIELD_ROWS, jnp.dot(source, cube.astype(bf16), preferred_element_type=f32))
                store(point_sums, 8, jnp.dot(source[:8], inv.astype(bf16), preferred_element_type=f32))

            one_way(fa, la, rb, sum_b, pt_b)
            one_way(fb, lb, ra, sum_a, pt_a)
            return carry

        lax.fori_loop(0, GROUP, slot, 0, unroll=GROUP)
        for i, value in enumerate(finish(block_b, sum_b, pt_b)):
            to_second[rows, i * PANELS : (i + 1) * PANELS] = value
        for i, value in enumerate(finish(block_a, sum_a, pt_a)):
            for piece in pieces(value, 3):
                near_first[:, i * PANELS : (i + 1) * PANELS] += lax.dot_general(
                    chosen, piece.astype(bf16), (((0,), (0,)), ((), ())), preferred_element_type=f32
                )
        return carry

    lax.fori_loop(0, second_ref.shape[0] // GROUP, group, 0)


def near_products(first, second, ids_lane):
    slots = second.shape[0]
    vmem = pl.BlockSpec(memory_space=pltpu.VMEM)

    def rows(count):
        return pltpu.VMEM((2, count * GROUP, 128), f32)

    return pl.pallas_call(
        functools.partial(near_kernel, ids_lane),
        out_shape=[
            jax.ShapeDtypeStruct((first.shape[0], 3 * PANELS), f32),
            jax.ShapeDtypeStruct((slots, 3 * PANELS), f32),
        ],
        in_specs=[vmem] * 2,
        out_specs=[vmem] * 2,
        scratch_shapes=[rows(FIELD_ROWS), rows(POINT_ROWS), rows(POINT_ROWS)] * 2
        + [rows(FIELD_ROWS), rows(8)] * 2,
        compiler_params=pltpu.CompilerParams(vmem_limit_bytes=32 << 20),
        cost_estimate=pl.CostEstimate(
            flops=slots * 2 * 2 * 64 * PANELS * PANELS, bytes_accessed=slots * 9216, transcendentals=0
        ),
    )(first, second)


def ends_kernel(start, count, recv, parents, ends, out):
    parts = parents.shape[1]
    sums = [jnp.zeros((ends.shape[0], 256), f32) for _ in range(parts)]
    for r in range(count):
        lifted = recv[:, start + 256 * r : start + 256 * (r + 1)]
        for m in range(parts):
            hit = (parents[r, m : m + 1, :] == ends[...]).astype(f32).astype(bf16)
            sums[m] += jnp.dot(hit, lifted, preferred_element_type=f32)
    lane = lax.broadcasted_iota(jnp.int32, (ends.shape[0], 128), 1)
    width = 128 // parts
    total = jnp.zeros((ends.shape[0], 128), f32)
    for m in range(parts):
        total += jnp.where(lane // width == m, sums[m][:, :128] + sums[m][:, 128:], 0.0)
    out[...] = total


def spread_kernel(parents, ends, sent, out):
    parts = parents.shape[1]
    width = 128 // parts
    lane = lax.broadcasted_iota(jnp.int32, sent.shape, 1)
    head, rest = pieces(sent[...], 2)
    for r in range(out.shape[0] // 128):
        rows = slice(r * 128, (r + 1) * 128)
        total = jnp.zeros((128, 256), f32)
        for m in range(parts):
            hit = (parents[rows, m : m + 1] == ends[...]).astype(f32).astype(bf16)
            here = lane // width == m
            both = jnp.concatenate([jnp.where(here, head, 0.0), jnp.where(here, rest, 0.0)], 1)
            total += jnp.dot(hit, both.astype(bf16), preferred_element_type=f32)
        out[rows, :] = total[:, :128] + total[:, 128:]


def one_hot(ids, count):
    return (ids[:, None] == jnp.arange(count, dtype=ids.dtype)[None, :]).astype(f32)


def shards(density, coords, basis, transfer, parent, near_pairs, near_count, far_pairs, coupling):
    highest = lax.Precision.HIGHEST
    own, _, panels = density.shape
    rank = basis.shape[1]
    rows, cols = lax.axis_size("row"), lax.axis_size("col")
    half = cols // rows
    my_row, my_col = lax.axis_index("row"), lax.axis_index("col")
    slots = near_pairs.shape[1]
    per_pair = slots // cols
    block = slots // rows
    vmem = pl.BlockSpec(memory_space=pltpu.VMEM)

    swap = [
        (r * cols + half * p + h, p * cols + half * r + h)
        for r in range(rows)
        for p in range(rows)
        for h in range(half)
    ]
    flat = density.reshape(own, 3 * panels)
    data = jnp.concatenate([flat, coords.reshape(own, 3 * panels)], axis=1)
    first_data = lax.ppermute(data, BOTH, swap)

    moments = jnp.einsum("crk,ck->cr", basis, flat, preferred_element_type=f32)
    lifted = jnp.einsum("crs,cs->cr", transfer, moments, precision=highest).reshape(-1, 128)
    lift_rows = lifted.shape[0]
    live = jnp.arange(slots) < near_count[0]
    ids = jnp.where(live[None], near_pairs % own, -1).astype(f32)
    ids = ids.reshape(2, rows, block).transpose(1, 0, 2).reshape(rows, 1, 2 * block)
    message = jnp.concatenate(
        [
            jnp.broadcast_to(lifted[None], (rows, lift_rows, 128)),
            jnp.pad(ids, ((0, 0), (0, 0), (0, 128 - 2 * block))),
        ],
        axis=1,
    )
    from_row = lax.all_to_all(message, "row", 0, 0, tiled=True)

    own_first = from_row[:, lift_rows, :block].reshape(-1)
    own_second = from_row[:, lift_rows, block : 2 * block].reshape(-1)
    place = jnp.arange(slots)
    same_owner = (place // block == my_row) & (half * my_row + place % block // per_pair == my_col)
    back_ids = jnp.where(same_owner & (own_first == own_second), -1.0, own_second)
    picked = jnp.dot(one_hot(own_second, own).astype(bf16), data, preferred_element_type=f32)
    head, rest = pieces(from_row[:, :lift_rows, :], 2)
    row_lifted = jnp.stack([head, rest], 2).transpose(1, 0, 2, 3).reshape(lift_rows, -1)
    message = jnp.concatenate(
        [
            picked.astype(bf16),
            jnp.broadcast_to(own_first[:, None], (slots, 128)).astype(bf16),
            jnp.tile(row_lifted.astype(bf16), (cols, 1)),
        ],
        axis=1,
    )
    second = lax.all_to_all(message, "col", 0, 0, tiled=True)
    ids_lane = 6 * panels

    parts = 128 // rank
    by_row = parent.reshape(rows, slots, parts)
    ends = far_pairs.reshape(-1)
    at_ends = pl.pallas_call(
        functools.partial(ends_kernel, ids_lane + 128, rows),
        out_shape=jax.ShapeDtypeStruct((ends.shape[0], 128), f32),
        in_specs=[vmem] * 3,
        out_specs=vmem,
    )(second, by_row.transpose(0, 2, 1), ends[:, None])
    at_ends = at_ends.reshape(-1, parts, rank).sum(axis=1)
    count = far_pairs.shape[1]
    sent_first = jnp.einsum("krs,ks->kr", coupling, at_ends[count:], precision=highest)
    sent_second = jnp.einsum("ksr,ks->kr", coupling, at_ends[:count], precision=highest)
    sent = jnp.tile(jnp.concatenate([sent_first, sent_second], axis=0), (1, parts))
    partial = pl.pallas_call(
        spread_kernel,
        out_shape=jax.ShapeDtypeStruct((rows * slots, 128), f32),
        in_specs=[vmem] * 3,
        out_specs=vmem,
    )(parent.reshape(-1, parts), ends[None], sent)
    row_locals = lax.all_to_all(partial.reshape(rows, slots, 128), "row", 0, 0, tiled=True)

    near_first, to_second = near_products(first_data, second, ids_lane)
    near_first = lax.ppermute(near_first, BOTH, swap)
    returned = lax.all_to_all(
        jnp.concatenate([to_second, row_locals.sum(axis=0)], axis=1), "col", 0, 0, tiled=True
    )
    near_second = jnp.einsum(
        "sc,sk->ck", one_hot(back_ids, own), returned[:, : 3 * panels], precision=highest
    )
    parent_locals = returned[:, 3 * panels :].reshape(cols, lift_rows, 128).sum(axis=0).reshape(own, rank)
    local_coef = jnp.einsum("csr,cs->cr", transfer, parent_locals, precision=highest)
    far_part = jnp.einsum("crk,cr->ck", basis.astype(f32), local_coef, precision=highest)
    return (near_first + near_second + far_part).reshape(own, 3, panels)


def solution(mesh):
    placed = (
        P(BOTH, None, None),
        P(BOTH, None, None),
        P(BOTH, None, None),
        P(BOTH, None, None),
        P(),
        P(None, BOTH),
        P(BOTH),
        P(None, BOTH),
        P(BOTH, None, None),
    )
    return jax.shard_map(
        shards, mesh=mesh, in_specs=placed, out_specs=P(BOTH, None, None), check_vma=False
    )
```

```python
import functools
import math

import jax
import jax.numpy as jnp
from jax import lax
from jax.experimental import pallas as pl
from jax.experimental.pallas import tpu as pltpu
from jax.sharding import PartitionSpec as P

REG_EPS = 0.02
EPS_SQ = REG_EPS * REG_EPS
STOKES_SCALE = 1.0 / (8.0 * math.pi)
BOTH = ("row", "col")
GROUP = 16
PANELS = 256
FIELD_ROWS = 40
POINT_ROWS = 16
f32, bf16 = jnp.float32, jnp.bfloat16


def pieces(value, count):
    out = []
    for _ in range(count):
        head = value.astype(bf16).astype(f32)
        out.append(head)
        value = value - head
    return out


def put(ref, row, value):
    for half in range(2):
        ref[half, row * GROUP : (row + 1) * GROUP, :] = value[:, half * 128 : (half + 1) * 128]


def get(ref, row):
    return jnp.concatenate([ref[half, row * GROUP : (row + 1) * GROUP, :] for half in range(2)], 1)


def split_parts(block):
    parts = [block[:, k * PANELS : (k + 1) * PANELS] for k in range(6)]
    return parts[:3], parts[3:]


def prepare_source(block, field, left):
    q, y = split_parts(block)
    one, zero = jnp.ones_like(q[0]), jnp.zeros_like(q[0])
    norm = pieces(y[0] * y[0] + y[1] * y[1] + y[2] * y[2] + EPS_SQ / 2, 3)
    along = y[0] * q[0] + y[1] * q[1] + y[2] * q[2]
    rows = list(q) + pieces(along, 3)
    for i in range(3):
        for j in range(3):
            rows += pieces(y[i] * q[j], 2)
    for i in range(3):
        rows += pieces(y[i] * along, 3)
    rows += [zero] * (FIELD_ROWS - len(rows))
    for k, value in enumerate(rows):
        put(field, k, value)
    for k, value in enumerate([-2 * v for v in y] + norm + [one] * 3 + [zero] * 7):
        put(left, k, value)


def prepare_target(block, right):
    _, x = split_parts(block)
    one, zero = jnp.ones_like(x[0]), jnp.zeros_like(x[0])
    norm = pieces(x[0] * x[0] + x[1] * x[1] + x[2] * x[2] + EPS_SQ / 2, 3)
    for k, value in enumerate(x + [one] * 3 + norm + [zero] * 7):
        put(right, k, value)


def finish(block, sums, point_sums):
    _, x = split_parts(block)
    mom = [get(sums, i) for i in range(3)]
    dot = x[0] * mom[0] + x[1] * mom[1] + x[2] * mom[2] - (get(sums, 3) + get(sums, 4) + get(sums, 5))
    out = []
    for i in range(3):
        cross = sum(x[j] * (get(sums, 6 + 2 * (3 * i + j)) + get(sums, 7 + 2 * (3 * i + j))) for j in range(3))
        tail = get(sums, 24 + 3 * i) + get(sums, 25 + 3 * i) + get(sums, 26 + 3 * i)
        total = get(point_sums, i) + EPS_SQ * mom[i] + ((x[i] * dot - cross) + tail)
        out.append(total * STOKES_SCALE)
    return out


def near_kernel(ids_lane, to_first, first_ref, second_ref, out, field, left, right, sums, point_sums):
    own = first_ref.shape[0]
    if to_first:
        out[...] = jnp.zeros_like(out)

    def group(g, carry):
        rows = pl.ds(pl.multiple_of(g * GROUP, GROUP), GROUP)
        ids = second_ref[rows, ids_lane : ids_lane + 128].astype(f32)[:, :own]
        chosen = (ids == lax.broadcasted_iota(jnp.int32, (GROUP, own), 1).astype(f32)).astype(bf16)
        first = jnp.dot(chosen, first_ref[...], preferred_element_type=f32)
        second = second_ref[rows, : 6 * PANELS].astype(f32)
        source, target = (second, first) if to_first else (first, second)
        prepare_source(source, field, left)
        prepare_target(target, right)

        def slot(s, carry):
            def load(ref, count):
                return jnp.concatenate(
                    [ref[half, pl.ds(s, count, stride=GROUP), :] for half in range(2)], 1
                ).astype(bf16)

            def store(ref, count, value):
                for half in range(2):
                    ref[half, pl.ds(s, count, stride=GROUP), :] = value[:, half * 128 : (half + 1) * 128]

            shifted = lax.dot_general(
                load(left, POINT_ROWS),
                load(right, POINT_ROWS),
                (((0,), (0,)), ((), ())),
                preferred_element_type=f32,
            )
            inv = lax.rsqrt(shifted)
            cube = inv * inv * inv
            moments = load(field, FIELD_ROWS)
            store(sums, FIELD_ROWS, jnp.dot(moments, cube.astype(bf16), preferred_element_type=f32))
            store(point_sums, 8, jnp.dot(moments[:8], inv.astype(bf16), preferred_element_type=f32))
            return carry

        lax.fori_loop(0, GROUP, slot, 0, unroll=GROUP)
        for i, value in enumerate(finish(target, sums, point_sums)):
            lanes = slice(i * PANELS, (i + 1) * PANELS)
            if not to_first:
                out[rows, lanes] = value
                continue
            for piece in pieces(value, 3):
                out[:, lanes] += lax.dot_general(
                    chosen, piece.astype(bf16), (((0,), (0,)), ((), ())), preferred_element_type=f32
                )
        return carry

    lax.fori_loop(0, second_ref.shape[0] // GROUP, group, 0)


def near_sums(first, second, ids_lane, to_first):
    slots = second.shape[0]
    vmem = pl.BlockSpec(memory_space=pltpu.VMEM)

    def rows(count):
        return pltpu.VMEM((2, count * GROUP, 128), f32)

    return pl.pallas_call(
        functools.partial(near_kernel, ids_lane, to_first),
        out_shape=jax.ShapeDtypeStruct((first.shape[0] if to_first else slots, 3 * PANELS), f32),
        in_specs=[vmem] * 2,
        out_specs=vmem,
        scratch_shapes=[rows(FIELD_ROWS), rows(POINT_ROWS), rows(POINT_ROWS), rows(FIELD_ROWS), rows(8)],
        compiler_params=pltpu.CompilerParams(vmem_limit_bytes=32 << 20),
        cost_estimate=pl.CostEstimate(
            flops=slots * 2 * 64 * PANELS * PANELS, bytes_accessed=slots * 9216, transcendentals=0
        ),
    )(first, second)


def far_kernel(start, recv, parents, ends, factors, out, hits):
    parts = parents.shape[1]
    count = ends.shape[1]
    rank = 128 // parts
    for m in range(parts):
        hits[:, m * count : (m + 1) * count] = (parents[:, m : m + 1] == ends[...]).astype(f32).astype(bf16)
    slots = recv.shape[0]
    found = jnp.zeros((128, parts * count), f32)
    for r in range(hits.shape[0] // slots):
        found += lax.dot_general(
            recv[:, start + 128 * r : start + 128 * (r + 1)],
            hits[r * slots : (r + 1) * slots, :],
            (((0,), (0,)), ((), ())),
            preferred_element_type=f32,
        )
    at_ends = sum(found[m * rank : (m + 1) * rank, m * count : (m + 1) * count] for m in range(parts))
    sent = jnp.sum(factors[...] * at_ends[None], axis=1)
    sent = jnp.concatenate([sent[:, count // 2 :], sent[:, : count // 2]], axis=1)
    zero = jnp.zeros_like(sent)
    table = [
        jnp.concatenate([piece if m == k else zero for k in range(parts)], axis=1)
        for piece in pieces(sent, 2)
        for m in range(parts)
    ]
    both = lax.dot_general(
        hits[...],
        jnp.concatenate(table, axis=0).astype(bf16),
        (((1,), (1,)), ((), ())),
        preferred_element_type=f32,
    )
    out[...] = both[:, :128] + both[:, 128:]


def one_hot(ids, count):
    return (ids[:, None] == jnp.arange(count, dtype=ids.dtype)[None, :]).astype(f32)


def shards(density, coords, basis, transfer, parent, near_pairs, near_count, far_pairs, coupling):
    highest = lax.Precision.HIGHEST
    own, _, panels = density.shape
    rank = basis.shape[1]
    rows, cols = lax.axis_size("row"), lax.axis_size("col")
    half = cols // rows
    my_row, my_col = lax.axis_index("row"), lax.axis_index("col")
    slots = near_pairs.shape[1]
    per_pair = slots // cols
    block = slots // rows
    vmem = pl.BlockSpec(memory_space=pltpu.VMEM)

    swap = [
        (r * cols + half * p + h, p * cols + half * r + h)
        for r in range(rows)
        for p in range(rows)
        for h in range(half)
    ]
    flat = density.reshape(own, 3 * panels)
    data = jnp.concatenate([flat, coords.reshape(own, 3 * panels)], axis=1)
    first_data = lax.ppermute(data, BOTH, swap)

    moments = jnp.einsum("crk,ck->cr", basis, flat, preferred_element_type=f32)
    lifted = jnp.einsum("crs,cs->cr", transfer, moments, precision=highest).reshape(-1, 128)
    lift_rows = lifted.shape[0]
    live = jnp.arange(slots) < near_count[0]
    ids = jnp.where(live[None], near_pairs % own, -1).astype(f32)
    ids = ids.reshape(2, rows, block).transpose(1, 0, 2).reshape(rows, 1, 2 * block)
    message = jnp.concatenate(
        [
            jnp.broadcast_to(lifted[None], (rows, lift_rows, 128)),
            jnp.pad(ids, ((0, 0), (0, 0), (0, 128 - 2 * block))),
        ],
        axis=1,
    )
    first_data, message = lax.optimization_barrier((first_data, message))
    from_row = lax.all_to_all(message, "row", 0, 0, tiled=True)

    own_first = from_row[:, lift_rows, :block].reshape(-1)
    own_second = from_row[:, lift_rows, block : 2 * block].reshape(-1)
    place = jnp.arange(slots)
    same_owner = (place // block == my_row) & (half * my_row + place % block // per_pair == my_col)
    back_ids = jnp.where(same_owner & (own_first == own_second), -1.0, own_second)
    picked = jnp.dot(one_hot(own_second, own).astype(bf16), data, preferred_element_type=f32)
    row_lifted = from_row[:, :lift_rows, :].astype(bf16).transpose(1, 0, 2).reshape(lift_rows, -1)
    message = jnp.concatenate(
        [
            picked.astype(bf16),
            jnp.broadcast_to(own_first[:, None], (slots, 128)).astype(bf16),
            jnp.tile(row_lifted, (cols, 1)),
        ],
        axis=1,
    )
    second = lax.all_to_all(message, "col", 0, 0, tiled=True)
    ids_lane = 6 * panels

    factors = jnp.concatenate([coupling.transpose(1, 2, 0), coupling.transpose(2, 1, 0)], axis=2)
    partial = pl.pallas_call(
        functools.partial(far_kernel, ids_lane + 128),
        out_shape=jax.ShapeDtypeStruct((rows * slots, 128), f32),
        in_specs=[vmem] * 4,
        out_specs=vmem,
        scratch_shapes=[pltpu.VMEM((rows * slots, far_pairs.size * (128 // rank)), bf16)],
        compiler_params=pltpu.CompilerParams(vmem_limit_bytes=32 << 20),
    )(second, parent.reshape(-1, 128 // rank), far_pairs[::-1].reshape(1, -1), factors)
    first_data, partial = lax.optimization_barrier((first_data, partial))
    row_locals = lax.all_to_all(partial.reshape(rows, slots, 128), "row", 0, 0, tiled=True)

    to_second = near_sums(first_data, second, ids_lane, False)
    returned = lax.all_to_all(
        jnp.concatenate([to_second, row_locals.sum(axis=0)], axis=1), "col", 0, 0, tiled=True
    )
    first_data, to_second = lax.optimization_barrier((first_data, to_second))
    near_first = lax.ppermute(near_sums(first_data, second, ids_lane, True), BOTH, swap)
    near_second = jnp.einsum(
        "sc,sk->ck", one_hot(back_ids, own), returned[:, : 3 * panels], precision=highest
    )
    parent_locals = returned[:, 3 * panels :].reshape(cols, lift_rows, 128).sum(axis=0).reshape(own, rank)
    local_coef = jnp.einsum("csr,cs->cr", transfer, parent_locals, precision=highest)
    far_part = jnp.einsum("crk,cr->ck", basis.astype(f32), local_coef, precision=highest)
    return (near_first + (near_second + far_part)).reshape(own, 3, panels)


def solution(mesh):
    placed = (
        P(BOTH, None, None),
        P(BOTH, None, None),
        P(BOTH, None, None),
        P(BOTH, None, None),
        P(),
        P(None, BOTH),
        P(BOTH),
        P(None, BOTH),
        P(BOTH, None, None),
    )
    return jax.shard_map(
        shards, mesh=mesh, in_specs=placed, out_specs=P(BOTH, None, None), check_vma=False
    )
```

```python
import functools
import math

import jax
import jax.numpy as jnp
from jax import lax
from jax.experimental import pallas as pl
from jax.experimental.pallas import tpu as pltpu
from jax.sharding import PartitionSpec as P

REG_EPS = 0.02
EPS_SQ = REG_EPS * REG_EPS
STOKES_SCALE = 1.0 / (8.0 * math.pi)
BOTH = ("row", "col")
GROUP = 16
BATCH = 8
PANELS = 256
FIELD_ROWS = 32
POINT_ROWS = 16
f32, bf16 = jnp.float32, jnp.bfloat16


def pieces(value, count):
    out = []
    for _ in range(count):
        head = value.astype(bf16).astype(f32)
        out.append(head)
        value = value - head
    return out


def put(ref, row, value):
    for half in range(2):
        ref[half, row * GROUP : (row + 1) * GROUP, :] = value[:, half * 128 : (half + 1) * 128]


def get(ref, row):
    return jnp.concatenate([ref[half, row * GROUP : (row + 1) * GROUP, :] for half in range(2)], 1)


def split_parts(block):
    parts = [block[:, k * PANELS : (k + 1) * PANELS] for k in range(6)]
    return parts[:3], parts[3:]


def prepare_source(block, field, left):
    q, y = split_parts(block)
    one, zero = jnp.ones_like(q[0]), jnp.zeros_like(q[0])
    square = y[0] * y[0] + y[1] * y[1] + y[2] * y[2]
    along = y[0] * q[0] + y[1] * q[1] + y[2] * q[2]
    rows = list(q)
    for i in range(3):
        for j in range(3):
            rows += pieces(y[i] * q[j], 2)
    for i in range(3):
        rows += pieces(square * q[i] + y[i] * along, 3)
    rows += [zero] * (FIELD_ROWS - len(rows))
    for k, value in enumerate(rows):
        put(field, k, value)
    for k, value in enumerate([-2 * v for v in y] + pieces(square + EPS_SQ / 2, 3) + [one] * 3 + [zero] * 7):
        put(left, k, value)


def prepare_target(block, right):
    _, x = split_parts(block)
    one, zero = jnp.ones_like(x[0]), jnp.zeros_like(x[0])
    norm = pieces(x[0] * x[0] + x[1] * x[1] + x[2] * x[2] + EPS_SQ / 2, 3)
    for k, value in enumerate(x + [one] * 3 + norm + [zero] * 7):
        put(right, k, value)


def finish(block, sums):
    _, x = split_parts(block)
    mom = [get(sums, i) for i in range(3)]
    cross = [[get(sums, 3 + 2 * (3 * i + j)) + get(sums, 4 + 2 * (3 * i + j)) for j in range(3)] for i in range(3)]
    dot = x[0] * mom[0] + x[1] * mom[1] + x[2] * mom[2] - (cross[0][0] + cross[1][1] + cross[2][2])
    square = x[0] * x[0] + x[1] * x[1] + x[2] * x[2] + 2 * EPS_SQ
    out = []
    for i in range(3):
        mixed = sum(x[j] * (cross[i][j] + 2 * cross[j][i]) for j in range(3))
        tail = get(sums, 21 + 3 * i) + get(sums, 22 + 3 * i) + get(sums, 23 + 3 * i)
        out.append(((square * mom[i] + x[i] * dot - mixed) + tail) * STOKES_SCALE)
    return out


def near_kernel(ids_lane, to_first, first_ref, second_ref, out, field, left, right, sums):
    own = first_ref.shape[0]
    if to_first:
        out[...] = jnp.zeros_like(out)

    def group(g, carry):
        rows = pl.ds(pl.multiple_of(g * GROUP, GROUP), GROUP)
        ids = second_ref[rows, ids_lane : ids_lane + 128].astype(f32)[:, :own]
        chosen = (ids == lax.broadcasted_iota(jnp.int32, (GROUP, own), 1).astype(f32)).astype(bf16)
        first = jnp.dot(chosen, first_ref[...], preferred_element_type=f32)
        second = second_ref[rows, : 6 * PANELS].astype(f32)
        source, target = (second, first) if to_first else (first, second)
        prepare_source(source, field, left)
        prepare_target(target, right)

        def load(ref, count, s):
            parts = [ref[half, pl.ds(s, count, stride=GROUP), :] for half in range(2)]
            return jnp.concatenate(parts, 1).astype(bf16)

        for start in range(0, GROUP, BATCH):
            batch = range(start, start + BATCH)
            shifted = [
                lax.dot_general(
                    load(left, POINT_ROWS, s),
                    load(right, POINT_ROWS, s),
                    (((0,), (0,)), ((), ())),
                    preferred_element_type=f32,
                )
                for s in batch
            ]
            cubes = []
            for value in shifted:
                inv = lax.rsqrt(value)
                cubes.append((inv * inv * inv).astype(bf16))
            for s, cube in zip(batch, cubes):
                total = jnp.dot(load(field, FIELD_ROWS, s), cube, preferred_element_type=f32)
                for half in range(2):
                    sums[half, pl.ds(s, FIELD_ROWS, stride=GROUP), :] = total[:, half * 128 : (half + 1) * 128]

        for i, value in enumerate(finish(target, sums)):
            lanes = slice(i * PANELS, (i + 1) * PANELS)
            if not to_first:
                out[rows, lanes] = value
                continue
            for piece in pieces(value, 3):
                out[:, lanes] += lax.dot_general(
                    chosen, piece.astype(bf16), (((0,), (0,)), ((), ())), preferred_element_type=f32
                )
        return carry

    lax.fori_loop(0, second_ref.shape[0] // GROUP, group, 0)


def near_sums(first, second, ids_lane, to_first):
    slots = second.shape[0]
    vmem = pl.BlockSpec(memory_space=pltpu.VMEM)

    def rows(count):
        return pltpu.VMEM((2, count * GROUP, 128), f32)

    return pl.pallas_call(
        functools.partial(near_kernel, ids_lane, to_first),
        out_shape=jax.ShapeDtypeStruct((first.shape[0] if to_first else slots, 3 * PANELS), f32),
        in_specs=[vmem] * 2,
        out_specs=vmem,
        scratch_shapes=[rows(FIELD_ROWS), rows(POINT_ROWS), rows(POINT_ROWS), rows(FIELD_ROWS)],
        compiler_params=pltpu.CompilerParams(vmem_limit_bytes=32 << 20),
        cost_estimate=pl.CostEstimate(
            flops=slots * 2 * 64 * PANELS * PANELS, bytes_accessed=slots * 9216, transcendentals=0
        ),
    )(first, second)


def far_kernel(start, recv, parents, ends, factors, out, hits):
    parts = parents.shape[1]
    count = ends.shape[1]
    rank = 128 // parts
    for m in range(parts):
        hits[:, m * count : (m + 1) * count] = (parents[:, m : m + 1] == ends[...]).astype(f32).astype(bf16)
    slots = recv.shape[0]
    found = jnp.zeros((128, parts * count), f32)
    for r in range(hits.shape[0] // slots):
        found += lax.dot_general(
            recv[:, start + 128 * r : start + 128 * (r + 1)],
            hits[r * slots : (r + 1) * slots, :],
            (((0,), (0,)), ((), ())),
            preferred_element_type=f32,
        )
    at_ends = sum(found[m * rank : (m + 1) * rank, m * count : (m + 1) * count] for m in range(parts))
    sent = jnp.sum(factors[...] * at_ends[None], axis=1)
    sent = jnp.concatenate([sent[:, count // 2 :], sent[:, : count // 2]], axis=1)
    zero = jnp.zeros_like(sent)
    table = [
        jnp.concatenate([piece if m == k else zero for k in range(parts)], axis=1)
        for piece in pieces(sent, 2)
        for m in range(parts)
    ]
    both = lax.dot_general(
        hits[...],
        jnp.concatenate(table, axis=0).astype(bf16),
        (((1,), (1,)), ((), ())),
        preferred_element_type=f32,
    )
    out[...] = both[:, :128] + both[:, 128:]


def one_hot(ids, count):
    return (ids[:, None] == jnp.arange(count, dtype=ids.dtype)[None, :]).astype(f32)


def shards(density, coords, basis, transfer, parent, near_pairs, near_count, far_pairs, coupling):
    highest = lax.Precision.HIGHEST
    own, _, panels = density.shape
    rank = basis.shape[1]
    rows, cols = lax.axis_size("row"), lax.axis_size("col")
    half = cols // rows
    my_row, my_col = lax.axis_index("row"), lax.axis_index("col")
    slots = near_pairs.shape[1]
    per_pair = slots // cols
    block = slots // rows
    vmem = pl.BlockSpec(memory_space=pltpu.VMEM)

    swap = [
        (r * cols + half * p + h, p * cols + half * r + h)
        for r in range(rows)
        for p in range(rows)
        for h in range(half)
    ]
    flat = density.reshape(own, 3 * panels)
    data = jnp.concatenate([flat, coords.reshape(own, 3 * panels)], axis=1)
    first_data = lax.ppermute(data, BOTH, swap)

    moments = jnp.einsum("crk,ck->cr", basis, flat, preferred_element_type=f32)
    lifted = jnp.einsum("crs,cs->cr", transfer, moments, precision=highest).reshape(-1, 128)
    lift_rows = lifted.shape[0]
    live = jnp.arange(slots) < near_count[0]
    ids = jnp.where(live[None], near_pairs % own, -1).astype(f32)
    ids = ids.reshape(2, rows, block).transpose(1, 0, 2).reshape(rows, 1, 2 * block)
    message = jnp.concatenate(
        [
            jnp.broadcast_to(lifted[None], (rows, lift_rows, 128)),
            jnp.pad(ids, ((0, 0), (0, 0), (0, 128 - 2 * block))),
        ],
        axis=1,
    )
    from_row = lax.all_to_all(message, "row", 0, 0, tiled=True)
    first_data, from_row = lax.optimization_barrier((first_data, from_row))

    own_first = from_row[:, lift_rows, :block].reshape(-1)
    own_second = from_row[:, lift_rows, block : 2 * block].reshape(-1)
    place = jnp.arange(slots)
    same_owner = (place // block == my_row) & (half * my_row + place % block // per_pair == my_col)
    back_ids = jnp.where(same_owner & (own_first == own_second), -1.0, own_second)
    picked = jnp.dot(one_hot(own_second, own).astype(bf16), data, preferred_element_type=f32)
    row_lifted = from_row[:, :lift_rows, :].astype(bf16).transpose(1, 0, 2).reshape(lift_rows, -1)
    message = jnp.concatenate(
        [
            picked.astype(bf16),
            jnp.broadcast_to(own_first[:, None], (slots, 128)).astype(bf16),
            jnp.tile(row_lifted, (cols, 1)),
        ],
        axis=1,
    )
    second = lax.all_to_all(message, "col", 0, 0, tiled=True)
    ids_lane = 6 * panels

    factors = jnp.concatenate([coupling.transpose(1, 2, 0), coupling.transpose(2, 1, 0)], axis=2)
    partial = pl.pallas_call(
        functools.partial(far_kernel, ids_lane + 128),
        out_shape=jax.ShapeDtypeStruct((rows * slots, 128), f32),
        in_specs=[vmem] * 4,
        out_specs=vmem,
        scratch_shapes=[pltpu.VMEM((rows * slots, far_pairs.size * (128 // rank)), bf16)],
        compiler_params=pltpu.CompilerParams(vmem_limit_bytes=32 << 20),
    )(second, parent.reshape(-1, 128 // rank), far_pairs[::-1].reshape(1, -1), factors)
    first_data, partial = lax.optimization_barrier((first_data, partial))
    row_locals = lax.all_to_all(partial.reshape(rows, slots, 128), "row", 0, 0, tiled=True)

    to_second = near_sums(first_data, second, ids_lane, False)
    returned = lax.all_to_all(
        jnp.concatenate([to_second, row_locals.sum(axis=0)], axis=1), "col", 0, 0, tiled=True
    )
    first_data, to_second = lax.optimization_barrier((first_data, to_second))
    near_first = lax.ppermute(near_sums(first_data, second, ids_lane, True), BOTH, swap)
    near_second = jnp.einsum(
        "sc,sk->ck", one_hot(back_ids, own), returned[:, : 3 * panels], precision=highest
    )
    parent_locals = returned[:, 3 * panels :].reshape(cols, lift_rows, 128).sum(axis=0).reshape(own, rank)
    local_coef = jnp.einsum("csr,cs->cr", transfer, parent_locals, precision=highest)
    far_part = jnp.einsum("crk,cr->ck", basis.astype(f32), local_coef, precision=highest)
    return (near_first + (near_second + far_part)).reshape(own, 3, panels)


def solution(mesh):
    placed = (
        P(BOTH, None, None),
        P(BOTH, None, None),
        P(BOTH, None, None),
        P(BOTH, None, None),
        P(),
        P(None, BOTH),
        P(BOTH),
        P(None, BOTH),
        P(BOTH, None, None),
    )
    return jax.shard_map(
        shards, mesh=mesh, in_specs=placed, out_specs=P(BOTH, None, None), check_vma=False
    )
```

```python
import functools
import math

import jax
import jax.numpy as jnp
from jax import lax
from jax.experimental import pallas as pl
from jax.experimental.pallas import tpu as pltpu
from jax.sharding import PartitionSpec as P

REG_EPS = 0.02
EPS_SQ = REG_EPS * REG_EPS
STOKES_SCALE = 1.0 / (8.0 * math.pi)
BOTH = ("row", "col")
GROUP = 16
BATCH = 8
PANELS = 256
FIELD_ROWS = 32
POINT_ROWS = 16
f32, bf16 = jnp.float32, jnp.bfloat16


def pieces(value, count):
    out = []
    for _ in range(count):
        head = value.astype(bf16).astype(f32)
        out.append(head)
        value = value - head
    return out


def put(ref, row, value):
    for half in range(2):
        ref[half, row * GROUP : (row + 1) * GROUP, :] = value[:, half * 128 : (half + 1) * 128]


def get(ref, row):
    return jnp.concatenate([ref[half, row * GROUP : (row + 1) * GROUP, :] for half in range(2)], 1)


def split_parts(block):
    parts = [block[:, k * PANELS : (k + 1) * PANELS] for k in range(6)]
    return parts[:3], parts[3:]


def prepare_source(block, field, left):
    q, y = split_parts(block)
    one, zero = jnp.ones_like(q[0]), jnp.zeros_like(q[0])
    square = y[0] * y[0] + y[1] * y[1] + y[2] * y[2]
    along = y[0] * q[0] + y[1] * q[1] + y[2] * q[2]
    rows = list(q)
    for i in range(3):
        for j in range(3):
            rows += pieces(y[i] * q[j], 2)
    for i in range(3):
        rows += pieces(square * q[i] + y[i] * along, 3)
    rows += [zero] * (FIELD_ROWS - len(rows))
    for k, value in enumerate(rows):
        put(field, k, value)
    if left is None:
        return
    for k, value in enumerate([-2 * v for v in y] + pieces(square + EPS_SQ / 2, 3) + [one] * 3 + [zero] * 7):
        put(left, k, value)


def prepare_target(block, right):
    _, x = split_parts(block)
    one, zero = jnp.ones_like(x[0]), jnp.zeros_like(x[0])
    norm = pieces(x[0] * x[0] + x[1] * x[1] + x[2] * x[2] + EPS_SQ / 2, 3)
    for k, value in enumerate(x + [one] * 3 + norm + [zero] * 7):
        put(right, k, value)


def finish(block, sums):
    _, x = split_parts(block)
    mom = [get(sums, i) for i in range(3)]
    cross = [[get(sums, 3 + 2 * (3 * i + j)) + get(sums, 4 + 2 * (3 * i + j)) for j in range(3)] for i in range(3)]
    dot = x[0] * mom[0] + x[1] * mom[1] + x[2] * mom[2] - (cross[0][0] + cross[1][1] + cross[2][2])
    square = x[0] * x[0] + x[1] * x[1] + x[2] * x[2] + 2 * EPS_SQ
    out = []
    for i in range(3):
        mixed = sum(x[j] * (cross[i][j] + 2 * cross[j][i]) for j in range(3))
        tail = get(sums, 21 + 3 * i) + get(sums, 22 + 3 * i) + get(sums, 23 + 3 * i)
        out.append(((square * mom[i] + x[i] * dot - mixed) + tail) * STOKES_SCALE)
    return out


def near_kernel(ids_lane, first_ref, second_ref, near_first, to_second, field_a, left, field_b, right, sums_a, sums_b):
    own = first_ref.shape[0]
    near_first[...] = jnp.zeros_like(near_first)

    def group(g, carry):
        rows = pl.ds(pl.multiple_of(g * GROUP, GROUP), GROUP)
        ids = second_ref[rows, ids_lane : ids_lane + 128].astype(f32)[:, :own]
        chosen = (ids == lax.broadcasted_iota(jnp.int32, (GROUP, own), 1).astype(f32)).astype(bf16)
        first = jnp.dot(chosen, first_ref[...], preferred_element_type=f32)
        second = second_ref[rows, : 6 * PANELS].astype(f32)
        prepare_source(first, field_a, left)
        prepare_source(second, field_b, None)
        prepare_target(second, right)

        def load(ref, count, s):
            parts = [ref[half, pl.ds(s, count, stride=GROUP), :] for half in range(2)]
            return jnp.concatenate(parts, 1).astype(bf16)

        def apply(field, cube, dim, sums, s):
            total = lax.dot_general(
                load(field, FIELD_ROWS, s), cube, (((1,), (dim,)), ((), ())), preferred_element_type=f32
            )
            for half in range(2):
                sums[half, pl.ds(s, FIELD_ROWS, stride=GROUP), :] = total[:, half * 128 : (half + 1) * 128]

        for start in range(0, GROUP, BATCH):
            batch = range(start, start + BATCH)
            shifted = [
                lax.dot_general(
                    load(left, POINT_ROWS, s),
                    load(right, POINT_ROWS, s),
                    (((0,), (0,)), ((), ())),
                    preferred_element_type=f32,
                )
                for s in batch
            ]
            cubes = []
            for value in shifted:
                inv = lax.rsqrt(value)
                cubes.append((inv * inv * inv).astype(bf16))
            for s, cube in zip(batch, cubes):
                apply(field_a, cube, 0, sums_b, s)
            for s, cube in zip(batch, cubes):
                apply(field_b, cube, 1, sums_a, s)

        for i, value in enumerate(finish(second, sums_b)):
            to_second[rows, i * PANELS : (i + 1) * PANELS] = value
        for i, value in enumerate(finish(first, sums_a)):
            for piece in pieces(value, 3):
                near_first[:, i * PANELS : (i + 1) * PANELS] += lax.dot_general(
                    chosen, piece.astype(bf16), (((0,), (0,)), ((), ())), preferred_element_type=f32
                )
        return carry

    lax.fori_loop(0, second_ref.shape[0] // GROUP, group, 0)


def near_sums(first, second, ids_lane):
    slots = second.shape[0]
    vmem = pl.BlockSpec(memory_space=pltpu.VMEM)

    def rows(count):
        return pltpu.VMEM((2, count * GROUP, 128), f32)

    return pl.pallas_call(
        functools.partial(near_kernel, ids_lane),
        out_shape=[
            jax.ShapeDtypeStruct((first.shape[0], 3 * PANELS), f32),
            jax.ShapeDtypeStruct((slots, 3 * PANELS), f32),
        ],
        in_specs=[vmem] * 2,
        out_specs=[vmem] * 2,
        scratch_shapes=[rows(FIELD_ROWS), rows(POINT_ROWS)] * 2 + [rows(FIELD_ROWS)] * 2,
        compiler_params=pltpu.CompilerParams(vmem_limit_bytes=32 << 20),
        cost_estimate=pl.CostEstimate(
            flops=slots * 2 * 2 * 64 * PANELS * PANELS, bytes_accessed=slots * 9216, transcendentals=0
        ),
    )(first, second)


def far_kernel(start, recv, parents, ends, factors, out, hits):
    parts = parents.shape[1]
    count = ends.shape[1]
    rank = 128 // parts
    for m in range(parts):
        hits[:, m * count : (m + 1) * count] = (parents[:, m : m + 1] == ends[...]).astype(f32).astype(bf16)
    slots = recv.shape[0]
    found = jnp.zeros((128, parts * count), f32)
    for r in range(hits.shape[0] // slots):
        found += lax.dot_general(
            recv[:, start + 128 * r : start + 128 * (r + 1)],
            hits[r * slots : (r + 1) * slots, :],
            (((0,), (0,)), ((), ())),
            preferred_element_type=f32,
        )
    at_ends = sum(found[m * rank : (m + 1) * rank, m * count : (m + 1) * count] for m in range(parts))
    sent = jnp.sum(factors[...] * at_ends[None], axis=1)
    sent = jnp.concatenate([sent[:, count // 2 :], sent[:, : count // 2]], axis=1)
    zero = jnp.zeros_like(sent)
    table = [
        jnp.concatenate([piece if m == k else zero for k in range(parts)], axis=1)
        for piece in pieces(sent, 2)
        for m in range(parts)
    ]
    both = lax.dot_general(
        hits[...],
        jnp.concatenate(table, axis=0).astype(bf16),
        (((1,), (1,)), ((), ())),
        preferred_element_type=f32,
    )
    out[...] = both[:, :128] + both[:, 128:]


def one_hot(ids, count):
    return (ids[:, None] == jnp.arange(count, dtype=ids.dtype)[None, :]).astype(f32)


def shards(density, coords, basis, transfer, parent, near_pairs, near_count, far_pairs, coupling):
    highest = lax.Precision.HIGHEST
    own, _, panels = density.shape
    rank = basis.shape[1]
    rows, cols = lax.axis_size("row"), lax.axis_size("col")
    half = cols // rows
    my_row, my_col = lax.axis_index("row"), lax.axis_index("col")
    slots = near_pairs.shape[1]
    per_pair = slots // cols
    block = slots // rows
    vmem = pl.BlockSpec(memory_space=pltpu.VMEM)

    swap = [
        (r * cols + half * p + h, p * cols + half * r + h)
        for r in range(rows)
        for p in range(rows)
        for h in range(half)
    ]
    flat = density.reshape(own, 3 * panels)
    data = jnp.concatenate([flat, coords.reshape(own, 3 * panels)], axis=1)
    first_data = lax.ppermute(data, BOTH, swap)

    moments = jnp.einsum("crk,ck->cr", basis, flat, preferred_element_type=f32)
    lifted = jnp.einsum("crs,cs->cr", transfer, moments, precision=highest).reshape(-1, 128)
    lift_rows = lifted.shape[0]
    live = jnp.arange(slots) < near_count[0]
    ids = jnp.where(live[None], near_pairs % own, -1).astype(f32)
    ids = ids.reshape(2, rows, block).transpose(1, 0, 2).reshape(rows, 1, 2 * block)
    message = jnp.concatenate(
        [
            jnp.broadcast_to(lifted[None], (rows, lift_rows, 128)),
            jnp.pad(ids, ((0, 0), (0, 0), (0, 128 - 2 * block))),
        ],
        axis=1,
    )
    from_row = lax.all_to_all(message, "row", 0, 0, tiled=True)
    first_data, from_row = lax.optimization_barrier((first_data, from_row))

    own_first = from_row[:, lift_rows, :block].reshape(-1)
    own_second = from_row[:, lift_rows, block : 2 * block].reshape(-1)
    place = jnp.arange(slots)
    same_owner = (place // block == my_row) & (half * my_row + place % block // per_pair == my_col)
    back_ids = jnp.where(same_owner & (own_first == own_second), -1.0, own_second)
    picked = jnp.dot(one_hot(own_second, own).astype(bf16), data, preferred_element_type=f32)
    row_lifted = from_row[:, :lift_rows, :].astype(bf16).transpose(1, 0, 2).reshape(lift_rows, -1)
    message = jnp.concatenate(
        [
            picked.astype(bf16),
            jnp.broadcast_to(own_first[:, None], (slots, 128)).astype(bf16),
            jnp.tile(row_lifted, (cols, 1)),
        ],
        axis=1,
    )
    second = lax.all_to_all(message, "col", 0, 0, tiled=True)
    ids_lane = 6 * panels

    factors = jnp.concatenate([coupling.transpose(1, 2, 0), coupling.transpose(2, 1, 0)], axis=2)
    partial = pl.pallas_call(
        functools.partial(far_kernel, ids_lane + 128),
        out_shape=jax.ShapeDtypeStruct((rows * slots, 128), f32),
        in_specs=[vmem] * 4,
        out_specs=vmem,
        scratch_shapes=[pltpu.VMEM((rows * slots, far_pairs.size * (128 // rank)), bf16)],
        compiler_params=pltpu.CompilerParams(vmem_limit_bytes=32 << 20),
    )(second, parent.reshape(-1, 128 // rank), far_pairs[::-1].reshape(1, -1), factors)
    first_data, partial = lax.optimization_barrier((first_data, partial))
    row_locals = lax.all_to_all(partial.reshape(rows, slots, 128), "row", 0, 0, tiled=True)

    near_first, to_second = near_sums(first_data, second, ids_lane)
    near_first = lax.ppermute(near_first, BOTH, swap)
    returned = lax.all_to_all(
        jnp.concatenate([to_second, row_locals.sum(axis=0)], axis=1), "col", 0, 0, tiled=True
    )
    near_second = jnp.einsum(
        "sc,sk->ck", one_hot(back_ids, own), returned[:, : 3 * panels], precision=highest
    )
    parent_locals = returned[:, 3 * panels :].reshape(cols, lift_rows, 128).sum(axis=0).reshape(own, rank)
    local_coef = jnp.einsum("csr,cs->cr", transfer, parent_locals, precision=highest)
    far_part = jnp.einsum("crk,cr->ck", basis.astype(f32), local_coef, precision=highest)
    return (near_first + (near_second + far_part)).reshape(own, 3, panels)


def solution(mesh):
    placed = (
        P(BOTH, None, None),
        P(BOTH, None, None),
        P(BOTH, None, None),
        P(BOTH, None, None),
        P(),
        P(None, BOTH),
        P(BOTH),
        P(None, BOTH),
        P(BOTH, None, None),
    )
    return jax.shard_map(
        shards, mesh=mesh, in_specs=placed, out_specs=P(BOTH, None, None), check_vma=False
    )
```

```python
import functools
import math

import jax
import jax.numpy as jnp
from jax import lax
from jax.experimental import pallas as pl
from jax.experimental.pallas import tpu as pltpu
from jax.sharding import PartitionSpec as P

REG_EPS = 0.02
EPS_SQ = REG_EPS * REG_EPS
STOKES_SCALE = 1.0 / (8.0 * math.pi)
BOTH = ("row", "col")
GROUP = 16
BATCH = 8
PANELS = 256
FIELD_ROWS = 32
POINT_ROWS = 16
f32, bf16 = jnp.float32, jnp.bfloat16


def pieces(value, count):
    out = []
    for _ in range(count):
        head = value.astype(bf16).astype(f32)
        out.append(head)
        value = value - head
    return out


def put(ref, row, value):
    for half in range(2):
        ref[half, row * GROUP : (row + 1) * GROUP, :] = value[:, half * 128 : (half + 1) * 128]


def get(ref, row):
    return jnp.concatenate([ref[half, row * GROUP : (row + 1) * GROUP, :] for half in range(2)], 1)


def split_parts(block):
    parts = [block[:, k * PANELS : (k + 1) * PANELS] for k in range(6)]
    return parts[:3], parts[3:]


def prepare_source(block, field, left):
    q, y = split_parts(block)
    one, zero = jnp.ones_like(q[0]), jnp.zeros_like(q[0])
    square = y[0] * y[0] + y[1] * y[1] + y[2] * y[2]
    along = y[0] * q[0] + y[1] * q[1] + y[2] * q[2]
    rows = list(q)
    for i in range(3):
        for j in range(3):
            rows += pieces(y[i] * q[j], 2)
    for i in range(3):
        rows += pieces(square * q[i] + y[i] * along, 3)
    rows += [zero] * (FIELD_ROWS - len(rows))
    for k, value in enumerate(rows):
        put(field, k, value)
    if left is None:
        return
    for k, value in enumerate([-2 * v for v in y] + pieces(square + EPS_SQ / 2, 3) + [one] * 3 + [zero] * 7):
        put(left, k, value)


def prepare_target(block, right):
    _, x = split_parts(block)
    one, zero = jnp.ones_like(x[0]), jnp.zeros_like(x[0])
    norm = pieces(x[0] * x[0] + x[1] * x[1] + x[2] * x[2] + EPS_SQ / 2, 3)
    for k, value in enumerate(x + [one] * 3 + norm + [zero] * 7):
        put(right, k, value)


def finish(block, sums):
    _, x = split_parts(block)
    mom = [get(sums, i) for i in range(3)]
    cross = [[get(sums, 3 + 2 * (3 * i + j)) + get(sums, 4 + 2 * (3 * i + j)) for j in range(3)] for i in range(3)]
    dot = x[0] * mom[0] + x[1] * mom[1] + x[2] * mom[2] - (cross[0][0] + cross[1][1] + cross[2][2])
    square = x[0] * x[0] + x[1] * x[1] + x[2] * x[2] + 2 * EPS_SQ
    out = []
    for i in range(3):
        mixed = sum(x[j] * (cross[i][j] + 2 * cross[j][i]) for j in range(3))
        tail = get(sums, 21 + 3 * i) + get(sums, 22 + 3 * i) + get(sums, 23 + 3 * i)
        out.append(((square * mom[i] + x[i] * dot - mixed) + tail) * STOKES_SCALE)
    return out


def near_kernel(ids_lane, first_ref, second_ref, near_first, to_second, field_a, left, field_b, right, sums_a, sums_b):
    own = first_ref.shape[0]
    near_first[...] = jnp.zeros_like(near_first)

    def group(g, carry):
        rows = pl.ds(pl.multiple_of(g * GROUP, GROUP), GROUP)
        ids = second_ref[rows, ids_lane : ids_lane + 128].astype(f32)[:, :own]
        chosen = (ids == lax.broadcasted_iota(jnp.int32, (GROUP, own), 1).astype(f32)).astype(bf16)
        first = jnp.dot(chosen, first_ref[...], preferred_element_type=f32)
        second = second_ref[rows, : 6 * PANELS].astype(f32)
        prepare_source(first, field_a, left)
        prepare_source(second, field_b, None)
        prepare_target(second, right)

        def load(ref, count, s):
            parts = [ref[half, pl.ds(s, count, stride=GROUP), :] for half in range(2)]
            return jnp.concatenate(parts, 1).astype(bf16)

        def apply(field, cube, dim, sums, s):
            total = lax.dot_general(
                load(field, FIELD_ROWS, s), cube, (((1,), (dim,)), ((), ())), preferred_element_type=f32
            )
            for half in range(2):
                sums[half, pl.ds(s, FIELD_ROWS, stride=GROUP), :] = total[:, half * 128 : (half + 1) * 128]

        for start in range(0, GROUP, BATCH):
            batch = range(start, start + BATCH)
            shifted = [
                lax.dot_general(
                    load(left, POINT_ROWS, s),
                    load(right, POINT_ROWS, s),
                    (((0,), (0,)), ((), ())),
                    preferred_element_type=f32,
                )
                for s in batch
            ]
            cubes = []
            for value in shifted:
                inv = lax.rsqrt(value)
                cubes.append((inv * inv * inv).astype(bf16))
            for s, cube in zip(batch, cubes):
                apply(field_a, cube, 0, sums_b, s)
            for s, cube in zip(batch, cubes):
                apply(field_b, cube, 1, sums_a, s)

        for i, value in enumerate(finish(second, sums_b)):
            to_second[rows, i * PANELS : (i + 1) * PANELS] = value
        for i, value in enumerate(finish(first, sums_a)):
            for piece in pieces(value, 3):
                near_first[:, i * PANELS : (i + 1) * PANELS] += lax.dot_general(
                    chosen, piece.astype(bf16), (((0,), (0,)), ((), ())), preferred_element_type=f32
                )
        return carry

    lax.fori_loop(0, second_ref.shape[0] // GROUP, group, 0)


def near_sums(first, second, ids_lane):
    slots = second.shape[0]
    vmem = pl.BlockSpec(memory_space=pltpu.VMEM)

    def rows(count):
        return pltpu.VMEM((2, count * GROUP, 128), f32)

    return pl.pallas_call(
        functools.partial(near_kernel, ids_lane),
        out_shape=[
            jax.ShapeDtypeStruct((first.shape[0], 3 * PANELS), f32),
            jax.ShapeDtypeStruct((slots, 3 * PANELS), f32),
        ],
        in_specs=[vmem] * 2,
        out_specs=[vmem] * 2,
        scratch_shapes=[rows(FIELD_ROWS), rows(POINT_ROWS)] * 2 + [rows(FIELD_ROWS)] * 2,
        compiler_params=pltpu.CompilerParams(vmem_limit_bytes=32 << 20),
        cost_estimate=pl.CostEstimate(
            flops=slots * 2 * 2 * 64 * PANELS * PANELS, bytes_accessed=slots * 9216, transcendentals=0
        ),
    )(first, second)


def far_kernel(start, recv, parents, ends, factors, out, hits):
    parts = parents.shape[1]
    count = ends.shape[1]
    rank = 128 // parts
    for m in range(parts):
        hits[:, m * count : (m + 1) * count] = (parents[:, m : m + 1] == ends[...]).astype(f32).astype(bf16)
    slots = recv.shape[0]
    found = jnp.zeros((128, parts * count), f32)
    for r in range(hits.shape[0] // slots):
        found += lax.dot_general(
            recv[:, start + 128 * r : start + 128 * (r + 1)],
            hits[r * slots : (r + 1) * slots, :],
            (((0,), (0,)), ((), ())),
            preferred_element_type=f32,
        )
    at_ends = sum(found[m * rank : (m + 1) * rank, m * count : (m + 1) * count] for m in range(parts))
    sent = jnp.sum(factors[...] * at_ends[None], axis=1)
    sent = jnp.concatenate([sent[:, count // 2 :], sent[:, : count // 2]], axis=1)
    zero = jnp.zeros_like(sent)
    table = [
        jnp.concatenate([piece if m == k else zero for k in range(parts)], axis=1)
        for piece in pieces(sent, 2)
        for m in range(parts)
    ]
    both = lax.dot_general(
        hits[...],
        jnp.concatenate(table, axis=0).astype(bf16),
        (((1,), (1,)), ((), ())),
        preferred_element_type=f32,
    )
    out[...] = both[:, :128] + both[:, 128:]


def own_lanes(own, rank):
    shape = (own, own * rank)
    return lax.broadcasted_iota(jnp.int32, shape, 1) // rank == lax.broadcasted_iota(jnp.int32, shape, 0)


def start_kernel(
    count, pairs, density, coords, basis_hbm, transfer_hbm, data, message, clouds, basis, transfer, sems
):
    sources = (density, coords, basis_hbm, transfer_hbm)
    targets = (clouds.at[:3], clouds.at[3:], basis, transfer)
    copies = [pltpu.make_async_copy(a, b, sems.at[k]) for k, (a, b) in enumerate(zip(sources, targets))]
    for copy in copies:
        copy.start()
    own, rank = density.shape[1], transfer.shape[1]
    mine = own_lanes(own, rank)
    across = (((1,), (1,)), ((), ()))
    copies[0].wait()
    copies[1].wait()
    flat = jnp.concatenate([clouds[i] for i in range(3)], axis=1)
    data[...] = jnp.concatenate([flat] + [clouds[i] for i in range(3, 6)], axis=1)
    copies[2].wait()
    every = jnp.where(mine, lax.dot_general(flat, basis[...], across, preferred_element_type=f32), 0.0)
    folded = sum(every[:, k : k + 128] for k in range(0, own * rank, 128))
    moments = sum(folded[:, k : k + rank] for k in range(0, 128, rank))
    copies[3].wait()
    lifted = lax.dot_general(
        moments, transfer[...], across, precision=lax.Precision.HIGHEST, preferred_element_type=f32
    )
    lifted = jnp.sum(jnp.where(mine, lifted, 0.0), axis=0, keepdims=True)
    ids = lax.rem(pairs[...], own)
    live = lax.broadcasted_iota(jnp.int32, ids.shape, 1) < count[0]
    rows = [lifted[:, k : k + 128] for k in range(0, own * rank, 128)]
    block = jnp.concatenate(rows + [jnp.where(live, ids, -1).astype(f32)], axis=0)
    for k in range(message.shape[0]):
        message[k] = block


def start(near_count, near_pairs, density, coords, basis, transfer, rows):
    own, rank, width = basis.shape
    panels = width // 3
    vmem, hbm = pl.BlockSpec(memory_space=pltpu.VMEM), pl.BlockSpec(memory_space=pltpu.HBM)
    return pl.pallas_call(
        start_kernel,
        out_shape=[
            jax.ShapeDtypeStruct((own, 2 * width), density.dtype),
            jax.ShapeDtypeStruct((rows, own * rank // 128 + 2, near_pairs.shape[1]), f32),
        ],
        in_specs=[pl.BlockSpec(memory_space=pltpu.SMEM), vmem] + [hbm] * 4,
        out_specs=[vmem] * 2,
        scratch_shapes=[
            pltpu.VMEM((6, own, panels), density.dtype),
            pltpu.VMEM((own * rank, width), basis.dtype),
            pltpu.VMEM((own * rank, rank), f32),
            pltpu.SemaphoreType.DMA((4,)),
        ],
        compiler_params=pltpu.CompilerParams(vmem_limit_bytes=60 << 20),
    )(
        near_count,
        near_pairs,
        density.transpose(1, 0, 2),
        coords.transpose(1, 0, 2),
        basis.reshape(own * rank, width),
        transfer.reshape(own * rank, rank),
    )


def end_kernel(back, returned, near_first, basis, transfer, out, velocity, sems):
    own, panels = velocity.shape[1:]
    rank = transfer.shape[1]
    mine = own_lanes(own, rank)
    lift_rows = own * rank // 128
    local = sum(returned[k : k + lift_rows, 3 * panels :] for k in range(0, returned.shape[0], lift_rows))
    local = jnp.concatenate([local[k : k + 1] for k in range(lift_rows)], axis=1)
    coef = jnp.dot(
        jnp.where(mine, local, 0.0), transfer[...], precision=lax.Precision.HIGHEST, preferred_element_type=f32
    )
    coef = pieces(jnp.where(mine, jnp.concatenate([coef] * own, axis=1), 0.0), 3)
    coef = jnp.concatenate(coef, axis=0).astype(bf16)
    slot = lax.broadcasted_iota(jnp.int32, (own, back.shape[1]), 0).astype(f32)
    chosen = (back[...] == slot).astype(f32).astype(bf16)
    copies = []
    for i in range(3):
        lanes = slice(i * panels, (i + 1) * panels)
        far = jnp.dot(coef, basis[:, lanes], preferred_element_type=f32)
        total = far[:own] + far[own : 2 * own] + far[2 * own :]
        for piece in pieces(returned[:, lanes], 3):
            total += jnp.dot(chosen, piece.astype(bf16), preferred_element_type=f32)
        velocity[i] = near_first[:, lanes] + total
        copies.append(pltpu.make_async_copy(velocity.at[i], out.at[i], sems.at[i]))
        copies[-1].start()
    for copy in copies:
        copy.wait()


def end(back, returned, near_first, basis, transfer):
    own, rank, width = basis.shape
    shape = (3, own, width // 3)
    return pl.pallas_call(
        end_kernel,
        out_shape=jax.ShapeDtypeStruct(shape, f32),
        in_specs=[pl.BlockSpec(memory_space=pltpu.VMEM)] * 5,
        out_specs=pl.BlockSpec(memory_space=pltpu.HBM),
        scratch_shapes=[pltpu.VMEM(shape, f32), pltpu.SemaphoreType.DMA((3,))],
        compiler_params=pltpu.CompilerParams(vmem_limit_bytes=8 << 20),
    )(
        back[None],
        returned,
        near_first,
        basis.reshape(own * rank, width),
        transfer.reshape(own * rank, rank),
    ).transpose(1, 0, 2)


def one_hot(ids, count):
    return (ids[:, None] == jnp.arange(count, dtype=ids.dtype)[None, :]).astype(f32)


def shards(density, coords, basis, transfer, parent, near_pairs, near_count, far_pairs, coupling):
    own, _, panels = density.shape
    rank = basis.shape[1]
    rows, cols = lax.axis_size("row"), lax.axis_size("col")
    half = cols // rows
    my_row, my_col = lax.axis_index("row"), lax.axis_index("col")
    slots = near_pairs.shape[1]
    per_pair = slots // cols
    block = slots // rows
    lift_rows = own * rank // 128
    vmem = pl.BlockSpec(memory_space=pltpu.VMEM)

    swap = [
        (r * cols + half * p + h, p * cols + half * r + h)
        for r in range(rows)
        for p in range(rows)
        for h in range(half)
    ]
    data, message = start(near_count, near_pairs, density, coords, basis, transfer, rows)
    from_row = lax.all_to_all(message, "row", 0, 0, tiled=True)
    data, from_row = lax.optimization_barrier((data, from_row))
    first_data = lax.ppermute(data, BOTH, swap)

    ids = lax.dynamic_slice_in_dim(from_row[:, lift_rows:, :], my_row * block, block, 2)
    own_first, own_second = ids[:, 0].reshape(-1), ids[:, 1].reshape(-1)
    place = jnp.arange(slots)
    same_owner = (place // block == my_row) & (half * my_row + place % block // per_pair == my_col)
    back_ids = jnp.where(same_owner & (own_first == own_second), -1.0, own_second)
    picked = jnp.dot(one_hot(own_second, own).astype(bf16), data, preferred_element_type=f32)
    row_lifted = from_row[:, :lift_rows, :].astype(bf16).transpose(1, 0, 2).reshape(lift_rows, -1)
    message = jnp.concatenate(
        [
            picked.astype(bf16),
            jnp.broadcast_to(own_first[:, None], (slots, 128)).astype(bf16),
            jnp.tile(row_lifted, (cols, 1)),
        ],
        axis=1,
    )
    second = lax.all_to_all(message, "col", 0, 0, tiled=True)
    ids_lane = 6 * panels
    first_data, second = lax.optimization_barrier((first_data, second))

    factors = jnp.concatenate([coupling.transpose(1, 2, 0), coupling.transpose(2, 1, 0)], axis=2)
    partial = pl.pallas_call(
        functools.partial(far_kernel, ids_lane + 128),
        out_shape=jax.ShapeDtypeStruct((rows * slots, 128), f32),
        in_specs=[vmem] * 4,
        out_specs=vmem,
        scratch_shapes=[pltpu.VMEM((rows * slots, far_pairs.size * (128 // rank)), bf16)],
        compiler_params=pltpu.CompilerParams(vmem_limit_bytes=32 << 20),
    )(second, parent.reshape(-1, 128 // rank), far_pairs[::-1].reshape(1, -1), factors)
    first_data, partial = lax.optimization_barrier((first_data, partial))
    row_locals = lax.all_to_all(partial.reshape(rows, slots, 128), "row", 0, 0, tiled=True)

    near_first, to_second = near_sums(first_data, second, ids_lane)
    near_first = lax.ppermute(near_first, BOTH, swap)
    returned = lax.all_to_all(
        jnp.concatenate([to_second, row_locals.sum(axis=0)], axis=1), "col", 0, 0, tiled=True
    )
    return end(back_ids, returned, near_first, basis, transfer)


def solution(mesh):
    placed = (
        P(BOTH, None, None),
        P(BOTH, None, None),
        P(BOTH, None, None),
        P(BOTH, None, None),
        P(),
        P(None, BOTH),
        P(BOTH),
        P(None, BOTH),
        P(BOTH, None, None),
    )
    return jax.shard_map(
        shards, mesh=mesh, in_specs=placed, out_specs=P(BOTH, None, None), check_vma=False
    )
```

```python
import functools
import math

import jax
import jax.numpy as jnp
from jax import lax
from jax.experimental import pallas as pl
from jax.experimental.pallas import tpu as pltpu
from jax.sharding import PartitionSpec as P

REG_EPS = 0.02
EPS_SQ = REG_EPS * REG_EPS
STOKES_SCALE = 1.0 / (8.0 * math.pi)
BOTH = ("row", "col")
GROUP = 16
BATCH = 8
PANELS = 256
FIELD_ROWS = 32
POINT_ROWS = 16
f32, bf16 = jnp.float32, jnp.bfloat16


def pieces(value, count):
    out = []
    for _ in range(count):
        head = value.astype(bf16).astype(f32)
        out.append(head)
        value = value - head
    return out


def put(ref, row, value):
    for half in range(2):
        ref[half, row * GROUP : (row + 1) * GROUP, :] = value[:, half * 128 : (half + 1) * 128]


def get(ref, row):
    return jnp.concatenate([ref[half, row * GROUP : (row + 1) * GROUP, :] for half in range(2)], 1)


def split_parts(block):
    parts = [block[:, k * PANELS : (k + 1) * PANELS] for k in range(6)]
    return parts[:3], parts[3:]


def prepare_source(block, field, left):
    q, y = split_parts(block)
    one, zero = jnp.ones_like(q[0]), jnp.zeros_like(q[0])
    square = y[0] * y[0] + y[1] * y[1] + y[2] * y[2]
    along = y[0] * q[0] + y[1] * q[1] + y[2] * q[2]
    rows = list(q)
    for i in range(3):
        for j in range(3):
            rows += pieces(y[i] * q[j], 2)
    for i in range(3):
        rows += pieces(square * q[i] + y[i] * along, 3)
    rows += [zero] * (FIELD_ROWS - len(rows))
    for k, value in enumerate(rows):
        put(field, k, value)
    if left is None:
        return
    for k, value in enumerate([-2 * v for v in y] + pieces(square + EPS_SQ / 2, 3) + [one] * 3 + [zero] * 7):
        put(left, k, value)


def prepare_target(block, right):
    _, x = split_parts(block)
    one, zero = jnp.ones_like(x[0]), jnp.zeros_like(x[0])
    norm = pieces(x[0] * x[0] + x[1] * x[1] + x[2] * x[2] + EPS_SQ / 2, 3)
    for k, value in enumerate(x + [one] * 3 + norm + [zero] * 7):
        put(right, k, value)


def finish(block, sums):
    _, x = split_parts(block)
    mom = [get(sums, i) for i in range(3)]
    cross = [[get(sums, 3 + 2 * (3 * i + j)) + get(sums, 4 + 2 * (3 * i + j)) for j in range(3)] for i in range(3)]
    dot = x[0] * mom[0] + x[1] * mom[1] + x[2] * mom[2] - (cross[0][0] + cross[1][1] + cross[2][2])
    square = x[0] * x[0] + x[1] * x[1] + x[2] * x[2] + 2 * EPS_SQ
    out = []
    for i in range(3):
        mixed = sum(x[j] * (cross[i][j] + 2 * cross[j][i]) for j in range(3))
        tail = get(sums, 21 + 3 * i) + get(sums, 22 + 3 * i) + get(sums, 23 + 3 * i)
        out.append(((square * mom[i] + x[i] * dot - mixed) + tail) * STOKES_SCALE)
    return out


def near_kernel(ids_lane, first_ref, second_ref, near_first, to_second, field_a, left, field_b, right, sums_a, sums_b):
    own = first_ref.shape[0]
    near_first[...] = jnp.zeros_like(near_first)

    def group(g, carry):
        rows = pl.ds(pl.multiple_of(g * GROUP, GROUP), GROUP)
        ids = second_ref[rows, ids_lane : ids_lane + 128].astype(f32)[:, :own]
        chosen = (ids == lax.broadcasted_iota(jnp.int32, (GROUP, own), 1).astype(f32)).astype(bf16)
        first = jnp.dot(chosen, first_ref[...], preferred_element_type=f32)
        second = second_ref[rows, : 6 * PANELS].astype(f32)
        prepare_source(first, field_a, left)
        prepare_source(second, field_b, None)
        prepare_target(second, right)

        def load(ref, count, s):
            parts = [ref[half, pl.ds(s, count, stride=GROUP), :] for half in range(2)]
            return jnp.concatenate(parts, 1).astype(bf16)

        def apply(field, cube, dim, sums, s):
            total = lax.dot_general(
                load(field, FIELD_ROWS, s), cube, (((1,), (dim,)), ((), ())), preferred_element_type=f32
            )
            for half in range(2):
                sums[half, pl.ds(s, FIELD_ROWS, stride=GROUP), :] = total[:, half * 128 : (half + 1) * 128]

        for start in range(0, GROUP, BATCH):
            batch = range(start, start + BATCH)
            shifted = [
                lax.dot_general(
                    load(left, POINT_ROWS, s),
                    load(right, POINT_ROWS, s),
                    (((0,), (0,)), ((), ())),
                    preferred_element_type=f32,
                )
                for s in batch
            ]
            cubes = []
            for value in shifted:
                inv = lax.rsqrt(value)
                cubes.append((inv * inv * inv).astype(bf16))
            for s, cube in zip(batch, cubes):
                apply(field_a, cube, 0, sums_b, s)
            for s, cube in zip(batch, cubes):
                apply(field_b, cube, 1, sums_a, s)

        for i, value in enumerate(finish(second, sums_b)):
            to_second[rows, i * PANELS : (i + 1) * PANELS] = value
        for i, value in enumerate(finish(first, sums_a)):
            for piece in pieces(value, 3):
                near_first[:, i * PANELS : (i + 1) * PANELS] += lax.dot_general(
                    chosen, piece.astype(bf16), (((0,), (0,)), ((), ())), preferred_element_type=f32
                )
        return carry

    lax.fori_loop(0, second_ref.shape[0] // GROUP, group, 0)


def near_sums(first, second, ids_lane):
    slots = second.shape[0]
    vmem = pl.BlockSpec(memory_space=pltpu.VMEM)

    def rows(count):
        return pltpu.VMEM((2, count * GROUP, 128), f32)

    return pl.pallas_call(
        functools.partial(near_kernel, ids_lane),
        out_shape=[
            jax.ShapeDtypeStruct((first.shape[0], 3 * PANELS), f32),
            jax.ShapeDtypeStruct((slots, 3 * PANELS), f32),
        ],
        in_specs=[vmem] * 2,
        out_specs=[vmem] * 2,
        scratch_shapes=[rows(FIELD_ROWS), rows(POINT_ROWS)] * 2 + [rows(FIELD_ROWS)] * 2,
        compiler_params=pltpu.CompilerParams(vmem_limit_bytes=32 << 20),
        cost_estimate=pl.CostEstimate(
            flops=slots * 2 * 2 * 64 * PANELS * PANELS, bytes_accessed=slots * 9216, transcendentals=0
        ),
    )(first, second)


def far_kernel(start, recv, parents, ends, factors, out, hits):
    parts = parents.shape[1]
    count = ends.shape[1]
    rank = 128 // parts
    for m in range(parts):
        hits[:, m * count : (m + 1) * count] = (parents[:, m : m + 1] == ends[...]).astype(f32).astype(bf16)
    slots = recv.shape[0]
    found = jnp.zeros((128, parts * count), f32)
    for r in range(hits.shape[0] // slots):
        found += lax.dot_general(
            recv[:, start + 128 * r : start + 128 * (r + 1)],
            hits[r * slots : (r + 1) * slots, :],
            (((0,), (0,)), ((), ())),
            preferred_element_type=f32,
        )
    at_ends = sum(found[m * rank : (m + 1) * rank, m * count : (m + 1) * count] for m in range(parts))
    sent = jnp.sum(factors[...] * at_ends[None], axis=1)
    sent = jnp.concatenate([sent[:, count // 2 :], sent[:, : count // 2]], axis=1)
    zero = jnp.zeros_like(sent)
    table = [
        jnp.concatenate([piece if m == k else zero for k in range(parts)], axis=1)
        for piece in pieces(sent, 2)
        for m in range(parts)
    ]
    both = lax.dot_general(
        hits[...],
        jnp.concatenate(table, axis=0).astype(bf16),
        (((1,), (1,)), ((), ())),
        preferred_element_type=f32,
    )
    out[...] = both[:, :128] + both[:, 128:]


def own_lanes(own, rank):
    shape = (own, own * rank)
    return lax.broadcasted_iota(jnp.int32, shape, 1) // rank == lax.broadcasted_iota(jnp.int32, shape, 0)


def join_kernel(density, coords, data):
    panels = density.shape[2]
    for k in range(3):
        data[:, k * panels : (k + 1) * panels] = density[k]
        data[:, (3 + k) * panels : (4 + k) * panels] = coords[k]


def join(density, coords):
    own, parts, panels = density.shape
    vmem = pl.BlockSpec(memory_space=pltpu.VMEM)
    return pl.pallas_call(
        join_kernel,
        out_shape=jax.ShapeDtypeStruct((own, 2 * parts * panels), density.dtype),
        in_specs=[vmem] * 2,
        out_specs=vmem,
        compiler_params=pltpu.CompilerParams(vmem_limit_bytes=8 << 20),
    )(density.transpose(1, 0, 2), coords.transpose(1, 0, 2))


def start_kernel(count, pairs, density_hbm, basis_hbm, transfer_hbm, message, density, basis, transfer, sems):
    sources = (density_hbm, basis_hbm, transfer_hbm)
    targets = (density, basis, transfer)
    copies = [pltpu.make_async_copy(a, b, sems.at[k]) for k, (a, b) in enumerate(zip(sources, targets))]
    for copy in copies:
        copy.start()
    own, rank = density.shape[1], transfer.shape[1]
    mine = own_lanes(own, rank)
    across = (((1,), (1,)), ((), ()))
    ids = lax.rem(pairs[...], own)
    live = lax.broadcasted_iota(jnp.int32, ids.shape, 1) < count[0]
    ids = jnp.where(live, ids, -1).astype(f32)
    copies[0].wait()
    flat = jnp.concatenate([density[i] for i in range(3)], axis=1)
    copies[1].wait()
    every = jnp.where(mine, lax.dot_general(flat, basis[...], across, preferred_element_type=f32), 0.0)
    folded = sum(every[:, k : k + 128] for k in range(0, own * rank, 128))
    moments = sum(folded[:, k : k + rank] for k in range(0, 128, rank))
    copies[2].wait()
    lifted = lax.dot_general(
        moments, transfer[...], across, precision=lax.Precision.HIGHEST, preferred_element_type=f32
    )
    lifted = jnp.sum(jnp.where(mine, lifted, 0.0), axis=0, keepdims=True)
    lifted = jnp.concatenate([lifted[:, k : k + 128] for k in range(0, own * rank, 128)], axis=0)
    rows = message.shape[0]
    block = ids.shape[1] // rows
    for k in range(rows):
        turned = jnp.concatenate([ids[:, k * block :], ids[:, : k * block]], axis=1) if k else ids
        message[k] = jnp.concatenate([lifted, turned], axis=0)


def start(near_count, near_pairs, density, basis, transfer, rows):
    own, rank, width = basis.shape
    vmem, hbm = pl.BlockSpec(memory_space=pltpu.VMEM), pl.BlockSpec(memory_space=pltpu.HBM)
    return pl.pallas_call(
        start_kernel,
        out_shape=jax.ShapeDtypeStruct((rows, own * rank // 128 + 2, near_pairs.shape[1]), f32),
        in_specs=[pl.BlockSpec(memory_space=pltpu.SMEM), vmem] + [hbm] * 3,
        out_specs=vmem,
        scratch_shapes=[
            pltpu.VMEM((3, own, width // 3), density.dtype),
            pltpu.VMEM((own * rank, width), basis.dtype),
            pltpu.VMEM((own * rank, rank), f32),
            pltpu.SemaphoreType.DMA((3,)),
        ],
        compiler_params=pltpu.CompilerParams(vmem_limit_bytes=60 << 20),
    )(
        near_count,
        near_pairs,
        density.transpose(1, 0, 2),
        basis.reshape(own * rank, width),
        transfer.reshape(own * rank, rank),
    )


def end_kernel(back, returned, near_first, basis, transfer, out, velocity, sems):
    own, panels = velocity.shape[1:]
    rank = transfer.shape[1]
    mine = own_lanes(own, rank)
    lift_rows = own * rank // 128
    local = sum(returned[k : k + lift_rows, 3 * panels :] for k in range(0, returned.shape[0], lift_rows))
    local = jnp.concatenate([local[k : k + 1] for k in range(lift_rows)], axis=1)
    coef = jnp.dot(
        jnp.where(mine, local, 0.0), transfer[...], precision=lax.Precision.HIGHEST, preferred_element_type=f32
    )
    coef = pieces(jnp.where(mine, jnp.concatenate([coef] * own, axis=1), 0.0), 3)
    coef = jnp.concatenate(coef, axis=0).astype(bf16)
    slot = lax.broadcasted_iota(jnp.int32, (own, back.shape[1]), 0).astype(f32)
    chosen = (back[...] == slot).astype(f32).astype(bf16)
    copies = []
    for i in range(3):
        lanes = slice(i * panels, (i + 1) * panels)
        far = jnp.dot(coef, basis[:, lanes], preferred_element_type=f32)
        total = far[:own] + far[own : 2 * own] + far[2 * own :]
        for piece in pieces(returned[:, lanes], 3):
            total += jnp.dot(chosen, piece.astype(bf16), preferred_element_type=f32)
        velocity[i] = near_first[:, lanes] + total
        copies.append(pltpu.make_async_copy(velocity.at[i], out.at[i], sems.at[i]))
        copies[-1].start()
    for copy in copies:
        copy.wait()


def end(back, returned, near_first, basis, transfer):
    own, rank, width = basis.shape
    shape = (3, own, width // 3)
    return pl.pallas_call(
        end_kernel,
        out_shape=jax.ShapeDtypeStruct(shape, f32),
        in_specs=[pl.BlockSpec(memory_space=pltpu.VMEM)] * 5,
        out_specs=pl.BlockSpec(memory_space=pltpu.HBM),
        scratch_shapes=[pltpu.VMEM(shape, f32), pltpu.SemaphoreType.DMA((3,))],
        compiler_params=pltpu.CompilerParams(vmem_limit_bytes=8 << 20),
    )(
        back[None],
        returned,
        near_first,
        basis.reshape(own * rank, width),
        transfer.reshape(own * rank, rank),
    ).transpose(1, 0, 2)


def one_hot(ids, count):
    return (ids[:, None] == jnp.arange(count, dtype=ids.dtype)[None, :]).astype(f32)


def shards(density, coords, basis, transfer, parent, near_pairs, near_count, far_pairs, coupling):
    own, _, panels = density.shape
    rank = basis.shape[1]
    rows, cols = lax.axis_size("row"), lax.axis_size("col")
    half = cols // rows
    my_row, my_col = lax.axis_index("row"), lax.axis_index("col")
    slots = near_pairs.shape[1]
    per_pair = slots // cols
    block = slots // rows
    lift_rows = own * rank // 128
    vmem = pl.BlockSpec(memory_space=pltpu.VMEM)

    swap = [
        (r * cols + half * p + h, p * cols + half * r + h)
        for r in range(rows)
        for p in range(rows)
        for h in range(half)
    ]
    message = start(near_count, near_pairs, density, basis, transfer, rows)
    density, coords, message = lax.optimization_barrier((density, coords, message))
    from_row = lax.all_to_all(message, "row", 0, 0, tiled=True)
    data = join(density, coords)
    first_data = lax.ppermute(data, BOTH, swap)
    first_data, from_row = lax.optimization_barrier((first_data, from_row))

    own_first = from_row[:, lift_rows, :block].reshape(-1)
    own_second = from_row[:, lift_rows + 1, :block].reshape(-1)
    place = jnp.arange(slots)
    same_owner = (place // block == my_row) & (half * my_row + place % block // per_pair == my_col)
    back_ids = jnp.where(same_owner & (own_first == own_second), -1.0, own_second)
    picked = jnp.dot(one_hot(own_second, own).astype(bf16), data, preferred_element_type=f32)
    row_lifted = from_row[:, :lift_rows, :].astype(bf16).transpose(1, 0, 2).reshape(lift_rows, -1)
    message = jnp.concatenate(
        [
            picked.astype(bf16),
            jnp.broadcast_to(own_first[:, None], (slots, 128)).astype(bf16),
            jnp.tile(row_lifted, (cols, 1)),
        ],
        axis=1,
    )
    second = lax.all_to_all(message, "col", 0, 0, tiled=True)
    ids_lane = 6 * panels

    factors = jnp.concatenate([coupling.transpose(1, 2, 0), coupling.transpose(2, 1, 0)], axis=2)
    partial = pl.pallas_call(
        functools.partial(far_kernel, ids_lane + 128),
        out_shape=jax.ShapeDtypeStruct((rows * slots, 128), f32),
        in_specs=[vmem] * 4,
        out_specs=vmem,
        scratch_shapes=[pltpu.VMEM((rows * slots, far_pairs.size * (128 // rank)), bf16)],
        compiler_params=pltpu.CompilerParams(vmem_limit_bytes=32 << 20),
    )(second, parent.reshape(-1, 128 // rank), far_pairs[::-1].reshape(1, -1), factors)
    first_data, partial = lax.optimization_barrier((first_data, partial))
    row_locals = lax.all_to_all(partial.reshape(rows, slots, 128), "row", 0, 0, tiled=True)

    near_first, to_second = near_sums(first_data, second, ids_lane)
    near_first = lax.ppermute(near_first, BOTH, swap)
    returned = lax.all_to_all(
        jnp.concatenate([to_second, row_locals.sum(axis=0)], axis=1), "col", 0, 0, tiled=True
    )
    return end(back_ids, returned, near_first, basis, transfer)


def solution(mesh):
    placed = (
        P(BOTH, None, None),
        P(BOTH, None, None),
        P(BOTH, None, None),
        P(BOTH, None, None),
        P(),
        P(None, BOTH),
        P(BOTH),
        P(None, BOTH),
        P(BOTH, None, None),
    )
    return jax.shard_map(
        shards, mesh=mesh, in_specs=placed, out_specs=P(BOTH, None, None), check_vma=False
    )
```

```python
import functools
import math

import jax
import jax.numpy as jnp
from jax import lax
from jax.experimental import pallas as pl
from jax.experimental.pallas import tpu as pltpu
from jax.sharding import PartitionSpec as P

REG_EPS = 0.02
EPS_SQ = REG_EPS * REG_EPS
STOKES_SCALE = 1.0 / (8.0 * math.pi)
BOTH = ("row", "col")
GROUP = 16
BATCH = 8
PANELS = 256
FIELD_ROWS = 32
POINT_ROWS = 16
f32, bf16 = jnp.float32, jnp.bfloat16


def pieces(value, count):
    out = []
    for _ in range(count):
        head = value.astype(bf16).astype(f32)
        out.append(head)
        value = value - head
    return out


def put(ref, row, value):
    for half in range(2):
        ref[half, row * GROUP : (row + 1) * GROUP, :] = value[:, half * 128 : (half + 1) * 128]


def get(ref, row):
    return jnp.concatenate([ref[half, row * GROUP : (row + 1) * GROUP, :] for half in range(2)], 1)


def split_parts(block):
    parts = [block[:, k * PANELS : (k + 1) * PANELS] for k in range(6)]
    return parts[:3], parts[3:]


def prepare_source(block, field, left):
    q, y = split_parts(block)
    one, zero = jnp.ones_like(q[0]), jnp.zeros_like(q[0])
    square = y[0] * y[0] + y[1] * y[1] + y[2] * y[2]
    along = y[0] * q[0] + y[1] * q[1] + y[2] * q[2]
    rows = list(q)
    for i in range(3):
        for j in range(3):
            rows += pieces(y[i] * q[j], 2)
    for i in range(3):
        rows += pieces(square * q[i] + y[i] * along, 3)
    rows += [zero] * (FIELD_ROWS - len(rows))
    for k, value in enumerate(rows):
        put(field, k, value)
    if left is None:
        return
    for k, value in enumerate([-2 * v for v in y] + pieces(square + EPS_SQ / 2, 3) + [one] * 3 + [zero] * 7):
        put(left, k, value)


def prepare_target(block, right):
    _, x = split_parts(block)
    one, zero = jnp.ones_like(x[0]), jnp.zeros_like(x[0])
    norm = pieces(x[0] * x[0] + x[1] * x[1] + x[2] * x[2] + EPS_SQ / 2, 3)
    for k, value in enumerate(x + [one] * 3 + norm + [zero] * 7):
        put(right, k, value)


def finish(block, sums):
    _, x = split_parts(block)
    mom = [get(sums, i) for i in range(3)]
    cross = [[get(sums, 3 + 2 * (3 * i + j)) + get(sums, 4 + 2 * (3 * i + j)) for j in range(3)] for i in range(3)]
    dot = x[0] * mom[0] + x[1] * mom[1] + x[2] * mom[2] - (cross[0][0] + cross[1][1] + cross[2][2])
    square = x[0] * x[0] + x[1] * x[1] + x[2] * x[2] + 2 * EPS_SQ
    out = []
    for i in range(3):
        mixed = sum(x[j] * (cross[i][j] + 2 * cross[j][i]) for j in range(3))
        tail = get(sums, 21 + 3 * i) + get(sums, 22 + 3 * i) + get(sums, 23 + 3 * i)
        out.append(((square * mom[i] + x[i] * dot - mixed) + tail) * STOKES_SCALE)
    return out


def near_kernel(ids_lane, first_ref, second_ref, near_first, to_second, field_a, left, field_b, right, sums_a, sums_b):
    own = first_ref.shape[0]
    near_first[...] = jnp.zeros_like(near_first)

    def group(g, carry):
        rows = pl.ds(pl.multiple_of(g * GROUP, GROUP), GROUP)
        ids = second_ref[rows, ids_lane : ids_lane + 128].astype(f32)[:, :own]
        chosen = (ids == lax.broadcasted_iota(jnp.int32, (GROUP, own), 1).astype(f32)).astype(bf16)
        first = jnp.dot(chosen, first_ref[...], preferred_element_type=f32)
        second = second_ref[rows, : 6 * PANELS].astype(f32)
        prepare_source(first, field_a, left)
        prepare_source(second, field_b, None)
        prepare_target(second, right)

        def load(ref, count, s):
            parts = [ref[half, pl.ds(s, count, stride=GROUP), :] for half in range(2)]
            return jnp.concatenate(parts, 1).astype(bf16)

        def apply(field, cube, dim, sums, s):
            total = lax.dot_general(
                load(field, FIELD_ROWS, s), cube, (((1,), (dim,)), ((), ())), preferred_element_type=f32
            )
            for half in range(2):
                sums[half, pl.ds(s, FIELD_ROWS, stride=GROUP), :] = total[:, half * 128 : (half + 1) * 128]

        for start in range(0, GROUP, BATCH):
            batch = range(start, start + BATCH)
            shifted = [
                lax.dot_general(
                    load(left, POINT_ROWS, s),
                    load(right, POINT_ROWS, s),
                    (((0,), (0,)), ((), ())),
                    preferred_element_type=f32,
                )
                for s in batch
            ]
            cubes = []
            for value in shifted:
                inv = lax.rsqrt(value)
                cubes.append((inv * inv * inv).astype(bf16))
            for s, cube in zip(batch, cubes):
                apply(field_a, cube, 0, sums_b, s)
            for s, cube in zip(batch, cubes):
                apply(field_b, cube, 1, sums_a, s)

        for i, value in enumerate(finish(second, sums_b)):
            to_second[rows, i * PANELS : (i + 1) * PANELS] = value
        for i, value in enumerate(finish(first, sums_a)):
            for piece in pieces(value, 3):
                near_first[:, i * PANELS : (i + 1) * PANELS] += lax.dot_general(
                    chosen, piece.astype(bf16), (((0,), (0,)), ((), ())), preferred_element_type=f32
                )
        return carry

    lax.fori_loop(0, second_ref.shape[0] // GROUP, group, 0)


def near_sums(first, second, ids_lane):
    slots = second.shape[0]
    vmem = pl.BlockSpec(memory_space=pltpu.VMEM)

    def rows(count):
        return pltpu.VMEM((2, count * GROUP, 128), f32)

    return pl.pallas_call(
        functools.partial(near_kernel, ids_lane),
        out_shape=[
            jax.ShapeDtypeStruct((first.shape[0], 3 * PANELS), f32),
            jax.ShapeDtypeStruct((slots, 3 * PANELS), f32),
        ],
        in_specs=[vmem] * 2,
        out_specs=[vmem] * 2,
        scratch_shapes=[rows(FIELD_ROWS), rows(POINT_ROWS)] * 2 + [rows(FIELD_ROWS)] * 2,
        compiler_params=pltpu.CompilerParams(vmem_limit_bytes=32 << 20),
        cost_estimate=pl.CostEstimate(
            flops=slots * 2 * 2 * 64 * PANELS * PANELS, bytes_accessed=slots * 9216, transcendentals=0
        ),
    )(first, second)


def hits_kernel(parents, ends, hits):
    count = ends.shape[1]
    for m in range(parents.shape[1]):
        hits[:, m * count : (m + 1) * count] = (parents[:, m : m + 1] == ends[...]).astype(f32).astype(bf16)


def far_kernel(start, recv, hits, factors, out):
    count = factors.shape[2]
    parts = hits.shape[1] // count
    rank = 128 // parts
    slots = recv.shape[0]
    found = jnp.zeros((128, parts * count), f32)
    for r in range(hits.shape[0] // slots):
        found += lax.dot_general(
            recv[:, start + 128 * r : start + 128 * (r + 1)],
            hits[r * slots : (r + 1) * slots, :],
            (((0,), (0,)), ((), ())),
            preferred_element_type=f32,
        )
    at_ends = sum(found[m * rank : (m + 1) * rank, m * count : (m + 1) * count] for m in range(parts))
    sent = jnp.sum(factors[...] * at_ends[None], axis=1)
    sent = jnp.concatenate([sent[:, count // 2 :], sent[:, : count // 2]], axis=1)
    zero = jnp.zeros_like(sent)
    table = [
        jnp.concatenate([piece if m == k else zero for k in range(parts)], axis=1)
        for piece in pieces(sent, 2)
        for m in range(parts)
    ]
    both = lax.dot_general(
        hits[...],
        jnp.concatenate(table, axis=0).astype(bf16),
        (((1,), (1,)), ((), ())),
        preferred_element_type=f32,
    )
    out[...] = both[:, :128] + both[:, 128:]


def own_lanes(own, rank):
    shape = (own, own * rank)
    return lax.broadcasted_iota(jnp.int32, shape, 1) // rank == lax.broadcasted_iota(jnp.int32, shape, 0)


def join_kernel(density, coords, data):
    panels = density.shape[2]
    for k in range(3):
        data[:, k * panels : (k + 1) * panels] = density[k]
        data[:, (3 + k) * panels : (4 + k) * panels] = coords[k]


def join(density, coords):
    own, parts, panels = density.shape
    vmem = pl.BlockSpec(memory_space=pltpu.VMEM)
    return pl.pallas_call(
        join_kernel,
        out_shape=jax.ShapeDtypeStruct((own, 2 * parts * panels), density.dtype),
        in_specs=[vmem] * 2,
        out_specs=vmem,
        compiler_params=pltpu.CompilerParams(vmem_limit_bytes=8 << 20),
    )(density.transpose(1, 0, 2), coords.transpose(1, 0, 2))


def start_kernel(count, pairs, density_hbm, basis_hbm, transfer_hbm, message, density, basis, transfer, sems):
    sources = (density_hbm, basis_hbm, transfer_hbm)
    targets = (density, basis, transfer)
    copies = [pltpu.make_async_copy(a, b, sems.at[k]) for k, (a, b) in enumerate(zip(sources, targets))]
    for copy in copies:
        copy.start()
    own, rank = density.shape[1], transfer.shape[1]
    mine = own_lanes(own, rank)
    across = (((1,), (1,)), ((), ()))
    ids = lax.rem(pairs[...], own)
    live = lax.broadcasted_iota(jnp.int32, ids.shape, 1) < count[0]
    ids = jnp.where(live, ids, -1).astype(f32)
    copies[0].wait()
    flat = jnp.concatenate([density[i] for i in range(3)], axis=1)
    copies[1].wait()
    every = jnp.where(mine, lax.dot_general(flat, basis[...], across, preferred_element_type=f32), 0.0)
    folded = sum(every[:, k : k + 128] for k in range(0, own * rank, 128))
    moments = sum(folded[:, k : k + rank] for k in range(0, 128, rank))
    copies[2].wait()
    lifted = lax.dot_general(
        moments, transfer[...], across, precision=lax.Precision.HIGHEST, preferred_element_type=f32
    )
    lifted = jnp.sum(jnp.where(mine, lifted, 0.0), axis=0, keepdims=True)
    lifted = jnp.concatenate([lifted[:, k : k + 128] for k in range(0, own * rank, 128)], axis=0)
    rows = message.shape[0]
    block = ids.shape[1] // rows
    for k in range(rows):
        turned = jnp.concatenate([ids[:, k * block :], ids[:, : k * block]], axis=1) if k else ids
        message[k] = jnp.concatenate([lifted, turned], axis=0)


def start(near_count, near_pairs, density, basis, transfer, rows):
    own, rank, width = basis.shape
    vmem, hbm = pl.BlockSpec(memory_space=pltpu.VMEM), pl.BlockSpec(memory_space=pltpu.HBM)
    return pl.pallas_call(
        start_kernel,
        out_shape=jax.ShapeDtypeStruct((rows, own * rank // 128 + 2, near_pairs.shape[1]), f32),
        in_specs=[pl.BlockSpec(memory_space=pltpu.SMEM), vmem] + [hbm] * 3,
        out_specs=vmem,
        scratch_shapes=[
            pltpu.VMEM((3, own, width // 3), density.dtype),
            pltpu.VMEM((own * rank, width), basis.dtype),
            pltpu.VMEM((own * rank, rank), f32),
            pltpu.SemaphoreType.DMA((3,)),
        ],
        compiler_params=pltpu.CompilerParams(vmem_limit_bytes=60 << 20),
    )(
        near_count,
        near_pairs,
        density.transpose(1, 0, 2),
        basis.reshape(own * rank, width),
        transfer.reshape(own * rank, rank),
    )


def end_kernel(back, returned, near_first, basis, transfer, out, velocity, sems):
    own, panels = velocity.shape[1:]
    rank = transfer.shape[1]
    mine = own_lanes(own, rank)
    lift_rows = own * rank // 128
    local = sum(returned[k : k + lift_rows, 3 * panels :] for k in range(0, returned.shape[0], lift_rows))
    local = jnp.concatenate([local[k : k + 1] for k in range(lift_rows)], axis=1)
    coef = jnp.dot(
        jnp.where(mine, local, 0.0), transfer[...], precision=lax.Precision.HIGHEST, preferred_element_type=f32
    )
    coef = pieces(jnp.where(mine, jnp.concatenate([coef] * own, axis=1), 0.0), 3)
    coef = jnp.concatenate(coef, axis=0).astype(bf16)
    slot = lax.broadcasted_iota(jnp.int32, (own, back.shape[1]), 0).astype(f32)
    chosen = (back[...] == slot).astype(f32).astype(bf16)
    copies = []
    for i in range(3):
        lanes = slice(i * panels, (i + 1) * panels)
        far = jnp.dot(coef, basis[:, lanes], preferred_element_type=f32)
        total = far[:own] + far[own : 2 * own] + far[2 * own :]
        for piece in pieces(returned[:, lanes], 3):
            total += jnp.dot(chosen, piece.astype(bf16), preferred_element_type=f32)
        velocity[i] = near_first[:, lanes] + total
        copies.append(pltpu.make_async_copy(velocity.at[i], out.at[i], sems.at[i]))
        copies[-1].start()
    for copy in copies:
        copy.wait()


def end(back, returned, near_first, basis, transfer):
    own, rank, width = basis.shape
    shape = (3, own, width // 3)
    return pl.pallas_call(
        end_kernel,
        out_shape=jax.ShapeDtypeStruct(shape, f32),
        in_specs=[pl.BlockSpec(memory_space=pltpu.VMEM)] * 5,
        out_specs=pl.BlockSpec(memory_space=pltpu.HBM),
        scratch_shapes=[pltpu.VMEM(shape, f32), pltpu.SemaphoreType.DMA((3,))],
        compiler_params=pltpu.CompilerParams(vmem_limit_bytes=8 << 20),
    )(
        back[None],
        returned,
        near_first,
        basis.reshape(own * rank, width),
        transfer.reshape(own * rank, rank),
    ).transpose(1, 0, 2)


def one_hot(ids, count):
    return (ids[:, None] == jnp.arange(count, dtype=ids.dtype)[None, :]).astype(f32)


def seat(p, r, h, rows):
    hops = rows // 2
    near = (2 * (p % 2) + h, 2 * (p % 2) + (3 * h - 1))[r % 2] % hops
    return (r // 2 + hops // 2) % hops * hops + near


def shards(density, coords, basis, transfer, parent, near_pairs, near_count, far_pairs, coupling):
    own, _, panels = density.shape
    rank = basis.shape[1]
    rows, cols = lax.axis_size("row"), lax.axis_size("col")
    half = cols // rows
    my_row, my_col = lax.axis_index("row"), lax.axis_index("col")
    slots = near_pairs.shape[1]
    per_pair = slots // cols
    block = slots // rows
    lift_rows = own * rank // 128
    vmem = pl.BlockSpec(memory_space=pltpu.VMEM)

    swap = [
        (r * cols + half * p + h, p * cols + seat(p, r, h, rows))
        for r in range(rows)
        for p in range(rows)
        for h in range(half)
    ]
    home = [(there, here) for here, there in swap]
    message = start(near_count, near_pairs, density, basis, transfer, rows)
    density, coords, message = lax.optimization_barrier((density, coords, message))
    from_row = lax.all_to_all(message, "row", 0, 0, tiled=True)
    data = join(density, coords)
    first_data = lax.ppermute(data, BOTH, swap)
    first_data, from_row = lax.optimization_barrier((first_data, from_row))

    ids = from_row[:, lift_rows:, :block].reshape(rows, 2, half, per_pair)
    same_owner = (jnp.arange(rows)[:, None] == my_row) & (half * my_row + jnp.arange(half) == my_col)
    back_ids = jnp.where(same_owner[:, :, None] & (ids[:, 0] == ids[:, 1]), -1.0, ids[:, 1])
    ids = jnp.concatenate([ids, back_ids[:, None]], axis=1)
    orders = [sorted((seat(p, r, h, rows), r, h) for r in range(rows) for h in range(half)) for p in range(2)]
    even, odd = (jnp.stack([ids[r, :, h] for _, r, h in order], axis=1).reshape(3, slots) for order in orders)
    own_first, own_second, back_ids = jnp.where(my_row % 2 == 0, even, odd)
    picked = jnp.dot(one_hot(own_second, own).astype(bf16), data, preferred_element_type=f32)
    row_lifted = from_row[:, :lift_rows, :].astype(bf16).transpose(1, 0, 2).reshape(lift_rows, -1)
    message = jnp.concatenate(
        [
            picked.astype(bf16),
            jnp.broadcast_to(own_first[:, None], (slots, 128)).astype(bf16),
            jnp.tile(row_lifted, (cols, 1)),
        ],
        axis=1,
    )
    second = lax.all_to_all(message, "col", 0, 0, tiled=True)
    ids_lane = 6 * panels

    factors = jnp.concatenate([coupling.transpose(1, 2, 0), coupling.transpose(2, 1, 0)], axis=2)
    parents, from_row = lax.optimization_barrier((parent.reshape(-1, 128 // rank), from_row))
    hits = pl.pallas_call(
        hits_kernel,
        out_shape=jax.ShapeDtypeStruct((rows * slots, far_pairs.size * (128 // rank)), bf16),
        in_specs=[vmem] * 2,
        out_specs=vmem,
        compiler_params=pltpu.CompilerParams(vmem_limit_bytes=16 << 20),
    )(parents, far_pairs[::-1].reshape(1, -1))
    partial = pl.pallas_call(
        functools.partial(far_kernel, ids_lane + 128),
        out_shape=jax.ShapeDtypeStruct((rows * slots, 128), f32),
        in_specs=[vmem] * 3,
        out_specs=vmem,
        compiler_params=pltpu.CompilerParams(vmem_limit_bytes=16 << 20),
    )(second, hits, factors)
    first_data, partial = lax.optimization_barrier((first_data, partial))
    row_locals = lax.all_to_all(partial.reshape(rows, slots, 128), "row", 0, 0, tiled=True)

    near_first, to_second = near_sums(first_data, second, ids_lane)
    near_first = lax.ppermute(near_first, BOTH, home)
    returned = lax.all_to_all(
        jnp.concatenate([to_second, row_locals.sum(axis=0)], axis=1), "col", 0, 0, tiled=True
    )
    return end(back_ids, returned, near_first, basis, transfer)


def solution(mesh):
    placed = (
        P(BOTH, None, None),
        P(BOTH, None, None),
        P(BOTH, None, None),
        P(BOTH, None, None),
        P(),
        P(None, BOTH),
        P(BOTH),
        P(None, BOTH),
        P(BOTH, None, None),
    )
    return jax.shard_map(
        shards, mesh=mesh, in_specs=placed, out_specs=P(BOTH, None, None), check_vma=False
    )
```

```python
import functools
import math

import jax
import jax.numpy as jnp
from jax import lax
from jax.experimental import pallas as pl
from jax.experimental.pallas import tpu as pltpu
from jax.sharding import PartitionSpec as P

REG_EPS = 0.02
EPS_SQ = REG_EPS * REG_EPS
STOKES_SCALE = 1.0 / (8.0 * math.pi)
BOTH = ("row", "col")
GROUP = 16
BATCH = 8
PANELS = 256
FIELD_ROWS = 32
POINT_ROWS = 16
f32, bf16 = jnp.float32, jnp.bfloat16


def pieces(value, count):
    out = []
    for _ in range(count):
        head = value.astype(bf16).astype(f32)
        out.append(head)
        value = value - head
    return out


def put(ref, row, value):
    for half in range(2):
        ref[half, row * GROUP : (row + 1) * GROUP, :] = value[:, half * 128 : (half + 1) * 128]


def get(ref, row):
    return jnp.concatenate([ref[half, row * GROUP : (row + 1) * GROUP, :] for half in range(2)], 1)


def split_parts(block):
    parts = [block[:, k * PANELS : (k + 1) * PANELS] for k in range(6)]
    return parts[:3], parts[3:]


def prepare_source(block, field, left):
    q, y = split_parts(block)
    one, zero = jnp.ones_like(q[0]), jnp.zeros_like(q[0])
    square = y[0] * y[0] + y[1] * y[1] + y[2] * y[2]
    along = y[0] * q[0] + y[1] * q[1] + y[2] * q[2]
    rows = list(q)
    for i in range(3):
        for j in range(3):
            rows += pieces(y[i] * q[j], 2)
    for i in range(3):
        rows += pieces(square * q[i] + y[i] * along, 3)
    rows += [zero] * (FIELD_ROWS - len(rows))
    for k, value in enumerate(rows):
        put(field, k, value)
    if left is None:
        return
    for k, value in enumerate([-2 * v for v in y] + pieces(square + EPS_SQ / 2, 3) + [one] * 3 + [zero] * 7):
        put(left, k, value)


def prepare_target(block, right):
    _, x = split_parts(block)
    one, zero = jnp.ones_like(x[0]), jnp.zeros_like(x[0])
    norm = pieces(x[0] * x[0] + x[1] * x[1] + x[2] * x[2] + EPS_SQ / 2, 3)
    for k, value in enumerate(x + [one] * 3 + norm + [zero] * 7):
        put(right, k, value)


def finish(block, sums):
    _, x = split_parts(block)
    mom = [get(sums, i) for i in range(3)]
    cross = [[get(sums, 3 + 2 * (3 * i + j)) + get(sums, 4 + 2 * (3 * i + j)) for j in range(3)] for i in range(3)]
    dot = x[0] * mom[0] + x[1] * mom[1] + x[2] * mom[2] - (cross[0][0] + cross[1][1] + cross[2][2])
    square = x[0] * x[0] + x[1] * x[1] + x[2] * x[2] + 2 * EPS_SQ
    out = []
    for i in range(3):
        mixed = sum(x[j] * (cross[i][j] + 2 * cross[j][i]) for j in range(3))
        tail = get(sums, 21 + 3 * i) + get(sums, 22 + 3 * i) + get(sums, 23 + 3 * i)
        out.append(((square * mom[i] + x[i] * dot - mixed) + tail) * STOKES_SCALE)
    return out


def near_kernel(ids_lane, first_ref, second_ref, near_first, to_second, field_a, left, field_b, right, sums_a, sums_b):
    own = first_ref.shape[0]
    near_first[...] = jnp.zeros_like(near_first)

    def group(g, carry):
        rows = pl.ds(pl.multiple_of(g * GROUP, GROUP), GROUP)
        ids = second_ref[rows, ids_lane : ids_lane + 128].astype(f32)[:, :own]
        chosen = (ids == lax.broadcasted_iota(jnp.int32, (GROUP, own), 1).astype(f32)).astype(bf16)
        first = jnp.dot(chosen, first_ref[...], preferred_element_type=f32)
        second = second_ref[rows, : 6 * PANELS].astype(f32)
        prepare_source(first, field_a, left)
        prepare_source(second, field_b, None)
        prepare_target(second, right)

        def load(ref, count, s):
            parts = [ref[half, pl.ds(s, count, stride=GROUP), :] for half in range(2)]
            return jnp.concatenate(parts, 1).astype(bf16)

        def apply(field, cube, dim, sums, s):
            total = lax.dot_general(
                load(field, FIELD_ROWS, s), cube, (((1,), (dim,)), ((), ())), preferred_element_type=f32
            )
            for half in range(2):
                sums[half, pl.ds(s, FIELD_ROWS, stride=GROUP), :] = total[:, half * 128 : (half + 1) * 128]

        for start in range(0, GROUP, BATCH):
            batch = range(start, start + BATCH)
            shifted = [
                lax.dot_general(
                    load(left, POINT_ROWS, s),
                    load(right, POINT_ROWS, s),
                    (((0,), (0,)), ((), ())),
                    preferred_element_type=f32,
                )
                for s in batch
            ]
            cubes = []
            for value in shifted:
                inv = lax.rsqrt(value)
                cubes.append((inv * inv * inv).astype(bf16))
            for s, cube in zip(batch, cubes):
                apply(field_a, cube, 0, sums_b, s)
            for s, cube in zip(batch, cubes):
                apply(field_b, cube, 1, sums_a, s)

        for i, value in enumerate(finish(second, sums_b)):
            to_second[rows, i * PANELS : (i + 1) * PANELS] = value
        for i, value in enumerate(finish(first, sums_a)):
            for piece in pieces(value, 3):
                near_first[:, i * PANELS : (i + 1) * PANELS] += lax.dot_general(
                    chosen, piece.astype(bf16), (((0,), (0,)), ((), ())), preferred_element_type=f32
                )
        return carry

    lax.fori_loop(0, second_ref.shape[0] // GROUP, group, 0)


def near_sums(first, second, ids_lane):
    slots = second.shape[0]
    vmem = pl.BlockSpec(memory_space=pltpu.VMEM)

    def rows(count):
        return pltpu.VMEM((2, count * GROUP, 128), f32)

    return pl.pallas_call(
        functools.partial(near_kernel, ids_lane),
        out_shape=[
            jax.ShapeDtypeStruct((first.shape[0], 3 * PANELS), f32),
            jax.ShapeDtypeStruct((slots, 3 * PANELS), f32),
        ],
        in_specs=[vmem] * 2,
        out_specs=[vmem] * 2,
        scratch_shapes=[rows(FIELD_ROWS), rows(POINT_ROWS)] * 2 + [rows(FIELD_ROWS)] * 2,
        compiler_params=pltpu.CompilerParams(vmem_limit_bytes=32 << 20),
        cost_estimate=pl.CostEstimate(
            flops=slots * 2 * 2 * 64 * PANELS * PANELS, bytes_accessed=slots * 9216, transcendentals=0
        ),
    )(first, second)


def hits_kernel(parents, ends, hits):
    count = ends.shape[1]
    for m in range(parents.shape[1]):
        hits[:, m * count : (m + 1) * count] = (parents[:, m : m + 1] == ends[...]).astype(f32).astype(bf16)


def far_kernel(start, recv, hits, factors, out):
    count = factors.shape[2]
    parts = hits.shape[1] // count
    rank = 128 // parts
    slots = recv.shape[0]
    found = jnp.zeros((128, parts * count), f32)
    for r in range(hits.shape[0] // slots):
        found += lax.dot_general(
            recv[:, start + 128 * r : start + 128 * (r + 1)],
            hits[r * slots : (r + 1) * slots, :],
            (((0,), (0,)), ((), ())),
            preferred_element_type=f32,
        )
    at_ends = sum(found[m * rank : (m + 1) * rank, m * count : (m + 1) * count] for m in range(parts))
    sent = jnp.sum(factors[...] * at_ends[None], axis=1)
    sent = jnp.concatenate([sent[:, count // 2 :], sent[:, : count // 2]], axis=1)
    zero = jnp.zeros_like(sent)
    table = [
        jnp.concatenate([piece if m == k else zero for k in range(parts)], axis=1)
        for piece in pieces(sent, 2)
        for m in range(parts)
    ]
    both = lax.dot_general(
        hits[...],
        jnp.concatenate(table, axis=0).astype(bf16),
        (((1,), (1,)), ((), ())),
        preferred_element_type=f32,
    )
    out[...] = both[:, :128] + both[:, 128:]


def own_lanes(own, rank):
    shape = (own, own * rank)
    return lax.broadcasted_iota(jnp.int32, shape, 1) // rank == lax.broadcasted_iota(jnp.int32, shape, 0)


def join_kernel(density, coords, data):
    panels = density.shape[2]
    for k in range(3):
        data[:, k * panels : (k + 1) * panels] = density[k]
        data[:, (3 + k) * panels : (4 + k) * panels] = coords[k]


def join(density, coords):
    own, parts, panels = density.shape
    vmem = pl.BlockSpec(memory_space=pltpu.VMEM)
    return pl.pallas_call(
        join_kernel,
        out_shape=jax.ShapeDtypeStruct((own, 2 * parts * panels), density.dtype),
        in_specs=[vmem] * 2,
        out_specs=vmem,
        compiler_params=pltpu.CompilerParams(vmem_limit_bytes=8 << 20),
    )(density.transpose(1, 0, 2), coords.transpose(1, 0, 2))


def start_kernel(count, pairs, density_hbm, basis_hbm, transfer_hbm, message, density, basis, transfer, sems):
    sources = (density_hbm, basis_hbm, transfer_hbm)
    targets = (density, basis, transfer)
    copies = [pltpu.make_async_copy(a, b, sems.at[k]) for k, (a, b) in enumerate(zip(sources, targets))]
    for copy in copies:
        copy.start()
    own, rank = density.shape[1], transfer.shape[1]
    mine = own_lanes(own, rank)
    across = (((1,), (1,)), ((), ()))
    ids = lax.rem(pairs[...], own)
    live = lax.broadcasted_iota(jnp.int32, ids.shape, 1) < count[0]
    ids = jnp.where(live, ids, -1).astype(f32)
    copies[0].wait()
    flat = jnp.concatenate([density[i] for i in range(3)], axis=1)
    copies[1].wait()
    every = jnp.where(mine, lax.dot_general(flat, basis[...], across, preferred_element_type=f32), 0.0)
    folded = sum(every[:, k : k + 128] for k in range(0, own * rank, 128))
    moments = sum(folded[:, k : k + rank] for k in range(0, 128, rank))
    copies[2].wait()
    wide = jnp.concatenate(pieces(moments, 3), axis=0).astype(bf16)
    lifted = sum(
        lax.dot_general(wide, piece.astype(bf16), across, preferred_element_type=f32)
        for piece in pieces(transfer[...], 2)
    )
    lifted = lifted[:own] + lifted[own : 2 * own] + lifted[2 * own :]
    lifted = jnp.sum(jnp.where(mine, lifted, 0.0), axis=0, keepdims=True)
    lifted = jnp.concatenate([lifted[:, k : k + 128] for k in range(0, own * rank, 128)], axis=0)
    rows = message.shape[0]
    block = ids.shape[1] // rows
    for k in range(rows):
        turned = jnp.concatenate([ids[:, k * block :], ids[:, : k * block]], axis=1) if k else ids
        message[k] = jnp.concatenate([lifted, turned], axis=0)


def start(near_count, near_pairs, density, basis, transfer, rows):
    own, rank, width = basis.shape
    vmem, hbm = pl.BlockSpec(memory_space=pltpu.VMEM), pl.BlockSpec(memory_space=pltpu.HBM)
    return pl.pallas_call(
        start_kernel,
        out_shape=jax.ShapeDtypeStruct((rows, own * rank // 128 + 2, near_pairs.shape[1]), f32),
        in_specs=[pl.BlockSpec(memory_space=pltpu.SMEM), vmem] + [hbm] * 3,
        out_specs=vmem,
        scratch_shapes=[
            pltpu.VMEM((3, own, width // 3), density.dtype),
            pltpu.VMEM((own * rank, width), basis.dtype),
            pltpu.VMEM((own * rank, rank), f32),
            pltpu.SemaphoreType.DMA((3,)),
        ],
        compiler_params=pltpu.CompilerParams(vmem_limit_bytes=60 << 20),
    )(
        near_count,
        near_pairs,
        density.transpose(1, 0, 2),
        basis.reshape(own * rank, width),
        transfer.reshape(own * rank, rank),
    )


def pick_kernel(orders, place, from_row, data, message_hbm, back, message, sems):
    rows, lift_rows = from_row.shape[0], from_row.shape[1] - 2
    own, wide = data.shape
    slots = message.shape[0]
    seats = len(orders[0])
    per_pair = slots // seats
    half = seats // rows

    def send(begin, stop):
        lanes = pl.ds(begin, stop - begin)
        copy = pltpu.make_async_copy(message.at[:, lanes], message_hbm.at[:, lanes], sems.at[min(begin, 1)])
        copy.start()
        return copy

    for r in range(rows):
        lifted = from_row[r, :lift_rows, :]
        lanes = slice(wide + 128 * (r + 1), wide + 128 * (r + 2))
        message[:, lanes] = jnp.concatenate([lifted] * (slots // lift_rows), axis=0).astype(bf16)
    copies = [send(wide + 128, message.shape[1])]
    lane = lax.broadcasted_iota(jnp.int32, (1, 128), 1)
    triples = []
    for r in range(rows):
        first, second = from_row[r, lift_rows : lift_rows + 1, :], from_row[r, lift_rows + 1 :, :]
        same = (place[0] == r) & (half * place[0] + lane // per_pair == place[1]) & (first == second)
        triples.append(jnp.concatenate([first, second, jnp.where(same, -1.0, second)], axis=0))
    even, odd = (
        jnp.concatenate([triples[r][:, h * per_pair : (h + 1) * per_pair] for r, h in order], axis=1)
        for order in orders
    )
    ids = jnp.where(place[0] % 2 == 0, even, odd)
    back[...] = ids[2:]
    down = (((0,), (0,)), ((), ()))
    cluster = lax.broadcasted_iota(jnp.int32, (own, slots), 0).astype(f32)
    first, second = ((ids[k : k + 1] == cluster).astype(f32).astype(bf16) for k in range(2))
    message[:, :wide] = lax.dot_general(second, data[...], down, preferred_element_type=f32).astype(bf16)
    names = (lax.broadcasted_iota(jnp.int32, (own, 128), 0) + 1).astype(f32).astype(bf16)
    names = lax.dot_general(first, names, down, preferred_element_type=f32) - 1.0
    message[:, wide : wide + 128] = names.astype(bf16)
    copies.append(send(0, wide + 128))
    for copy in copies:
        copy.wait()


def pick(place, from_row, data, slots, orders):
    vmem = pl.BlockSpec(memory_space=pltpu.VMEM)
    wide = data.shape[1] + 128 * (1 + from_row.shape[0])
    return pl.pallas_call(
        functools.partial(pick_kernel, orders),
        out_shape=[jax.ShapeDtypeStruct((slots, wide), bf16), jax.ShapeDtypeStruct((1, slots), f32)],
        in_specs=[pl.BlockSpec(memory_space=pltpu.SMEM)] + [vmem] * 2,
        out_specs=[pl.BlockSpec(memory_space=pltpu.HBM), vmem],
        scratch_shapes=[pltpu.VMEM((slots, wide), bf16), pltpu.SemaphoreType.DMA((2,))],
        compiler_params=pltpu.CompilerParams(vmem_limit_bytes=8 << 20),
    )(place, from_row, data)


def end_kernel(back, returned, near_first, basis, transfer, out, velocity, sems):
    own, panels = velocity.shape[1:]
    rank = transfer.shape[1]
    mine = own_lanes(own, rank)
    lift_rows = own * rank // 128
    local = sum(returned[k : k + lift_rows, 3 * panels :] for k in range(0, returned.shape[0], lift_rows))
    local = jnp.concatenate([local[k : k + 1] for k in range(lift_rows)], axis=1)
    coef = jnp.dot(
        jnp.where(mine, local, 0.0), transfer[...], precision=lax.Precision.HIGHEST, preferred_element_type=f32
    )
    coef = pieces(jnp.where(mine, jnp.concatenate([coef] * own, axis=1), 0.0), 3)
    coef = jnp.concatenate(coef, axis=0).astype(bf16)
    slot = lax.broadcasted_iota(jnp.int32, (own, back.shape[1]), 0).astype(f32)
    chosen = (back[...] == slot).astype(f32).astype(bf16)
    copies = []
    for i in range(3):
        lanes = slice(i * panels, (i + 1) * panels)
        far = jnp.dot(coef, basis[:, lanes], preferred_element_type=f32)
        total = far[:own] + far[own : 2 * own] + far[2 * own :]
        for piece in pieces(returned[:, lanes], 3):
            total += jnp.dot(chosen, piece.astype(bf16), preferred_element_type=f32)
        velocity[i] = near_first[:, lanes] + total
        copies.append(pltpu.make_async_copy(velocity.at[i], out.at[i], sems.at[i]))
        copies[-1].start()
    for copy in copies:
        copy.wait()


def end(back, returned, near_first, basis, transfer):
    own, rank, width = basis.shape
    shape = (3, own, width // 3)
    return pl.pallas_call(
        end_kernel,
        out_shape=jax.ShapeDtypeStruct(shape, f32),
        in_specs=[pl.BlockSpec(memory_space=pltpu.VMEM)] * 5,
        out_specs=pl.BlockSpec(memory_space=pltpu.HBM),
        scratch_shapes=[pltpu.VMEM(shape, f32), pltpu.SemaphoreType.DMA((3,))],
        compiler_params=pltpu.CompilerParams(vmem_limit_bytes=8 << 20),
    )(
        back,
        returned,
        near_first,
        basis.reshape(own * rank, width),
        transfer.reshape(own * rank, rank),
    ).transpose(1, 0, 2)


def seat(p, r, h, rows):
    hops = rows // 2
    near = (2 * (p % 2) + h, 2 * (p % 2) + (3 * h - 1))[r % 2] % hops
    return (r // 2 + hops // 2) % hops * hops + near


def shards(density, coords, basis, transfer, parent, near_pairs, near_count, far_pairs, coupling):
    own, _, panels = density.shape
    rank = basis.shape[1]
    rows, cols = lax.axis_size("row"), lax.axis_size("col")
    half = cols // rows
    slots = near_pairs.shape[1]
    vmem = pl.BlockSpec(memory_space=pltpu.VMEM)

    swap = [
        (r * cols + half * p + h, p * cols + seat(p, r, h, rows))
        for r in range(rows)
        for p in range(rows)
        for h in range(half)
    ]
    home = [(there, here) for here, there in swap]
    message = start(near_count, near_pairs, density, basis, transfer, rows)
    density, coords, message = lax.optimization_barrier((density, coords, message))
    from_row = lax.all_to_all(message, "row", 0, 0, tiled=True)
    data = join(density, coords)
    first_data = lax.ppermute(data, BOTH, swap)

    place = jnp.stack([lax.axis_index("row"), lax.axis_index("col")])
    orders = [sorted((seat(p, r, h, rows), r, h) for r in range(rows) for h in range(half)) for p in range(2)]
    orders = [[(r, h) for _, r, h in order] for order in orders]
    message, back_ids = pick(place, from_row, data, slots, orders)
    second = lax.all_to_all(message, "col", 0, 0, tiled=True)
    ids_lane = 6 * panels

    factors = jnp.concatenate([coupling.transpose(1, 2, 0), coupling.transpose(2, 1, 0)], axis=2)
    parents, from_row = lax.optimization_barrier((parent.reshape(-1, 128 // rank), from_row))
    hits = pl.pallas_call(
        hits_kernel,
        out_shape=jax.ShapeDtypeStruct((rows * slots, far_pairs.size * (128 // rank)), bf16),
        in_specs=[vmem] * 2,
        out_specs=vmem,
        compiler_params=pltpu.CompilerParams(vmem_limit_bytes=16 << 20),
    )(parents, far_pairs[::-1].reshape(1, -1))
    partial = pl.pallas_call(
        functools.partial(far_kernel, ids_lane + 128),
        out_shape=jax.ShapeDtypeStruct((rows * slots, 128), f32),
        in_specs=[vmem] * 3,
        out_specs=vmem,
        compiler_params=pltpu.CompilerParams(vmem_limit_bytes=16 << 20),
    )(second, hits, factors)
    first_data, partial = lax.optimization_barrier((first_data, partial))
    row_locals = lax.all_to_all(partial.reshape(rows, slots, 128), "row", 0, 0, tiled=True)

    near_first, to_second = near_sums(first_data, second, ids_lane)
    near_first = lax.ppermute(near_first, BOTH, home)
    returned = lax.all_to_all(
        jnp.concatenate([to_second, row_locals.sum(axis=0)], axis=1), "col", 0, 0, tiled=True
    )
    return end(back_ids, returned, near_first, basis, transfer)


def solution(mesh):
    placed = (
        P(BOTH, None, None),
        P(BOTH, None, None),
        P(BOTH, None, None),
        P(BOTH, None, None),
        P(),
        P(None, BOTH),
        P(BOTH),
        P(None, BOTH),
        P(BOTH, None, None),
    )
    return jax.shard_map(
        shards, mesh=mesh, in_specs=placed, out_specs=P(BOTH, None, None), check_vma=False
    )
```

```python
import functools
import math

import jax
import jax.numpy as jnp
from jax import lax
from jax.experimental import pallas as pl
from jax.experimental.pallas import tpu as pltpu
from jax.sharding import PartitionSpec as P

REG_EPS = 0.02
EPS_SQ = REG_EPS * REG_EPS
STOKES_SCALE = 1.0 / (8.0 * math.pi)
BOTH = ("row", "col")
GROUP = 16
BATCH = 8
PANELS = 256
FIELD_ROWS = 32
POINT_ROWS = 16
f32, bf16 = jnp.float32, jnp.bfloat16


def pieces(value, count):
    out = []
    for _ in range(count):
        head = value.astype(bf16).astype(f32)
        out.append(head)
        value = value - head
    return out


def put(ref, row, value):
    for half in range(2):
        ref[half, row * GROUP : (row + 1) * GROUP, :] = value[:, half * 128 : (half + 1) * 128]


def get(ref, row):
    return jnp.concatenate([ref[half, row * GROUP : (row + 1) * GROUP, :] for half in range(2)], 1)


def split_parts(block):
    parts = [block[:, k * PANELS : (k + 1) * PANELS] for k in range(6)]
    return parts[:3], parts[3:]


def prepare_source(block, field, left):
    q, y = split_parts(block)
    one, zero = jnp.ones_like(q[0]), jnp.zeros_like(q[0])
    square = y[0] * y[0] + y[1] * y[1] + y[2] * y[2]
    along = y[0] * q[0] + y[1] * q[1] + y[2] * q[2]
    rows = list(q)
    for i in range(3):
        for j in range(3):
            rows += pieces(y[i] * q[j], 2)
    for i in range(3):
        rows += pieces(square * q[i] + y[i] * along, 3)
    rows += [zero] * (FIELD_ROWS - len(rows))
    for k, value in enumerate(rows):
        put(field, k, value)
    if left is None:
        return
    for k, value in enumerate([-2 * v for v in y] + pieces(square + EPS_SQ / 2, 3) + [one] * 3 + [zero] * 7):
        put(left, k, value)


def prepare_target(block, right):
    _, x = split_parts(block)
    one, zero = jnp.ones_like(x[0]), jnp.zeros_like(x[0])
    norm = pieces(x[0] * x[0] + x[1] * x[1] + x[2] * x[2] + EPS_SQ / 2, 3)
    for k, value in enumerate(x + [one] * 3 + norm + [zero] * 7):
        put(right, k, value)


def finish(block, sums):
    _, x = split_parts(block)
    mom = [get(sums, i) for i in range(3)]
    cross = [[get(sums, 3 + 2 * (3 * i + j)) + get(sums, 4 + 2 * (3 * i + j)) for j in range(3)] for i in range(3)]
    dot = x[0] * mom[0] + x[1] * mom[1] + x[2] * mom[2] - (cross[0][0] + cross[1][1] + cross[2][2])
    square = x[0] * x[0] + x[1] * x[1] + x[2] * x[2] + 2 * EPS_SQ
    out = []
    for i in range(3):
        mixed = sum(x[j] * (cross[i][j] + 2 * cross[j][i]) for j in range(3))
        tail = get(sums, 21 + 3 * i) + get(sums, 22 + 3 * i) + get(sums, 23 + 3 * i)
        out.append(((square * mom[i] + x[i] * dot - mixed) + tail) * STOKES_SCALE)
    return out


def near_kernel(ids_lane, first_ref, second_ref, near_first, to_second, field_a, left, field_b, right, sums_a, sums_b):
    own = first_ref.shape[0]
    near_first[...] = jnp.zeros_like(near_first)

    def group(g, carry):
        rows = pl.ds(pl.multiple_of(g * GROUP, GROUP), GROUP)
        ids = second_ref[rows, ids_lane : ids_lane + 128].astype(f32)[:, :own]
        chosen = (ids == lax.broadcasted_iota(jnp.int32, (GROUP, own), 1).astype(f32)).astype(bf16)
        first = jnp.dot(chosen, first_ref[...], preferred_element_type=f32)
        second = second_ref[rows, : 6 * PANELS].astype(f32)
        prepare_source(first, field_a, left)
        prepare_source(second, field_b, None)
        prepare_target(second, right)

        def load(ref, count, s):
            parts = [ref[half, pl.ds(s, count, stride=GROUP), :] for half in range(2)]
            return jnp.concatenate(parts, 1).astype(bf16)

        def apply(field, cube, dim, sums, s):
            total = lax.dot_general(
                load(field, FIELD_ROWS, s), cube, (((1,), (dim,)), ((), ())), preferred_element_type=f32
            )
            for half in range(2):
                sums[half, pl.ds(s, FIELD_ROWS, stride=GROUP), :] = total[:, half * 128 : (half + 1) * 128]

        for start in range(0, GROUP, BATCH):
            batch = range(start, start + BATCH)
            shifted = [
                lax.dot_general(
                    load(left, POINT_ROWS, s),
                    load(right, POINT_ROWS, s),
                    (((0,), (0,)), ((), ())),
                    preferred_element_type=f32,
                )
                for s in batch
            ]
            cubes = []
            for value in shifted:
                inv = lax.rsqrt(value)
                cubes.append((inv * inv * inv).astype(bf16))
            for s, cube in zip(batch, cubes):
                apply(field_a, cube, 0, sums_b, s)
            for s, cube in zip(batch, cubes):
                apply(field_b, cube, 1, sums_a, s)

        for i, value in enumerate(finish(second, sums_b)):
            to_second[rows, i * PANELS : (i + 1) * PANELS] = value
        for i, value in enumerate(finish(first, sums_a)):
            for piece in pieces(value, 3):
                near_first[:, i * PANELS : (i + 1) * PANELS] += lax.dot_general(
                    chosen, piece.astype(bf16), (((0,), (0,)), ((), ())), preferred_element_type=f32
                )
        return carry

    lax.fori_loop(0, second_ref.shape[0] // GROUP, group, 0)


def near_sums(first, second, ids_lane):
    slots = second.shape[0]
    vmem = pl.BlockSpec(memory_space=pltpu.VMEM)

    def rows(count):
        return pltpu.VMEM((2, count * GROUP, 128), f32)

    return pl.pallas_call(
        functools.partial(near_kernel, ids_lane),
        out_shape=[
            jax.ShapeDtypeStruct((first.shape[0], 3 * PANELS), f32),
            jax.ShapeDtypeStruct((slots, 3 * PANELS), f32),
        ],
        in_specs=[vmem] * 2,
        out_specs=[vmem] * 2,
        scratch_shapes=[rows(FIELD_ROWS), rows(POINT_ROWS)] * 2 + [rows(FIELD_ROWS)] * 2,
        compiler_params=pltpu.CompilerParams(vmem_limit_bytes=32 << 20),
        cost_estimate=pl.CostEstimate(
            flops=slots * 2 * 2 * 64 * PANELS * PANELS, bytes_accessed=slots * 9216, transcendentals=0
        ),
    )(first, second)


def hits_kernel(parents, ends, hits):
    count = ends.shape[1]
    for m in range(parents.shape[1]):
        hits[:, m * count : (m + 1) * count] = (parents[:, m : m + 1] == ends[...]).astype(f32).astype(bf16)


def far_kernel(start, recv, hits, factors, out):
    count = factors.shape[2]
    parts = hits.shape[1] // count
    rank = 128 // parts
    slots = recv.shape[0]
    found = jnp.zeros((128, parts * count), f32)
    for r in range(hits.shape[0] // slots):
        found += lax.dot_general(
            recv[:, start + 128 * r : start + 128 * (r + 1)],
            hits[r * slots : (r + 1) * slots, :],
            (((0,), (0,)), ((), ())),
            preferred_element_type=f32,
        )
    at_ends = sum(found[m * rank : (m + 1) * rank, m * count : (m + 1) * count] for m in range(parts))
    sent = jnp.sum(factors[...] * at_ends[None], axis=1)
    sent = jnp.concatenate([sent[:, count // 2 :], sent[:, : count // 2]], axis=1)
    zero = jnp.zeros_like(sent)
    table = [
        jnp.concatenate([piece if m == k else zero for k in range(parts)], axis=1)
        for piece in pieces(sent, 2)
        for m in range(parts)
    ]
    both = lax.dot_general(
        hits[...],
        jnp.concatenate(table, axis=0).astype(bf16),
        (((1,), (1,)), ((), ())),
        preferred_element_type=f32,
    )
    out[...] = both[:, :128] + both[:, 128:]


def own_lanes(own, rank):
    shape = (own, own * rank)
    return lax.broadcasted_iota(jnp.int32, shape, 1) // rank == lax.broadcasted_iota(jnp.int32, shape, 0)


def join_kernel(density, coords, data):
    panels = density.shape[2]
    for k in range(3):
        data[:, k * panels : (k + 1) * panels] = density[k]
        data[:, (3 + k) * panels : (4 + k) * panels] = coords[k]


def join(density, coords):
    own, parts, panels = density.shape
    vmem = pl.BlockSpec(memory_space=pltpu.VMEM)
    return pl.pallas_call(
        join_kernel,
        out_shape=jax.ShapeDtypeStruct((own, 2 * parts * panels), density.dtype),
        in_specs=[vmem] * 2,
        out_specs=vmem,
        compiler_params=pltpu.CompilerParams(vmem_limit_bytes=8 << 20),
    )(density.transpose(1, 0, 2), coords.transpose(1, 0, 2))


def start_kernel(count, pairs, density_hbm, basis_hbm, transfer_hbm, message, density, basis, transfer, sems):
    own, rank = density.shape[1], transfer.shape[1]
    step = 256
    chunks = [pl.ds(k, step) for k in range(0, own * rank, step)]
    sources = [density_hbm] + [basis_hbm.at[c] for c in chunks] + [transfer_hbm]
    targets = [density] + [basis.at[c] for c in chunks] + [transfer]
    copies = [pltpu.make_async_copy(a, b, sems.at[k]) for k, (a, b) in enumerate(zip(sources, targets))]
    for copy in copies:
        copy.start()
    mine = own_lanes(own, rank)
    across = (((1,), (1,)), ((), ()))
    ids = lax.rem(pairs[...], own)
    live = lax.broadcasted_iota(jnp.int32, ids.shape, 1) < count[0]
    ids = jnp.where(live, ids, -1).astype(f32)
    copies[0].wait()
    flat = jnp.concatenate([density[i] for i in range(3)], axis=1)
    folded = jnp.zeros((own, 128), f32)
    for k, chunk in enumerate(chunks):
        copies[1 + k].wait()
        every = lax.dot_general(flat, basis[chunk, :], across, preferred_element_type=f32)
        every = jnp.where(mine[:, k * step : (k + 1) * step], every, 0.0)
        folded += sum(every[:, m : m + 128] for m in range(0, step, 128))
    moments = sum(folded[:, k : k + rank] for k in range(0, 128, rank))
    copies[-1].wait()
    wide = jnp.concatenate(pieces(moments, 3), axis=0).astype(bf16)
    lifted = sum(
        lax.dot_general(wide, piece.astype(bf16), across, preferred_element_type=f32)
        for piece in pieces(transfer[...], 2)
    )
    lifted = lifted[:own] + lifted[own : 2 * own] + lifted[2 * own :]
    lifted = jnp.sum(jnp.where(mine, lifted, 0.0), axis=0, keepdims=True)
    lifted = jnp.concatenate([lifted[:, k : k + 128] for k in range(0, own * rank, 128)], axis=0)
    rows = message.shape[0]
    block = ids.shape[1] // rows
    for k in range(rows):
        turned = jnp.concatenate([ids[:, k * block :], ids[:, : k * block]], axis=1) if k else ids
        message[k] = jnp.concatenate([lifted, turned], axis=0)


def start(near_count, near_pairs, density, basis, transfer, rows):
    own, rank, width = basis.shape
    vmem, hbm = pl.BlockSpec(memory_space=pltpu.VMEM), pl.BlockSpec(memory_space=pltpu.HBM)
    return pl.pallas_call(
        start_kernel,
        out_shape=jax.ShapeDtypeStruct((rows, own * rank // 128 + 2, near_pairs.shape[1]), f32),
        in_specs=[pl.BlockSpec(memory_space=pltpu.SMEM), vmem] + [hbm] * 3,
        out_specs=vmem,
        scratch_shapes=[
            pltpu.VMEM((3, own, width // 3), density.dtype),
            pltpu.VMEM((own * rank, width), basis.dtype),
            pltpu.VMEM((own * rank, rank), f32),
            pltpu.SemaphoreType.DMA((own * rank // 256 + 2,)),
        ],
        compiler_params=pltpu.CompilerParams(vmem_limit_bytes=60 << 20),
    )(
        near_count,
        near_pairs,
        density.transpose(1, 0, 2),
        basis.reshape(own * rank, width),
        transfer.reshape(own * rank, rank),
    )


def pick_kernel(orders, place, from_row, data, message_hbm, back, message, sems):
    rows, lift_rows = from_row.shape[0], from_row.shape[1] - 2
    own, wide = data.shape
    slots = message.shape[0]
    seats = len(orders[0])
    per_pair = slots // seats
    half = seats // rows

    def send(begin, stop):
        lanes = pl.ds(begin, stop - begin)
        copy = pltpu.make_async_copy(message.at[:, lanes], message_hbm.at[:, lanes], sems.at[min(begin, 1)])
        copy.start()
        return copy

    for r in range(rows):
        lifted = from_row[r, :lift_rows, :]
        lanes = slice(wide + 128 * (r + 1), wide + 128 * (r + 2))
        message[:, lanes] = jnp.concatenate([lifted] * (slots // lift_rows), axis=0).astype(bf16)
    copies = [send(wide + 128, message.shape[1])]
    lane = lax.broadcasted_iota(jnp.int32, (1, 128), 1)
    triples = []
    for r in range(rows):
        first, second = from_row[r, lift_rows : lift_rows + 1, :], from_row[r, lift_rows + 1 :, :]
        same = (place[0] == r) & (half * place[0] + lane // per_pair == place[1]) & (first == second)
        triples.append(jnp.concatenate([first, second, jnp.where(same, -1.0, second)], axis=0))
    even, odd = (
        jnp.concatenate([triples[r][:, h * per_pair : (h + 1) * per_pair] for r, h in order], axis=1)
        for order in orders
    )
    ids = jnp.where(place[0] % 2 == 0, even, odd)
    back[...] = ids[2:]
    down = (((0,), (0,)), ((), ()))
    cluster = lax.broadcasted_iota(jnp.int32, (own, slots), 0).astype(f32)
    first, second = ((ids[k : k + 1] == cluster).astype(f32).astype(bf16) for k in range(2))
    message[:, :wide] = lax.dot_general(second, data[...], down, preferred_element_type=f32).astype(bf16)
    names = (lax.broadcasted_iota(jnp.int32, (own, 128), 0) + 1).astype(f32).astype(bf16)
    names = lax.dot_general(first, names, down, preferred_element_type=f32) - 1.0
    message[:, wide : wide + 128] = names.astype(bf16)
    copies.append(send(0, wide + 128))
    for copy in copies:
        copy.wait()


def pick(place, from_row, data, slots, orders):
    vmem = pl.BlockSpec(memory_space=pltpu.VMEM)
    wide = data.shape[1] + 128 * (1 + from_row.shape[0])
    return pl.pallas_call(
        functools.partial(pick_kernel, orders),
        out_shape=[jax.ShapeDtypeStruct((slots, wide), bf16), jax.ShapeDtypeStruct((1, slots), f32)],
        in_specs=[pl.BlockSpec(memory_space=pltpu.SMEM)] + [vmem] * 2,
        out_specs=[pl.BlockSpec(memory_space=pltpu.HBM), vmem],
        scratch_shapes=[pltpu.VMEM((slots, wide), bf16), pltpu.SemaphoreType.DMA((2,))],
        compiler_params=pltpu.CompilerParams(vmem_limit_bytes=8 << 20),
    )(place, from_row, data)


def end_kernel(back, returned, near_first, basis, transfer, out, velocity, sems):
    own, panels = velocity.shape[1:]
    rank = transfer.shape[1]
    mine = own_lanes(own, rank)
    lift_rows = own * rank // 128
    local = sum(returned[k : k + lift_rows, 3 * panels :] for k in range(0, returned.shape[0], lift_rows))
    local = jnp.concatenate([local[k : k + 1] for k in range(lift_rows)], axis=1)
    wide = jnp.concatenate(pieces(jnp.where(mine, local, 0.0), 3), axis=0).astype(bf16)
    coef = sum(
        jnp.dot(wide, piece.astype(bf16), preferred_element_type=f32) for piece in pieces(transfer[...], 3)
    )
    coef = coef[:own] + coef[own : 2 * own] + coef[2 * own :]
    coef = pieces(jnp.where(mine, jnp.concatenate([coef] * own, axis=1), 0.0), 3)
    coef = jnp.concatenate(coef, axis=0).astype(bf16)
    slot = lax.broadcasted_iota(jnp.int32, (own, back.shape[1]), 0).astype(f32)
    chosen = (back[...] == slot).astype(f32).astype(bf16)
    copies = []
    for i in range(3):
        lanes = slice(i * panels, (i + 1) * panels)
        far = jnp.dot(coef, basis[:, lanes], preferred_element_type=f32)
        total = far[:own] + far[own : 2 * own] + far[2 * own :]
        for piece in pieces(returned[:, lanes], 3):
            total += jnp.dot(chosen, piece.astype(bf16), preferred_element_type=f32)
        velocity[i] = near_first[:, lanes] + total
        copies.append(pltpu.make_async_copy(velocity.at[i], out.at[i], sems.at[i]))
        copies[-1].start()
    for copy in copies:
        copy.wait()


def end(back, returned, near_first, basis, transfer):
    own, rank, width = basis.shape
    shape = (3, own, width // 3)
    return pl.pallas_call(
        end_kernel,
        out_shape=jax.ShapeDtypeStruct(shape, f32),
        in_specs=[pl.BlockSpec(memory_space=pltpu.VMEM)] * 5,
        out_specs=pl.BlockSpec(memory_space=pltpu.HBM),
        scratch_shapes=[pltpu.VMEM(shape, f32), pltpu.SemaphoreType.DMA((3,))],
        compiler_params=pltpu.CompilerParams(vmem_limit_bytes=8 << 20),
    )(
        back,
        returned,
        near_first,
        basis.reshape(own * rank, width),
        transfer.reshape(own * rank, rank),
    ).transpose(1, 0, 2)


def seat(p, r, h, rows):
    hops = rows // 2
    near = (2 * (p % 2) + h, 2 * (p % 2) + (3 * h - 1))[r % 2] % hops
    return (r // 2 + hops // 2) % hops * hops + near


def shards(density, coords, basis, transfer, parent, near_pairs, near_count, far_pairs, coupling):
    own, _, panels = density.shape
    rank = basis.shape[1]
    rows, cols = lax.axis_size("row"), lax.axis_size("col")
    half = cols // rows
    slots = near_pairs.shape[1]
    vmem = pl.BlockSpec(memory_space=pltpu.VMEM)

    swap = [
        (r * cols + half * p + h, p * cols + seat(p, r, h, rows))
        for r in range(rows)
        for p in range(rows)
        for h in range(half)
    ]
    home = [(there, here) for here, there in swap]
    message = start(near_count, near_pairs, density, basis, transfer, rows)
    density, coords, message = lax.optimization_barrier((density, coords, message))
    from_row = lax.all_to_all(message, "row", 0, 0, tiled=True)
    data = join(density, coords)
    first_data = lax.ppermute(data, BOTH, swap)
    first_data, from_row = lax.optimization_barrier((first_data, from_row))

    place = jnp.stack([lax.axis_index("row"), lax.axis_index("col")])
    orders = [sorted((seat(p, r, h, rows), r, h) for r in range(rows) for h in range(half)) for p in range(2)]
    orders = [[(r, h) for _, r, h in order] for order in orders]
    message, back_ids = pick(place, from_row, data, slots, orders)
    second = lax.all_to_all(message, "col", 0, 0, tiled=True)
    ids_lane = 6 * panels

    factors = jnp.concatenate([coupling.transpose(1, 2, 0), coupling.transpose(2, 1, 0)], axis=2)
    parents, from_row = lax.optimization_barrier((parent.reshape(-1, 128 // rank), from_row))
    hits = pl.pallas_call(
        hits_kernel,
        out_shape=jax.ShapeDtypeStruct((rows * slots, far_pairs.size * (128 // rank)), bf16),
        in_specs=[vmem] * 2,
        out_specs=vmem,
        compiler_params=pltpu.CompilerParams(vmem_limit_bytes=16 << 20),
    )(parents, far_pairs[::-1].reshape(1, -1))
    partial = pl.pallas_call(
        functools.partial(far_kernel, ids_lane + 128),
        out_shape=jax.ShapeDtypeStruct((rows * slots, 128), f32),
        in_specs=[vmem] * 3,
        out_specs=vmem,
        compiler_params=pltpu.CompilerParams(vmem_limit_bytes=16 << 20),
    )(second, hits, factors)
    first_data, partial = lax.optimization_barrier((first_data, partial))
    row_locals = lax.all_to_all(partial.reshape(rows, slots, 128), "row", 0, 0, tiled=True)

    near_first, to_second = near_sums(first_data, second, ids_lane)
    near_first = lax.ppermute(near_first, BOTH, home)
    returned = lax.all_to_all(
        jnp.concatenate([to_second, row_locals.sum(axis=0)], axis=1), "col", 0, 0, tiled=True
    )
    return end(back_ids, returned, near_first, basis, transfer)


def solution(mesh):
    placed = (
        P(BOTH, None, None),
        P(BOTH, None, None),
        P(BOTH, None, None),
        P(BOTH, None, None),
        P(),
        P(None, BOTH),
        P(BOTH),
        P(None, BOTH),
        P(BOTH, None, None),
    )
    return jax.shard_map(
        shards, mesh=mesh, in_specs=placed, out_specs=P(BOTH, None, None), check_vma=False
    )
```

```python
import functools
import math

import jax
import jax.numpy as jnp
from jax import lax
from jax.experimental import pallas as pl
from jax.experimental.pallas import tpu as pltpu
from jax.sharding import PartitionSpec as P

REG_EPS = 0.02
EPS_SQ = REG_EPS * REG_EPS
STOKES_SCALE = 1.0 / (8.0 * math.pi)
BOTH = ("row", "col")
GROUP = 16
BATCH = 8
PANELS = 256
FIELD_ROWS = 32
POINT_ROWS = 16
f32, bf16 = jnp.float32, jnp.bfloat16


def pieces(value, count):
    out = []
    for _ in range(count):
        head = value.astype(bf16).astype(f32)
        out.append(head)
        value = value - head
    return out


def put(ref, row, value):
    for half in range(2):
        ref[half, row * GROUP : (row + 1) * GROUP, :] = value[:, half * 128 : (half + 1) * 128]


def get(ref, row):
    return jnp.concatenate([ref[half, row * GROUP : (row + 1) * GROUP, :] for half in range(2)], 1)


def split_parts(block):
    parts = [block[:, k * PANELS : (k + 1) * PANELS] for k in range(6)]
    return parts[:3], parts[3:]


def prepare_source(block, field, left):
    q, y = split_parts(block)
    one, zero = jnp.ones_like(q[0]), jnp.zeros_like(q[0])
    square = y[0] * y[0] + y[1] * y[1] + y[2] * y[2]
    along = y[0] * q[0] + y[1] * q[1] + y[2] * q[2]
    rows = list(q)
    for i in range(3):
        for j in range(3):
            rows += pieces(y[i] * q[j], 2)
    for i in range(3):
        rows += pieces(square * q[i] + y[i] * along, 3)
    rows += [zero] * (FIELD_ROWS - len(rows))
    for k, value in enumerate(rows):
        put(field, k, value)
    if left is None:
        return
    for k, value in enumerate([-2 * v for v in y] + pieces(square + EPS_SQ / 2, 3) + [one] * 3 + [zero] * 7):
        put(left, k, value)


def prepare_target(block, right):
    _, x = split_parts(block)
    one, zero = jnp.ones_like(x[0]), jnp.zeros_like(x[0])
    norm = pieces(x[0] * x[0] + x[1] * x[1] + x[2] * x[2] + EPS_SQ / 2, 3)
    for k, value in enumerate(x + [one] * 3 + norm + [zero] * 7):
        put(right, k, value)


def finish(block, sums):
    _, x = split_parts(block)
    mom = [get(sums, i) for i in range(3)]
    cross = [[get(sums, 3 + 2 * (3 * i + j)) + get(sums, 4 + 2 * (3 * i + j)) for j in range(3)] for i in range(3)]
    dot = x[0] * mom[0] + x[1] * mom[1] + x[2] * mom[2] - (cross[0][0] + cross[1][1] + cross[2][2])
    square = x[0] * x[0] + x[1] * x[1] + x[2] * x[2] + 2 * EPS_SQ
    out = []
    for i in range(3):
        mixed = sum(x[j] * (cross[i][j] + 2 * cross[j][i]) for j in range(3))
        tail = get(sums, 21 + 3 * i) + get(sums, 22 + 3 * i) + get(sums, 23 + 3 * i)
        out.append(((square * mom[i] + x[i] * dot - mixed) + tail) * STOKES_SCALE)
    return out


def near_kernel(
    ids_lane, first_ref, second_ref, near_first, out_hbm, to_second, field_a, left, field_b, right, sums_a, sums_b, sem
):
    own = first_ref.shape[0]
    near_first[...] = jnp.zeros_like(near_first)

    def group(g, carry):
        rows = pl.ds(pl.multiple_of(g * GROUP, GROUP), GROUP)
        ids = second_ref[rows, ids_lane : ids_lane + 128].astype(f32)[:, :own]
        chosen = (ids == lax.broadcasted_iota(jnp.int32, (GROUP, own), 1).astype(f32)).astype(bf16)
        first = jnp.dot(chosen, first_ref[...], preferred_element_type=f32)
        second = second_ref[rows, : 6 * PANELS].astype(f32)
        prepare_source(first, field_a, left)
        prepare_source(second, field_b, None)
        prepare_target(second, right)

        def load(ref, count, s):
            parts = [ref[half, pl.ds(s, count, stride=GROUP), :] for half in range(2)]
            return jnp.concatenate(parts, 1).astype(bf16)

        def apply(field, cube, dim, sums, s):
            total = lax.dot_general(
                load(field, FIELD_ROWS, s), cube, (((1,), (dim,)), ((), ())), preferred_element_type=f32
            )
            for half in range(2):
                sums[half, pl.ds(s, FIELD_ROWS, stride=GROUP), :] = total[:, half * 128 : (half + 1) * 128]

        for start in range(0, GROUP, BATCH):
            batch = range(start, start + BATCH)
            shifted = [
                lax.dot_general(
                    load(left, POINT_ROWS, s),
                    load(right, POINT_ROWS, s),
                    (((0,), (0,)), ((), ())),
                    preferred_element_type=f32,
                )
                for s in batch
            ]
            cubes = []
            for value in shifted:
                inv = lax.rsqrt(value)
                cubes.append((inv * inv * inv).astype(bf16))
            for s, cube in zip(batch, cubes):
                apply(field_a, cube, 0, sums_b, s)
            for s, cube in zip(batch, cubes):
                apply(field_b, cube, 1, sums_a, s)

        for i, value in enumerate(finish(second, sums_b)):
            to_second[rows, i * PANELS : (i + 1) * PANELS] = value
        pltpu.make_async_copy(to_second.at[rows], out_hbm.at[rows, pl.ds(0, 3 * PANELS)], sem).start()
        for i, value in enumerate(finish(first, sums_a)):
            for piece in pieces(value, 3):
                near_first[:, i * PANELS : (i + 1) * PANELS] += lax.dot_general(
                    chosen, piece.astype(bf16), (((0,), (0,)), ((), ())), preferred_element_type=f32
                )
        return carry

    lax.fori_loop(0, second_ref.shape[0] // GROUP, group, 0)
    pltpu.make_async_copy(to_second, out_hbm.at[:, pl.ds(0, 3 * PANELS)], sem).wait()


def near_sums(first, second, ids_lane):
    slots = second.shape[0]
    vmem = pl.BlockSpec(memory_space=pltpu.VMEM)

    def rows(count):
        return pltpu.VMEM((2, count * GROUP, 128), f32)

    return pl.pallas_call(
        functools.partial(near_kernel, ids_lane),
        out_shape=[
            jax.ShapeDtypeStruct((first.shape[0], 3 * PANELS), f32),
            jax.ShapeDtypeStruct((slots, 3 * PANELS + 128), f32),
        ],
        in_specs=[vmem] * 2,
        out_specs=[vmem, pl.BlockSpec(memory_space=pltpu.HBM)],
        scratch_shapes=[pltpu.VMEM((slots, 3 * PANELS), f32)]
        + [rows(FIELD_ROWS), rows(POINT_ROWS)] * 2
        + [rows(FIELD_ROWS)] * 2
        + [pltpu.SemaphoreType.DMA],
        compiler_params=pltpu.CompilerParams(vmem_limit_bytes=32 << 20),
        cost_estimate=pl.CostEstimate(
            flops=slots * 2 * 2 * 64 * PANELS * PANELS, bytes_accessed=slots * 9216, transcendentals=0
        ),
    )(first, second)


def hits_kernel(parents, ends, hits):
    count = ends.shape[1]
    for m in range(parents.shape[1]):
        hits[:, m * count : (m + 1) * count] = (parents[:, m : m + 1] == ends[...]).astype(f32).astype(bf16)


def far_kernel(start, recv, hits, factors, out_hbm, out, sems):
    count = factors.shape[2]
    parts = hits.shape[1] // count
    rank = 128 // parts
    slots = recv.shape[0]
    found = jnp.zeros((128, parts * count), f32)
    for r in range(hits.shape[0] // slots):
        found += lax.dot_general(
            recv[:, start + 128 * r : start + 128 * (r + 1)],
            hits[r * slots : (r + 1) * slots, :],
            (((0,), (0,)), ((), ())),
            preferred_element_type=f32,
        )
    at_ends = sum(found[m * rank : (m + 1) * rank, m * count : (m + 1) * count] for m in range(parts))
    sent = jnp.sum(factors[...] * at_ends[None], axis=1)
    sent = jnp.concatenate([sent[:, count // 2 :], sent[:, : count // 2]], axis=1)
    zero = jnp.zeros_like(sent)
    table = [
        jnp.concatenate([piece if m == k else zero for k in range(parts)], axis=1)
        for piece in pieces(sent, 2)
        for m in range(parts)
    ]
    table = jnp.concatenate(table, axis=0).astype(bf16)
    copies = []
    for k in range(0, out.shape[0], 256):
        rows = pl.ds(k, 256)
        both = lax.dot_general(hits[rows, :], table, (((1,), (1,)), ((), ())), preferred_element_type=f32)
        out[rows, :] = both[:, :128] + both[:, 128:]
        copies.append(pltpu.make_async_copy(out.at[rows], out_hbm.at[rows], sems.at[len(copies)]))
        copies[-1].start()
    for copy in copies:
        copy.wait()


def own_lanes(own, rank):
    shape = (own, own * rank)
    return lax.broadcasted_iota(jnp.int32, shape, 1) // rank == lax.broadcasted_iota(jnp.int32, shape, 0)


def join_kernel(density, coords, data):
    panels = density.shape[2]
    for k in range(3):
        data[:, k * panels : (k + 1) * panels] = density[k]
        data[:, (3 + k) * panels : (4 + k) * panels] = coords[k]


def join(density, coords):
    own, parts, panels = density.shape
    vmem = pl.BlockSpec(memory_space=pltpu.VMEM)
    return pl.pallas_call(
        join_kernel,
        out_shape=jax.ShapeDtypeStruct((own, 2 * parts * panels), density.dtype),
        in_specs=[vmem] * 2,
        out_specs=vmem,
        compiler_params=pltpu.CompilerParams(vmem_limit_bytes=8 << 20),
    )(density.transpose(1, 0, 2), coords.transpose(1, 0, 2))


def start_kernel(
    count_hbm, pairs_hbm, density_hbm, basis_hbm, transfer_hbm, message, count, pairs, density, basis, transfer, sems
):
    own, rank = density.shape[1], transfer.shape[1]
    step = 256
    chunks = [pl.ds(k, step) for k in range(0, own * rank, step)]
    sources = [density_hbm] + [basis_hbm.at[c] for c in chunks] + [transfer_hbm, count_hbm, pairs_hbm]
    targets = [density] + [basis.at[c] for c in chunks] + [transfer, count, pairs]
    copies = [pltpu.make_async_copy(a, b, sems.at[k]) for k, (a, b) in enumerate(zip(sources, targets))]
    for copy in copies:
        copy.start()
    mine = own_lanes(own, rank)
    across = (((1,), (1,)), ((), ()))
    copies[0].wait()
    flat = jnp.concatenate([density[i] for i in range(3)], axis=1)
    folded = jnp.zeros((own, 128), f32)
    for k, chunk in enumerate(chunks):
        copies[1 + k].wait()
        every = lax.dot_general(flat, basis[chunk, :], across, preferred_element_type=f32)
        every = jnp.where(mine[:, k * step : (k + 1) * step], every, 0.0)
        folded += sum(every[:, m : m + 128] for m in range(0, step, 128))
    moments = sum(folded[:, k : k + rank] for k in range(0, 128, rank))
    copies[-3].wait()
    wide = jnp.concatenate(pieces(moments, 3), axis=0).astype(bf16)
    lifted = sum(
        lax.dot_general(wide, piece.astype(bf16), across, preferred_element_type=f32)
        for piece in pieces(transfer[...], 2)
    )
    lifted = lifted[:own] + lifted[own : 2 * own] + lifted[2 * own :]
    lifted = jnp.sum(jnp.where(mine, lifted, 0.0), axis=0, keepdims=True)
    lifted = jnp.concatenate([lifted[:, k : k + 128] for k in range(0, own * rank, 128)], axis=0)
    copies[-2].wait()
    copies[-1].wait()
    ids = lax.rem(pairs[...], own)
    live = lax.broadcasted_iota(jnp.int32, ids.shape, 1) < count[0, 0]
    ids = jnp.where(live, ids, -1).astype(f32)
    rows = message.shape[0]
    block = ids.shape[1] // rows
    for k in range(rows):
        turned = jnp.concatenate([ids[:, k * block :], ids[:, : k * block]], axis=1) if k else ids
        message[k] = jnp.concatenate([lifted, turned], axis=0)


def start(near_count, near_pairs, density, basis, transfer, rows):
    own, rank, width = basis.shape
    vmem, hbm = pl.BlockSpec(memory_space=pltpu.VMEM), pl.BlockSpec(memory_space=pltpu.HBM)
    return pl.pallas_call(
        start_kernel,
        out_shape=jax.ShapeDtypeStruct((rows, own * rank // 128 + 2, near_pairs.shape[1]), f32),
        in_specs=[hbm] * 5,
        out_specs=vmem,
        scratch_shapes=[
            pltpu.SMEM((1, 1), jnp.int32),
            pltpu.VMEM(near_pairs.shape, jnp.int32),
            pltpu.VMEM((3, own, width // 3), density.dtype),
            pltpu.VMEM((own * rank, width), basis.dtype),
            pltpu.VMEM((own * rank, rank), f32),
            pltpu.SemaphoreType.DMA((own * rank // 256 + 4,)),
        ],
        compiler_params=pltpu.CompilerParams(vmem_limit_bytes=60 << 20),
    )(
        near_count.reshape(1, 1),
        near_pairs,
        density.transpose(1, 0, 2),
        basis.reshape(own * rank, width),
        transfer.reshape(own * rank, rank),
    )


def pick_kernel(orders, place, from_row, data, message_hbm, back, message, sems):
    rows, lift_rows = from_row.shape[0], from_row.shape[1] - 2
    own, wide = data.shape
    slots = message.shape[0]
    seats = len(orders[0])
    per_pair = slots // seats
    half = seats // rows

    def send(begin, stop):
        lanes = pl.ds(begin, stop - begin)
        copy = pltpu.make_async_copy(message.at[:, lanes], message_hbm.at[:, lanes], sems.at[min(begin, 1)])
        copy.start()
        return copy

    for r in range(rows):
        lifted = from_row[r, :lift_rows, :]
        lanes = slice(wide + 128 * (r + 1), wide + 128 * (r + 2))
        message[:, lanes] = jnp.concatenate([lifted] * (slots // lift_rows), axis=0).astype(bf16)
    copies = [send(wide + 128, message.shape[1])]
    lane = lax.broadcasted_iota(jnp.int32, (1, 128), 1)
    triples = []
    for r in range(rows):
        first, second = from_row[r, lift_rows : lift_rows + 1, :], from_row[r, lift_rows + 1 :, :]
        same = (place[0] == r) & (half * place[0] + lane // per_pair == place[1]) & (first == second)
        triples.append(jnp.concatenate([first, second, jnp.where(same, -1.0, second)], axis=0))
    even, odd = (
        jnp.concatenate([triples[r][:, h * per_pair : (h + 1) * per_pair] for r, h in order], axis=1)
        for order in orders
    )
    ids = jnp.where(place[0] % 2 == 0, even, odd)
    back[...] = ids[2:]
    down = (((0,), (0,)), ((), ()))
    cluster = lax.broadcasted_iota(jnp.int32, (own, slots), 0).astype(f32)
    first, second = ((ids[k : k + 1] == cluster).astype(f32).astype(bf16) for k in range(2))
    message[:, :wide] = lax.dot_general(second, data[...], down, preferred_element_type=f32).astype(bf16)
    names = (lax.broadcasted_iota(jnp.int32, (own, 128), 0) + 1).astype(f32).astype(bf16)
    names = lax.dot_general(first, names, down, preferred_element_type=f32) - 1.0
    message[:, wide : wide + 128] = names.astype(bf16)
    copies.append(send(0, wide + 128))
    for copy in copies:
        copy.wait()


def pick(place, from_row, data, slots, orders):
    vmem = pl.BlockSpec(memory_space=pltpu.VMEM)
    wide = data.shape[1] + 128 * (1 + from_row.shape[0])
    return pl.pallas_call(
        functools.partial(pick_kernel, orders),
        out_shape=[jax.ShapeDtypeStruct((slots, wide), bf16), jax.ShapeDtypeStruct((1, slots), f32)],
        in_specs=[pl.BlockSpec(memory_space=pltpu.SMEM)] + [vmem] * 2,
        out_specs=[pl.BlockSpec(memory_space=pltpu.HBM), vmem],
        scratch_shapes=[pltpu.VMEM((slots, wide), bf16), pltpu.SemaphoreType.DMA((2,))],
        compiler_params=pltpu.CompilerParams(vmem_limit_bytes=8 << 20),
    )(place, from_row, data)


def end_kernel(back, returned, near_first, basis, transfer, out, velocity, sems):
    own, panels = velocity.shape[1:]
    rank = transfer.shape[1]
    mine = own_lanes(own, rank)
    lift_rows = own * rank // 128
    local = sum(returned[k : k + lift_rows, 3 * panels :] for k in range(0, returned.shape[0], lift_rows))
    local = jnp.concatenate([local[k : k + 1] for k in range(lift_rows)], axis=1)
    wide = jnp.concatenate(pieces(jnp.where(mine, local, 0.0), 3), axis=0).astype(bf16)
    coef = sum(
        jnp.dot(wide, piece.astype(bf16), preferred_element_type=f32) for piece in pieces(transfer[...], 3)
    )
    coef = coef[:own] + coef[own : 2 * own] + coef[2 * own :]
    coef = pieces(jnp.where(mine, jnp.concatenate([coef] * own, axis=1), 0.0), 3)
    coef = jnp.concatenate(coef, axis=0).astype(bf16)
    slot = lax.broadcasted_iota(jnp.int32, (own, back.shape[1]), 0).astype(f32)
    chosen = (back[...] == slot).astype(f32).astype(bf16)
    copies = []
    for i in range(3):
        lanes = slice(i * panels, (i + 1) * panels)
        far = jnp.dot(coef, basis[:, lanes], preferred_element_type=f32)
        total = far[:own] + far[own : 2 * own] + far[2 * own :]
        for piece in pieces(returned[:, lanes], 3):
            total += jnp.dot(chosen, piece.astype(bf16), preferred_element_type=f32)
        velocity[i] = near_first[:, lanes] + total
        copies.append(pltpu.make_async_copy(velocity.at[i], out.at[i], sems.at[i]))
        copies[-1].start()
    for copy in copies:
        copy.wait()


def end(back, returned, near_first, basis, transfer):
    own, rank, width = basis.shape
    shape = (3, own, width // 3)
    return pl.pallas_call(
        end_kernel,
        out_shape=jax.ShapeDtypeStruct(shape, f32),
        in_specs=[pl.BlockSpec(memory_space=pltpu.VMEM)] * 5,
        out_specs=pl.BlockSpec(memory_space=pltpu.HBM),
        scratch_shapes=[pltpu.VMEM(shape, f32), pltpu.SemaphoreType.DMA((3,))],
        compiler_params=pltpu.CompilerParams(vmem_limit_bytes=8 << 20),
    )(
        back,
        returned,
        near_first,
        basis.reshape(own * rank, width),
        transfer.reshape(own * rank, rank),
    ).transpose(1, 0, 2)


def seat(p, r, h, rows):
    hops = rows // 2
    near = (2 * (p % 2) + h, 2 * (p % 2) + (3 * h - 1))[r % 2] % hops
    return (r // 2 + hops // 2) % hops * hops + near


def shards(density, coords, basis, transfer, parent, near_pairs, near_count, far_pairs, coupling):
    own, _, panels = density.shape
    rank = basis.shape[1]
    rows, cols = lax.axis_size("row"), lax.axis_size("col")
    half = cols // rows
    slots = near_pairs.shape[1]
    vmem = pl.BlockSpec(memory_space=pltpu.VMEM)

    swap = [
        (r * cols + half * p + h, p * cols + seat(p, r, h, rows))
        for r in range(rows)
        for p in range(rows)
        for h in range(half)
    ]
    home = [(there, here) for here, there in swap]
    message = start(near_count, near_pairs, density, basis, transfer, rows)
    density, coords, message = lax.optimization_barrier((density, coords, message))
    from_row = lax.all_to_all(message, "row", 0, 0, tiled=True)
    data = join(density, coords)
    first_data = lax.ppermute(data, BOTH, swap)
    first_data, from_row = lax.optimization_barrier((first_data, from_row))

    place = jnp.stack([lax.axis_index("row"), lax.axis_index("col")])
    orders = [sorted((seat(p, r, h, rows), r, h) for r in range(rows) for h in range(half)) for p in range(2)]
    orders = [[(r, h) for _, r, h in order] for order in orders]
    message, back_ids = pick(place, from_row, data, slots, orders)
    second = lax.all_to_all(message, "col", 0, 0, tiled=True)
    ids_lane = 6 * panels

    factors = jnp.concatenate([coupling.transpose(1, 2, 0), coupling.transpose(2, 1, 0)], axis=2)
    parents, from_row = lax.optimization_barrier((parent.reshape(-1, 128 // rank), from_row))
    hits = pl.pallas_call(
        hits_kernel,
        out_shape=jax.ShapeDtypeStruct((rows * slots, far_pairs.size * (128 // rank)), bf16),
        in_specs=[vmem] * 2,
        out_specs=vmem,
        compiler_params=pltpu.CompilerParams(vmem_limit_bytes=16 << 20),
    )(parents, far_pairs[::-1].reshape(1, -1))
    partial = pl.pallas_call(
        functools.partial(far_kernel, ids_lane + 128),
        out_shape=jax.ShapeDtypeStruct((rows * slots, 128), f32),
        in_specs=[vmem] * 3,
        out_specs=pl.BlockSpec(memory_space=pltpu.HBM),
        scratch_shapes=[pltpu.VMEM((rows * slots, 128), f32), pltpu.SemaphoreType.DMA((rows * slots // 256,))],
        compiler_params=pltpu.CompilerParams(vmem_limit_bytes=16 << 20),
    )(second, hits, factors)
    first_data, partial = lax.optimization_barrier((first_data, partial))
    row_locals = lax.all_to_all(partial.reshape(rows, slots, 128), "row", 0, 0, tiled=True)

    near_first, to_second = near_sums(first_data, second, ids_lane)
    near_first = lax.ppermute(near_first, BOTH, home)
    message = lax.dynamic_update_slice(to_second, row_locals.sum(axis=0), (0, 3 * panels))
    returned = lax.all_to_all(message, "col", 0, 0, tiled=True)
    return end(back_ids, returned, near_first, basis, transfer)


def solution(mesh):
    placed = (
        P(BOTH, None, None),
        P(BOTH, None, None),
        P(BOTH, None, None),
        P(BOTH, None, None),
        P(),
        P(None, BOTH),
        P(BOTH),
        P(None, BOTH),
        P(BOTH, None, None),
    )
    return jax.shard_map(
        shards, mesh=mesh, in_specs=placed, out_specs=P(BOTH, None, None), check_vma=False
    )
```

```python
import functools
import math

import jax
import jax.numpy as jnp
from jax import lax
from jax.experimental import pallas as pl
from jax.experimental.pallas import tpu as pltpu
from jax.sharding import PartitionSpec as P

REG_EPS = 0.02
EPS_SQ = REG_EPS * REG_EPS
STOKES_SCALE = 1.0 / (8.0 * math.pi)
BOTH = ("row", "col")
GROUP = 16
BATCH = 8
PANELS = 256
FIELD_ROWS = 32
POINT_ROWS = 16
f32, bf16 = jnp.float32, jnp.bfloat16


def pieces(value, count):
    out = []
    for _ in range(count):
        head = value.astype(bf16).astype(f32)
        out.append(head)
        value = value - head
    return out


def put(ref, row, value):
    for half in range(2):
        ref[half, row * GROUP : (row + 1) * GROUP, :] = value[:, half * 128 : (half + 1) * 128]


def get(ref, row):
    return jnp.concatenate([ref[half, row * GROUP : (row + 1) * GROUP, :] for half in range(2)], 1)


def split_parts(block):
    parts = [block[:, k * PANELS : (k + 1) * PANELS] for k in range(6)]
    return parts[:3], parts[3:]


def prepare_source(block, field, left):
    q, y = split_parts(block)
    one, zero = jnp.ones_like(q[0]), jnp.zeros_like(q[0])
    square = y[0] * y[0] + y[1] * y[1] + y[2] * y[2]
    along = y[0] * q[0] + y[1] * q[1] + y[2] * q[2]
    rows = list(q)
    for i in range(3):
        for j in range(3):
            rows += pieces(y[i] * q[j], 2)
    for i in range(3):
        rows += pieces(square * q[i] + y[i] * along, 3)
    rows += [zero] * (FIELD_ROWS - len(rows))
    for k, value in enumerate(rows):
        put(field, k, value)
    if left is None:
        return
    for k, value in enumerate([-2 * v for v in y] + pieces(square + EPS_SQ / 2, 3) + [one] * 3 + [zero] * 7):
        put(left, k, value)


def prepare_target(block, right):
    _, x = split_parts(block)
    one, zero = jnp.ones_like(x[0]), jnp.zeros_like(x[0])
    norm = pieces(x[0] * x[0] + x[1] * x[1] + x[2] * x[2] + EPS_SQ / 2, 3)
    for k, value in enumerate(x + [one] * 3 + norm + [zero] * 7):
        put(right, k, value)


def finish(block, sums):
    _, x = split_parts(block)
    mom = [get(sums, i) for i in range(3)]
    cross = [[get(sums, 3 + 2 * (3 * i + j)) + get(sums, 4 + 2 * (3 * i + j)) for j in range(3)] for i in range(3)]
    dot = x[0] * mom[0] + x[1] * mom[1] + x[2] * mom[2] - (cross[0][0] + cross[1][1] + cross[2][2])
    square = x[0] * x[0] + x[1] * x[1] + x[2] * x[2] + 2 * EPS_SQ
    out = []
    for i in range(3):
        mixed = sum(x[j] * (cross[i][j] + 2 * cross[j][i]) for j in range(3))
        tail = get(sums, 21 + 3 * i) + get(sums, 22 + 3 * i) + get(sums, 23 + 3 * i)
        out.append(((square * mom[i] + x[i] * dot - mixed) + tail) * STOKES_SCALE)
    return out


def near_kernel(ids_lane, first_ref, second_ref, near_first, out_hbm, to_second, sem, *scratch):
    own = first_ref.shape[0]
    near_first[...] = jnp.zeros_like(near_first)
    sets = scratch[: len(scratch) // 2], scratch[len(scratch) // 2 :]

    def load(ref, count, s):
        parts = [ref[half, pl.ds(s, count, stride=GROUP), :] for half in range(2)]
        return jnp.concatenate(parts, 1).astype(bf16)

    def apply(field, cube, dim, sums, s):
        total = lax.dot_general(
            load(field, FIELD_ROWS, s), cube, (((1,), (dim,)), ((), ())), preferred_element_type=f32
        )
        for half in range(2):
            sums[half, pl.ds(s, FIELD_ROWS, stride=GROUP), :] = total[:, half * 128 : (half + 1) * 128]

    def two_groups(g, carry):
        begun = []
        for k, (field_a, left, field_b, right, _, _) in enumerate(sets):
            rows = pl.ds(pl.multiple_of((2 * g + k) * GROUP, GROUP), GROUP)
            ids = second_ref[rows, ids_lane : ids_lane + 128].astype(f32)[:, :own]
            chosen = (ids == lax.broadcasted_iota(jnp.int32, (GROUP, own), 1).astype(f32)).astype(bf16)
            first = jnp.dot(chosen, first_ref[...], preferred_element_type=f32)
            second = second_ref[rows, : 6 * PANELS].astype(f32)
            prepare_source(first, field_a, left)
            prepare_source(second, field_b, None)
            prepare_target(second, right)
            begun.append((rows, chosen, first, second))

        for field_a, left, field_b, right, sums_a, sums_b in sets:
            for start in range(0, GROUP, BATCH):
                batch = range(start, start + BATCH)
                shifted = [
                    lax.dot_general(
                        load(left, POINT_ROWS, s),
                        load(right, POINT_ROWS, s),
                        (((0,), (0,)), ((), ())),
                        preferred_element_type=f32,
                    )
                    for s in batch
                ]
                cubes = []
                for value in shifted:
                    inv = lax.rsqrt(value)
                    cubes.append((inv * inv * inv).astype(bf16))
                for s, cube in zip(batch, cubes):
                    apply(field_a, cube, 0, sums_b, s)
                for s, cube in zip(batch, cubes):
                    apply(field_b, cube, 1, sums_a, s)

        for (rows, chosen, first, second), (*_, sums_a, sums_b) in zip(begun, sets):
            for i, value in enumerate(finish(second, sums_b)):
                to_second[rows, i * PANELS : (i + 1) * PANELS] = value
            pltpu.make_async_copy(to_second.at[rows], out_hbm.at[rows, pl.ds(0, 3 * PANELS)], sem).start()
            for i, value in enumerate(finish(first, sums_a)):
                for piece in pieces(value, 3):
                    near_first[:, i * PANELS : (i + 1) * PANELS] += lax.dot_general(
                        chosen, piece.astype(bf16), (((0,), (0,)), ((), ())), preferred_element_type=f32
                    )
        return carry

    lax.fori_loop(0, second_ref.shape[0] // (2 * GROUP), two_groups, 0)
    pltpu.make_async_copy(to_second, out_hbm.at[:, pl.ds(0, 3 * PANELS)], sem).wait()


def near_sums(first, second, ids_lane):
    slots = second.shape[0]
    vmem = pl.BlockSpec(memory_space=pltpu.VMEM)

    def rows(count):
        return pltpu.VMEM((2, count * GROUP, 128), f32)

    return pl.pallas_call(
        functools.partial(near_kernel, ids_lane),
        out_shape=[
            jax.ShapeDtypeStruct((first.shape[0], 3 * PANELS), f32),
            jax.ShapeDtypeStruct((slots, 3 * PANELS + 128), f32),
        ],
        in_specs=[vmem] * 2,
        out_specs=[vmem, pl.BlockSpec(memory_space=pltpu.HBM)],
        scratch_shapes=[pltpu.VMEM((slots, 3 * PANELS), f32), pltpu.SemaphoreType.DMA]
        + ([rows(FIELD_ROWS), rows(POINT_ROWS)] * 2 + [rows(FIELD_ROWS)] * 2) * 2,
        compiler_params=pltpu.CompilerParams(vmem_limit_bytes=32 << 20),
        cost_estimate=pl.CostEstimate(
            flops=slots * 2 * 2 * 64 * PANELS * PANELS, bytes_accessed=slots * 9216, transcendentals=0
        ),
    )(first, second)


def hits_kernel(parents, ends, hits):
    count = ends.shape[1]
    for m in range(parents.shape[1]):
        hits[:, m * count : (m + 1) * count] = (parents[:, m : m + 1] == ends[...]).astype(f32).astype(bf16)


def far_kernel(start, recv, hits, factors, out_hbm, out, sems):
    count = factors.shape[2]
    parts = hits.shape[1] // count
    rank = 128 // parts
    slots = recv.shape[0]
    found = jnp.zeros((128, parts * count), f32)
    for r in range(hits.shape[0] // slots):
        found += lax.dot_general(
            recv[:, start + 128 * r : start + 128 * (r + 1)],
            hits[r * slots : (r + 1) * slots, :],
            (((0,), (0,)), ((), ())),
            preferred_element_type=f32,
        )
    at_ends = sum(found[m * rank : (m + 1) * rank, m * count : (m + 1) * count] for m in range(parts))
    sent = jnp.sum(factors[...] * at_ends[None], axis=1)
    sent = jnp.concatenate([sent[:, count // 2 :], sent[:, : count // 2]], axis=1)
    zero = jnp.zeros_like(sent)
    table = [
        jnp.concatenate([piece if m == k else zero for k in range(parts)], axis=1)
        for piece in pieces(sent, 2)
        for m in range(parts)
    ]
    table = jnp.concatenate(table, axis=0).astype(bf16)
    copies = []
    for k in range(0, out.shape[0], 256):
        rows = pl.ds(k, 256)
        both = lax.dot_general(hits[rows, :], table, (((1,), (1,)), ((), ())), preferred_element_type=f32)
        out[rows, :] = both[:, :128] + both[:, 128:]
        copies.append(pltpu.make_async_copy(out.at[rows], out_hbm.at[rows], sems.at[len(copies)]))
        copies[-1].start()
    for copy in copies:
        copy.wait()


def own_lanes(own, rank):
    shape = (own, own * rank)
    return lax.broadcasted_iota(jnp.int32, shape, 1) // rank == lax.broadcasted_iota(jnp.int32, shape, 0)


def join_kernel(density, coords, data):
    panels = density.shape[2]
    for k in range(3):
        data[:, k * panels : (k + 1) * panels] = density[k]
        data[:, (3 + k) * panels : (4 + k) * panels] = coords[k]


def join(density, coords):
    own, parts, panels = density.shape
    vmem = pl.BlockSpec(memory_space=pltpu.VMEM)
    return pl.pallas_call(
        join_kernel,
        out_shape=jax.ShapeDtypeStruct((own, 2 * parts * panels), density.dtype),
        in_specs=[vmem] * 2,
        out_specs=vmem,
        compiler_params=pltpu.CompilerParams(vmem_limit_bytes=8 << 20),
    )(density.transpose(1, 0, 2), coords.transpose(1, 0, 2))


def start_kernel(
    count_hbm, pairs_hbm, density_hbm, basis_hbm, transfer_hbm, message, count, pairs, density, basis, transfer, sems
):
    own, rank = density.shape[1], transfer.shape[1]
    step = 256
    chunks = [pl.ds(k, step) for k in range(0, own * rank, step)]
    sources = [density_hbm] + [basis_hbm.at[c] for c in chunks] + [transfer_hbm, count_hbm, pairs_hbm]
    targets = [density] + [basis.at[c] for c in chunks] + [transfer, count, pairs]
    copies = [pltpu.make_async_copy(a, b, sems.at[k]) for k, (a, b) in enumerate(zip(sources, targets))]
    for copy in copies:
        copy.start()
    mine = own_lanes(own, rank)
    across = (((1,), (1,)), ((), ()))
    copies[0].wait()
    flat = jnp.concatenate([density[i] for i in range(3)], axis=1)
    folded = jnp.zeros((own, 128), f32)
    for k, chunk in enumerate(chunks):
        copies[1 + k].wait()
        every = lax.dot_general(flat, basis[chunk, :], across, preferred_element_type=f32)
        every = jnp.where(mine[:, k * step : (k + 1) * step], every, 0.0)
        folded += sum(every[:, m : m + 128] for m in range(0, step, 128))
    moments = sum(folded[:, k : k + rank] for k in range(0, 128, rank))
    copies[-3].wait()
    wide = jnp.concatenate(pieces(moments, 3), axis=0).astype(bf16)
    lifted = sum(
        lax.dot_general(wide, piece.astype(bf16), across, preferred_element_type=f32)
        for piece in pieces(transfer[...], 2)
    )
    lifted = lifted[:own] + lifted[own : 2 * own] + lifted[2 * own :]
    lifted = jnp.sum(jnp.where(mine, lifted, 0.0), axis=0, keepdims=True)
    lifted = jnp.concatenate([lifted[:, k : k + 128] for k in range(0, own * rank, 128)], axis=0)
    copies[-2].wait()
    copies[-1].wait()
    ids = lax.rem(pairs[...], own)
    live = lax.broadcasted_iota(jnp.int32, ids.shape, 1) < count[0, 0]
    ids = jnp.where(live, ids, -1).astype(f32)
    rows = message.shape[0]
    block = ids.shape[1] // rows
    for k in range(rows):
        turned = jnp.concatenate([ids[:, k * block :], ids[:, : k * block]], axis=1) if k else ids
        message[k] = jnp.concatenate([lifted, turned], axis=0)


def start(near_count, near_pairs, density, basis, transfer, rows):
    own, rank, width = basis.shape
    vmem, hbm = pl.BlockSpec(memory_space=pltpu.VMEM), pl.BlockSpec(memory_space=pltpu.HBM)
    return pl.pallas_call(
        start_kernel,
        out_shape=jax.ShapeDtypeStruct((rows, own * rank // 128 + 2, near_pairs.shape[1]), f32),
        in_specs=[hbm] * 5,
        out_specs=vmem,
        scratch_shapes=[
            pltpu.SMEM((1, 1), jnp.int32),
            pltpu.VMEM(near_pairs.shape, jnp.int32),
            pltpu.VMEM((3, own, width // 3), density.dtype),
            pltpu.VMEM((own * rank, width), basis.dtype),
            pltpu.VMEM((own * rank, rank), f32),
            pltpu.SemaphoreType.DMA((own * rank // 256 + 4,)),
        ],
        compiler_params=pltpu.CompilerParams(vmem_limit_bytes=60 << 20),
    )(
        near_count.reshape(1, 1),
        near_pairs,
        density.transpose(1, 0, 2),
        basis.reshape(own * rank, width),
        transfer.reshape(own * rank, rank),
    )


def pick_kernel(orders, place, from_row, data, message_hbm, back, message, sems):
    rows, lift_rows = from_row.shape[0], from_row.shape[1] - 2
    own, wide = data.shape
    slots = message.shape[0]
    seats = len(orders[0])
    per_pair = slots // seats
    half = seats // rows

    def send(begin, stop):
        lanes = pl.ds(begin, stop - begin)
        copy = pltpu.make_async_copy(message.at[:, lanes], message_hbm.at[:, lanes], sems.at[min(begin, 1)])
        copy.start()
        return copy

    for r in range(rows):
        lifted = from_row[r, :lift_rows, :]
        lanes = slice(wide + 128 * (r + 1), wide + 128 * (r + 2))
        message[:, lanes] = jnp.concatenate([lifted] * (slots // lift_rows), axis=0).astype(bf16)
    copies = [send(wide + 128, message.shape[1])]
    lane = lax.broadcasted_iota(jnp.int32, (1, 128), 1)
    triples = []
    for r in range(rows):
        first, second = from_row[r, lift_rows : lift_rows + 1, :], from_row[r, lift_rows + 1 :, :]
        same = (place[0] == r) & (half * place[0] + lane // per_pair == place[1]) & (first == second)
        triples.append(jnp.concatenate([first, second, jnp.where(same, -1.0, second)], axis=0))
    even, odd = (
        jnp.concatenate([triples[r][:, h * per_pair : (h + 1) * per_pair] for r, h in order], axis=1)
        for order in orders
    )
    ids = jnp.where(place[0] % 2 == 0, even, odd)
    back[...] = ids[2:]
    down = (((0,), (0,)), ((), ()))
    cluster = lax.broadcasted_iota(jnp.int32, (own, slots), 0).astype(f32)
    first, second = ((ids[k : k + 1] == cluster).astype(f32).astype(bf16) for k in range(2))
    message[:, :wide] = lax.dot_general(second, data[...], down, preferred_element_type=f32).astype(bf16)
    names = (lax.broadcasted_iota(jnp.int32, (own, 128), 0) + 1).astype(f32).astype(bf16)
    names = lax.dot_general(first, names, down, preferred_element_type=f32) - 1.0
    message[:, wide : wide + 128] = names.astype(bf16)
    copies.append(send(0, wide + 128))
    for copy in copies:
        copy.wait()


def pick(place, from_row, data, slots, orders):
    vmem = pl.BlockSpec(memory_space=pltpu.VMEM)
    wide = data.shape[1] + 128 * (1 + from_row.shape[0])
    return pl.pallas_call(
        functools.partial(pick_kernel, orders),
        out_shape=[jax.ShapeDtypeStruct((slots, wide), bf16), jax.ShapeDtypeStruct((1, slots), f32)],
        in_specs=[pl.BlockSpec(memory_space=pltpu.SMEM)] + [vmem] * 2,
        out_specs=[pl.BlockSpec(memory_space=pltpu.HBM), vmem],
        scratch_shapes=[pltpu.VMEM((slots, wide), bf16), pltpu.SemaphoreType.DMA((2,))],
        compiler_params=pltpu.CompilerParams(vmem_limit_bytes=8 << 20),
    )(place, from_row, data)


def end_kernel(back, returned, near_first, basis, transfer, out, velocity, sems):
    own, panels = velocity.shape[1:]
    rank = transfer.shape[1]
    mine = own_lanes(own, rank)
    lift_rows = own * rank // 128
    local = sum(returned[k : k + lift_rows, 3 * panels :] for k in range(0, returned.shape[0], lift_rows))
    local = jnp.concatenate([local[k : k + 1] for k in range(lift_rows)], axis=1)
    wide = jnp.concatenate(pieces(jnp.where(mine, local, 0.0), 3), axis=0).astype(bf16)
    coef = sum(
        jnp.dot(wide, piece.astype(bf16), preferred_element_type=f32) for piece in pieces(transfer[...], 3)
    )
    coef = coef[:own] + coef[own : 2 * own] + coef[2 * own :]
    coef = pieces(jnp.where(mine, jnp.concatenate([coef] * own, axis=1), 0.0), 3)
    coef = jnp.concatenate(coef, axis=0).astype(bf16)
    slot = lax.broadcasted_iota(jnp.int32, (own, back.shape[1]), 0).astype(f32)
    chosen = (back[...] == slot).astype(f32).astype(bf16)
    copies = []
    for i in range(3):
        lanes = slice(i * panels, (i + 1) * panels)
        far = jnp.dot(coef, basis[:, lanes], preferred_element_type=f32)
        total = far[:own] + far[own : 2 * own] + far[2 * own :]
        for piece in pieces(returned[:, lanes], 3):
            total += jnp.dot(chosen, piece.astype(bf16), preferred_element_type=f32)
        velocity[i] = near_first[:, lanes] + total
        copies.append(pltpu.make_async_copy(velocity.at[i], out.at[i], sems.at[i]))
        copies[-1].start()
    for copy in copies:
        copy.wait()


def end(back, returned, near_first, basis, transfer):
    own, rank, width = basis.shape
    shape = (3, own, width // 3)
    return pl.pallas_call(
        end_kernel,
        out_shape=jax.ShapeDtypeStruct(shape, f32),
        in_specs=[pl.BlockSpec(memory_space=pltpu.VMEM)] * 5,
        out_specs=pl.BlockSpec(memory_space=pltpu.HBM),
        scratch_shapes=[pltpu.VMEM(shape, f32), pltpu.SemaphoreType.DMA((3,))],
        compiler_params=pltpu.CompilerParams(vmem_limit_bytes=8 << 20),
    )(
        back,
        returned,
        near_first,
        basis.reshape(own * rank, width),
        transfer.reshape(own * rank, rank),
    ).transpose(1, 0, 2)


def seat(p, r, h, rows):
    hops = rows // 2
    near = (2 * (p % 2) + h, 2 * (p % 2) + (3 * h - 1))[r % 2] % hops
    return (r // 2 + hops // 2) % hops * hops + near


def shards(density, coords, basis, transfer, parent, near_pairs, near_count, far_pairs, coupling):
    own, _, panels = density.shape
    rank = basis.shape[1]
    rows, cols = lax.axis_size("row"), lax.axis_size("col")
    half = cols // rows
    slots = near_pairs.shape[1]
    vmem = pl.BlockSpec(memory_space=pltpu.VMEM)

    swap = [
        (r * cols + half * p + h, p * cols + seat(p, r, h, rows))
        for r in range(rows)
        for p in range(rows)
        for h in range(half)
    ]
    home = [(there, here) for here, there in swap]
    message = start(near_count, near_pairs, density, basis, transfer, rows)
    density, coords, message = lax.optimization_barrier((density, coords, message))
    from_row = lax.all_to_all(message, "row", 0, 0, tiled=True)
    data = join(density, coords)
    first_data = lax.ppermute(data, BOTH, swap)
    first_data, from_row = lax.optimization_barrier((first_data, from_row))

    place = jnp.stack([lax.axis_index("row"), lax.axis_index("col")])
    orders = [sorted((seat(p, r, h, rows), r, h) for r in range(rows) for h in range(half)) for p in range(2)]
    orders = [[(r, h) for _, r, h in order] for order in orders]
    message, back_ids = pick(place, from_row, data, slots, orders)
    second = lax.all_to_all(message, "col", 0, 0, tiled=True)
    ids_lane = 6 * panels

    factors = jnp.concatenate([coupling.transpose(1, 2, 0), coupling.transpose(2, 1, 0)], axis=2)
    parents, from_row = lax.optimization_barrier((parent.reshape(-1, 128 // rank), from_row))
    hits = pl.pallas_call(
        hits_kernel,
        out_shape=jax.ShapeDtypeStruct((rows * slots, far_pairs.size * (128 // rank)), bf16),
        in_specs=[vmem] * 2,
        out_specs=vmem,
        compiler_params=pltpu.CompilerParams(vmem_limit_bytes=16 << 20),
    )(parents, far_pairs[::-1].reshape(1, -1))
    partial = pl.pallas_call(
        functools.partial(far_kernel, ids_lane + 128),
        out_shape=jax.ShapeDtypeStruct((rows * slots, 128), f32),
        in_specs=[vmem] * 3,
        out_specs=pl.BlockSpec(memory_space=pltpu.HBM),
        scratch_shapes=[pltpu.VMEM((rows * slots, 128), f32), pltpu.SemaphoreType.DMA((rows * slots // 256,))],
        compiler_params=pltpu.CompilerParams(vmem_limit_bytes=16 << 20),
    )(second, hits, factors)
    first_data, partial = lax.optimization_barrier((first_data, partial))
    row_locals = lax.all_to_all(partial.reshape(rows, slots, 128), "row", 0, 0, tiled=True)

    near_first, to_second = near_sums(first_data, second, ids_lane)
    near_first = lax.ppermute(near_first, BOTH, home)
    message = lax.dynamic_update_slice(to_second, row_locals.sum(axis=0), (0, 3 * panels))
    returned = lax.all_to_all(message, "col", 0, 0, tiled=True)
    return end(back_ids, returned, near_first, basis, transfer)


def solution(mesh):
    placed = (
        P(BOTH, None, None),
        P(BOTH, None, None),
        P(BOTH, None, None),
        P(BOTH, None, None),
        P(),
        P(None, BOTH),
        P(BOTH),
        P(None, BOTH),
        P(BOTH, None, None),
    )
    return jax.shard_map(
        shards, mesh=mesh, in_specs=placed, out_specs=P(BOTH, None, None), check_vma=False
    )
```

```python
import functools
import math

import jax
import jax.numpy as jnp
from jax import lax
from jax.experimental import pallas as pl
from jax.experimental.pallas import tpu as pltpu
from jax.sharding import PartitionSpec as P

REG_EPS = 0.02
EPS_SQ = REG_EPS * REG_EPS
STOKES_SCALE = 1.0 / (8.0 * math.pi)
BOTH = ("row", "col")
GROUP = 16
BATCH = 8
GROUPS = 4
PANELS = 256
FIELD_ROWS = 32
POINT_ROWS = 16
f32, bf16 = jnp.float32, jnp.bfloat16


def pieces(value, count):
    out = []
    for _ in range(count):
        head = value.astype(bf16).astype(f32)
        out.append(head)
        value = value - head
    return out


def put(ref, row, value):
    for half in range(2):
        ref[half, row * GROUP : (row + 1) * GROUP, :] = value[:, half * 128 : (half + 1) * 128]


def get(ref, row):
    return jnp.concatenate([ref[half, row * GROUP : (row + 1) * GROUP, :] for half in range(2)], 1)


def split_parts(block):
    parts = [block[:, k * PANELS : (k + 1) * PANELS] for k in range(6)]
    return parts[:3], parts[3:]


def prepare_source(block, field, left):
    q, y = split_parts(block)
    one, zero = jnp.ones_like(q[0]), jnp.zeros_like(q[0])
    square = y[0] * y[0] + y[1] * y[1] + y[2] * y[2]
    along = y[0] * q[0] + y[1] * q[1] + y[2] * q[2]
    rows = list(q)
    for i in range(3):
        for j in range(3):
            rows += pieces(y[i] * q[j], 2)
    for i in range(3):
        rows += pieces(square * q[i] + y[i] * along, 3)
    rows += [zero] * (FIELD_ROWS - len(rows))
    for k, value in enumerate(rows):
        put(field, k, value)
    if left is None:
        return
    for k, value in enumerate([-2 * v for v in y] + pieces(square + EPS_SQ / 2, 3) + [one] * 3 + [zero] * 7):
        put(left, k, value)


def prepare_target(block, right):
    _, x = split_parts(block)
    one, zero = jnp.ones_like(x[0]), jnp.zeros_like(x[0])
    norm = pieces(x[0] * x[0] + x[1] * x[1] + x[2] * x[2] + EPS_SQ / 2, 3)
    for k, value in enumerate(x + [one] * 3 + norm + [zero] * 7):
        put(right, k, value)


def finish(block, sums):
    _, x = split_parts(block)
    mom = [get(sums, i) for i in range(3)]
    cross = [[get(sums, 3 + 2 * (3 * i + j)) + get(sums, 4 + 2 * (3 * i + j)) for j in range(3)] for i in range(3)]
    dot = x[0] * mom[0] + x[1] * mom[1] + x[2] * mom[2] - (cross[0][0] + cross[1][1] + cross[2][2])
    square = x[0] * x[0] + x[1] * x[1] + x[2] * x[2] + 2 * EPS_SQ
    out = []
    for i in range(3):
        mixed = sum(x[j] * (cross[i][j] + 2 * cross[j][i]) for j in range(3))
        tail = get(sums, 21 + 3 * i) + get(sums, 22 + 3 * i) + get(sums, 23 + 3 * i)
        out.append(((square * mom[i] + x[i] * dot - mixed) + tail) * STOKES_SCALE)
    return out


def near_kernel(ids_lane, first_ref, second_ref, near_first, out_hbm, to_second, sem, *scratch):
    own = first_ref.shape[0]
    near_first[...] = jnp.zeros_like(near_first)
    sets = [scratch[k : k + 6] for k in range(0, len(scratch), 6)]

    def load(ref, count, s):
        parts = [ref[half, pl.ds(s, count, stride=GROUP), :] for half in range(2)]
        return jnp.concatenate(parts, 1).astype(bf16)

    def apply(field, cube, dim, sums, s):
        total = lax.dot_general(
            load(field, FIELD_ROWS, s), cube, (((1,), (dim,)), ((), ())), preferred_element_type=f32
        )
        for half in range(2):
            sums[half, pl.ds(s, FIELD_ROWS, stride=GROUP), :] = total[:, half * 128 : (half + 1) * 128]

    def some_groups(g, carry):
        begun = []
        for k, (field_a, left, field_b, right, _, _) in enumerate(sets):
            rows = pl.ds(pl.multiple_of((len(sets) * g + k) * GROUP, GROUP), GROUP)
            ids = second_ref[rows, ids_lane : ids_lane + 128].astype(f32)[:, :own]
            chosen = (ids == lax.broadcasted_iota(jnp.int32, (GROUP, own), 1).astype(f32)).astype(bf16)
            first = jnp.dot(chosen, first_ref[...], preferred_element_type=f32)
            second = second_ref[rows, : 6 * PANELS].astype(f32)
            prepare_source(first, field_a, left)
            prepare_source(second, field_b, None)
            prepare_target(second, right)
            begun.append((rows, chosen, first, second))

        for field_a, left, field_b, right, sums_a, sums_b in sets:
            for start in range(0, GROUP, BATCH):
                batch = range(start, start + BATCH)
                shifted = [
                    lax.dot_general(
                        load(left, POINT_ROWS, s),
                        load(right, POINT_ROWS, s),
                        (((0,), (0,)), ((), ())),
                        preferred_element_type=f32,
                    )
                    for s in batch
                ]
                cubes = []
                for value in shifted:
                    inv = lax.rsqrt(value)
                    cubes.append((inv * inv * inv).astype(bf16))
                for s, cube in zip(batch, cubes):
                    apply(field_a, cube, 0, sums_b, s)
                for s, cube in zip(batch, cubes):
                    apply(field_b, cube, 1, sums_a, s)

        for (rows, chosen, first, second), (*_, sums_a, sums_b) in zip(begun, sets):
            for i, value in enumerate(finish(second, sums_b)):
                to_second[rows, i * PANELS : (i + 1) * PANELS] = value
            pltpu.make_async_copy(to_second.at[rows], out_hbm.at[rows, pl.ds(0, 3 * PANELS)], sem).start()
            for i, value in enumerate(finish(first, sums_a)):
                for piece in pieces(value, 3):
                    near_first[:, i * PANELS : (i + 1) * PANELS] += lax.dot_general(
                        chosen, piece.astype(bf16), (((0,), (0,)), ((), ())), preferred_element_type=f32
                    )
        return carry

    lax.fori_loop(0, second_ref.shape[0] // (len(sets) * GROUP), some_groups, 0)
    pltpu.make_async_copy(to_second, out_hbm.at[:, pl.ds(0, 3 * PANELS)], sem).wait()


def near_sums(first, second, ids_lane):
    slots = second.shape[0]
    vmem = pl.BlockSpec(memory_space=pltpu.VMEM)

    def rows(count):
        return pltpu.VMEM((2, count * GROUP, 128), f32)

    return pl.pallas_call(
        functools.partial(near_kernel, ids_lane),
        out_shape=[
            jax.ShapeDtypeStruct((first.shape[0], 3 * PANELS), f32),
            jax.ShapeDtypeStruct((slots, 3 * PANELS + 128), f32),
        ],
        in_specs=[vmem] * 2,
        out_specs=[vmem, pl.BlockSpec(memory_space=pltpu.HBM)],
        scratch_shapes=[pltpu.VMEM((slots, 3 * PANELS), f32), pltpu.SemaphoreType.DMA]
        + ([rows(FIELD_ROWS), rows(POINT_ROWS)] * 2 + [rows(FIELD_ROWS)] * 2) * GROUPS,
        compiler_params=pltpu.CompilerParams(vmem_limit_bytes=32 << 20),
        cost_estimate=pl.CostEstimate(
            flops=slots * 2 * 2 * 64 * PANELS * PANELS, bytes_accessed=slots * 9216, transcendentals=0
        ),
    )(first, second)


def hits_kernel(parents, ends, hits):
    count = ends.shape[1]
    for m in range(parents.shape[1]):
        hits[:, m * count : (m + 1) * count] = (parents[:, m : m + 1] == ends[...]).astype(f32).astype(bf16)


def far_kernel(start, recv, hits, factors, out_hbm, out, sems):
    count = factors.shape[2]
    parts = hits.shape[1] // count
    rank = 128 // parts
    slots = recv.shape[0]
    found = jnp.zeros((128, parts * count), f32)
    for r in range(hits.shape[0] // slots):
        found += lax.dot_general(
            recv[:, start + 128 * r : start + 128 * (r + 1)],
            hits[r * slots : (r + 1) * slots, :],
            (((0,), (0,)), ((), ())),
            preferred_element_type=f32,
        )
    at_ends = sum(found[m * rank : (m + 1) * rank, m * count : (m + 1) * count] for m in range(parts))
    sent = jnp.sum(factors[...] * at_ends[None], axis=1)
    sent = jnp.concatenate([sent[:, count // 2 :], sent[:, : count // 2]], axis=1)
    zero = jnp.zeros_like(sent)
    table = [
        jnp.concatenate([piece if m == k else zero for k in range(parts)], axis=1)
        for piece in pieces(sent, 2)
        for m in range(parts)
    ]
    table = jnp.concatenate(table, axis=0).astype(bf16)
    copies = []
    for k in range(0, out.shape[0], 256):
        rows = pl.ds(k, 256)
        both = lax.dot_general(hits[rows, :], table, (((1,), (1,)), ((), ())), preferred_element_type=f32)
        out[rows, :] = both[:, :128] + both[:, 128:]
        copies.append(pltpu.make_async_copy(out.at[rows], out_hbm.at[rows], sems.at[len(copies)]))
        copies[-1].start()
    for copy in copies:
        copy.wait()


def own_lanes(own, rank):
    shape = (own, own * rank)
    return lax.broadcasted_iota(jnp.int32, shape, 1) // rank == lax.broadcasted_iota(jnp.int32, shape, 0)


def join_kernel(density, coords, data):
    panels = density.shape[2]
    for k in range(3):
        data[:, k * panels : (k + 1) * panels] = density[k]
        data[:, (3 + k) * panels : (4 + k) * panels] = coords[k]


def join(density, coords):
    own, parts, panels = density.shape
    vmem = pl.BlockSpec(memory_space=pltpu.VMEM)
    return pl.pallas_call(
        join_kernel,
        out_shape=jax.ShapeDtypeStruct((own, 2 * parts * panels), density.dtype),
        in_specs=[vmem] * 2,
        out_specs=vmem,
        compiler_params=pltpu.CompilerParams(vmem_limit_bytes=8 << 20),
    )(density.transpose(1, 0, 2), coords.transpose(1, 0, 2))


def start_kernel(
    count_hbm, pairs_hbm, density_hbm, basis_hbm, transfer_hbm, message, count, pairs, density, basis, transfer, sems
):
    own, rank = density.shape[1], transfer.shape[1]
    step = 256
    chunks = [pl.ds(k, step) for k in range(0, own * rank, step)]
    sources = [density_hbm] + [basis_hbm.at[c] for c in chunks] + [transfer_hbm, count_hbm, pairs_hbm]
    targets = [density] + [basis.at[c] for c in chunks] + [transfer, count, pairs]
    copies = [pltpu.make_async_copy(a, b, sems.at[k]) for k, (a, b) in enumerate(zip(sources, targets))]
    for copy in copies:
        copy.start()
    mine = own_lanes(own, rank)
    across = (((1,), (1,)), ((), ()))
    copies[0].wait()
    flat = jnp.concatenate([density[i] for i in range(3)], axis=1)
    folded = jnp.zeros((own, 128), f32)
    for k, chunk in enumerate(chunks):
        copies[1 + k].wait()
        every = lax.dot_general(flat, basis[chunk, :], across, preferred_element_type=f32)
        every = jnp.where(mine[:, k * step : (k + 1) * step], every, 0.0)
        folded += sum(every[:, m : m + 128] for m in range(0, step, 128))
    moments = sum(folded[:, k : k + rank] for k in range(0, 128, rank))
    copies[-3].wait()
    wide = jnp.concatenate(pieces(moments, 3), axis=0).astype(bf16)
    lifted = sum(
        lax.dot_general(wide, piece.astype(bf16), across, preferred_element_type=f32)
        for piece in pieces(transfer[...], 2)
    )
    lifted = lifted[:own] + lifted[own : 2 * own] + lifted[2 * own :]
    lifted = jnp.sum(jnp.where(mine, lifted, 0.0), axis=0, keepdims=True)
    lifted = jnp.concatenate([lifted[:, k : k + 128] for k in range(0, own * rank, 128)], axis=0)
    copies[-2].wait()
    copies[-1].wait()
    ids = lax.rem(pairs[...], own)
    live = lax.broadcasted_iota(jnp.int32, ids.shape, 1) < count[0, 0]
    ids = jnp.where(live, ids, -1).astype(f32)
    rows = message.shape[0]
    block = ids.shape[1] // rows
    for k in range(rows):
        turned = jnp.concatenate([ids[:, k * block :], ids[:, : k * block]], axis=1) if k else ids
        message[k] = jnp.concatenate([lifted, turned], axis=0)


def start(near_count, near_pairs, density, basis, transfer, rows):
    own, rank, width = basis.shape
    vmem, hbm = pl.BlockSpec(memory_space=pltpu.VMEM), pl.BlockSpec(memory_space=pltpu.HBM)
    return pl.pallas_call(
        start_kernel,
        out_shape=jax.ShapeDtypeStruct((rows, own * rank // 128 + 2, near_pairs.shape[1]), f32),
        in_specs=[hbm] * 5,
        out_specs=vmem,
        scratch_shapes=[
            pltpu.SMEM((1, 1), jnp.int32),
            pltpu.VMEM(near_pairs.shape, jnp.int32),
            pltpu.VMEM((3, own, width // 3), density.dtype),
            pltpu.VMEM((own * rank, width), basis.dtype),
            pltpu.VMEM((own * rank, rank), f32),
            pltpu.SemaphoreType.DMA((own * rank // 256 + 4,)),
        ],
        compiler_params=pltpu.CompilerParams(vmem_limit_bytes=60 << 20),
    )(
        near_count.reshape(1, 1),
        near_pairs,
        density.transpose(1, 0, 2),
        basis.reshape(own * rank, width),
        transfer.reshape(own * rank, rank),
    )


def pick_kernel(orders, place, from_row, data, message_hbm, back, message, sems):
    rows, lift_rows = from_row.shape[0], from_row.shape[1] - 2
    own, wide = data.shape
    slots = message.shape[0]
    seats = len(orders[0])
    per_pair = slots // seats
    half = seats // rows

    def send(begin, stop):
        lanes = pl.ds(begin, stop - begin)
        copy = pltpu.make_async_copy(message.at[:, lanes], message_hbm.at[:, lanes], sems.at[min(begin, 1)])
        copy.start()
        return copy

    for r in range(rows):
        lifted = from_row[r, :lift_rows, :]
        lanes = slice(wide + 128 * (r + 1), wide + 128 * (r + 2))
        message[:, lanes] = jnp.concatenate([lifted] * (slots // lift_rows), axis=0).astype(bf16)
    copies = [send(wide + 128, message.shape[1])]
    lane = lax.broadcasted_iota(jnp.int32, (1, 128), 1)
    triples = []
    for r in range(rows):
        first, second = from_row[r, lift_rows : lift_rows + 1, :], from_row[r, lift_rows + 1 :, :]
        same = (place[0] == r) & (half * place[0] + lane // per_pair == place[1]) & (first == second)
        triples.append(jnp.concatenate([first, second, jnp.where(same, -1.0, second)], axis=0))
    even, odd = (
        jnp.concatenate([triples[r][:, h * per_pair : (h + 1) * per_pair] for r, h in order], axis=1)
        for order in orders
    )
    ids = jnp.where(place[0] % 2 == 0, even, odd)
    back[...] = ids[2:]
    down = (((0,), (0,)), ((), ()))
    cluster = lax.broadcasted_iota(jnp.int32, (own, slots), 0).astype(f32)
    first, second = ((ids[k : k + 1] == cluster).astype(f32).astype(bf16) for k in range(2))
    message[:, :wide] = lax.dot_general(second, data[...], down, preferred_element_type=f32).astype(bf16)
    names = (lax.broadcasted_iota(jnp.int32, (own, 128), 0) + 1).astype(f32).astype(bf16)
    names = lax.dot_general(first, names, down, preferred_element_type=f32) - 1.0
    message[:, wide : wide + 128] = names.astype(bf16)
    copies.append(send(0, wide + 128))
    for copy in copies:
        copy.wait()


def pick(place, from_row, data, slots, orders):
    vmem = pl.BlockSpec(memory_space=pltpu.VMEM)
    wide = data.shape[1] + 128 * (1 + from_row.shape[0])
    return pl.pallas_call(
        functools.partial(pick_kernel, orders),
        out_shape=[jax.ShapeDtypeStruct((slots, wide), bf16), jax.ShapeDtypeStruct((1, slots), f32)],
        in_specs=[pl.BlockSpec(memory_space=pltpu.SMEM)] + [vmem] * 2,
        out_specs=[pl.BlockSpec(memory_space=pltpu.HBM), vmem],
        scratch_shapes=[pltpu.VMEM((slots, wide), bf16), pltpu.SemaphoreType.DMA((2,))],
        compiler_params=pltpu.CompilerParams(vmem_limit_bytes=8 << 20),
    )(place, from_row, data)


def part_kernel(joined, parts):
    panels = parts.shape[2]
    for i in range(parts.shape[0]):
        parts[i] = joined[:, i * panels : (i + 1) * panels]


def part(joined):
    own, width = joined.shape
    vmem = pl.BlockSpec(memory_space=pltpu.VMEM)
    return pl.pallas_call(
        part_kernel,
        out_shape=jax.ShapeDtypeStruct((3, own, width // 3), joined.dtype),
        in_specs=[vmem],
        out_specs=vmem,
        compiler_params=pltpu.CompilerParams(vmem_limit_bytes=8 << 20),
        cost_estimate=pl.CostEstimate(flops=1 << 34, bytes_accessed=1 << 18, transcendentals=0),
    )(joined)


def end_kernel(back, returned, near_first, basis, transfer, out, velocity, sems):
    own, panels = velocity.shape[1:]
    rank = transfer.shape[1]
    mine = own_lanes(own, rank)
    lift_rows = own * rank // 128
    local = sum(returned[k : k + lift_rows, 3 * panels :] for k in range(0, returned.shape[0], lift_rows))
    local = jnp.concatenate([local[k : k + 1] for k in range(lift_rows)], axis=1)
    wide = jnp.concatenate(pieces(jnp.where(mine, local, 0.0), 3), axis=0).astype(bf16)
    coef = sum(
        jnp.dot(wide, piece.astype(bf16), preferred_element_type=f32) for piece in pieces(transfer[...], 3)
    )
    coef = coef[:own] + coef[own : 2 * own] + coef[2 * own :]
    coef = pieces(jnp.where(mine, jnp.concatenate([coef] * own, axis=1), 0.0), 3)
    coef = jnp.concatenate(coef, axis=0).astype(bf16)
    slot = lax.broadcasted_iota(jnp.int32, (own, back.shape[1]), 0).astype(f32)
    chosen = (back[...] == slot).astype(f32).astype(bf16)
    copies = []
    for i in range(3):
        lanes = slice(i * panels, (i + 1) * panels)
        far = jnp.dot(coef, basis[:, lanes], preferred_element_type=f32)
        total = far[:own] + far[own : 2 * own] + far[2 * own :]
        for piece in pieces(returned[:, lanes], 3):
            total += jnp.dot(chosen, piece.astype(bf16), preferred_element_type=f32)
        velocity[i] = near_first[i] + total
        copies.append(pltpu.make_async_copy(velocity.at[i], out.at[i], sems.at[i]))
        copies[-1].start()
    for copy in copies:
        copy.wait()


def end(back, returned, near_first, basis, transfer):
    own, rank, width = basis.shape
    shape = (3, own, width // 3)
    return pl.pallas_call(
        end_kernel,
        out_shape=jax.ShapeDtypeStruct(shape, f32),
        in_specs=[pl.BlockSpec(memory_space=pltpu.VMEM)] * 5,
        out_specs=pl.BlockSpec(memory_space=pltpu.HBM),
        scratch_shapes=[pltpu.VMEM(shape, f32), pltpu.SemaphoreType.DMA((3,))],
        compiler_params=pltpu.CompilerParams(vmem_limit_bytes=8 << 20),
    )(
        back,
        returned,
        near_first,
        basis.reshape(own * rank, width),
        transfer.reshape(own * rank, rank),
    ).transpose(1, 0, 2)


def seat(p, r, h, rows):
    hops = rows // 2
    near = (2 * (p % 2) + h, 2 * (p % 2) + (3 * h - 1))[r % 2] % hops
    return (r // 2 + hops // 2) % hops * hops + near


def shards(density, coords, basis, transfer, parent, near_pairs, near_count, far_pairs, coupling):
    own, _, panels = density.shape
    rank = basis.shape[1]
    rows, cols = lax.axis_size("row"), lax.axis_size("col")
    half = cols // rows
    slots = near_pairs.shape[1]
    vmem = pl.BlockSpec(memory_space=pltpu.VMEM)

    swap = [
        (r * cols + half * p + h, p * cols + seat(p, r, h, rows))
        for r in range(rows)
        for p in range(rows)
        for h in range(half)
    ]
    home = [(there, here) for here, there in swap]
    message = start(near_count, near_pairs, density, basis, transfer, rows)
    density, coords, message = lax.optimization_barrier((density, coords, message))
    from_row = lax.all_to_all(message, "row", 0, 0, tiled=True)
    data = join(density, coords)
    first_data = lax.ppermute(data, BOTH, swap)
    first_data, from_row = lax.optimization_barrier((first_data, from_row))

    place = jnp.stack([lax.axis_index("row"), lax.axis_index("col")])
    orders = [sorted((seat(p, r, h, rows), r, h) for r in range(rows) for h in range(half)) for p in range(2)]
    orders = [[(r, h) for _, r, h in order] for order in orders]
    message, back_ids = pick(place, from_row, data, slots, orders)
    second = lax.all_to_all(message, "col", 0, 0, tiled=True)
    ids_lane = 6 * panels

    factors = jnp.concatenate([coupling.transpose(1, 2, 0), coupling.transpose(2, 1, 0)], axis=2)
    parents, from_row = lax.optimization_barrier((parent.reshape(-1, 128 // rank), from_row))
    hits = pl.pallas_call(
        hits_kernel,
        out_shape=jax.ShapeDtypeStruct((rows * slots, far_pairs.size * (128 // rank)), bf16),
        in_specs=[vmem] * 2,
        out_specs=vmem,
        compiler_params=pltpu.CompilerParams(vmem_limit_bytes=16 << 20),
    )(parents, far_pairs[::-1].reshape(1, -1))
    partial = pl.pallas_call(
        functools.partial(far_kernel, ids_lane + 128),
        out_shape=jax.ShapeDtypeStruct((rows * slots, 128), f32),
        in_specs=[vmem] * 3,
        out_specs=pl.BlockSpec(memory_space=pltpu.HBM),
        scratch_shapes=[pltpu.VMEM((rows * slots, 128), f32), pltpu.SemaphoreType.DMA((rows * slots // 256,))],
        compiler_params=pltpu.CompilerParams(vmem_limit_bytes=16 << 20),
    )(second, hits, factors)
    first_data, partial = lax.optimization_barrier((first_data, partial))
    row_locals = lax.all_to_all(partial.reshape(rows, slots, 128), "row", 0, 0, tiled=True)

    near_first, to_second = near_sums(first_data, second, ids_lane)
    near_first = lax.ppermute(near_first, BOTH, home)
    message = lax.dynamic_update_slice(to_second, row_locals.sum(axis=0), (0, 3 * panels))
    returned = lax.all_to_all(message, "col", 0, 0, tiled=True)
    return end(back_ids, returned, part(near_first), basis, transfer)


def solution(mesh):
    placed = (
        P(BOTH, None, None),
        P(BOTH, None, None),
        P(BOTH, None, None),
        P(BOTH, None, None),
        P(),
        P(None, BOTH),
        P(BOTH),
        P(None, BOTH),
        P(BOTH, None, None),
    )
    return jax.shard_map(
        shards, mesh=mesh, in_specs=placed, out_specs=P(BOTH, None, None), check_vma=False
    )
```

```python
import functools
import math

import jax
import jax.numpy as jnp
from jax import lax
from jax.experimental import pallas as pl
from jax.experimental.pallas import tpu as pltpu
from jax.sharding import PartitionSpec as P

REG_EPS = 0.02
EPS_SQ = REG_EPS * REG_EPS
STOKES_SCALE = 1.0 / (8.0 * math.pi)
BOTH = ("row", "col")
GROUP = 16
BATCH = 8
GROUPS = 4
PANELS = 256
FIELD_ROWS = 32
POINT_ROWS = 16
f32, bf16 = jnp.float32, jnp.bfloat16


def pieces(value, count):
    out = []
    for _ in range(count):
        head = value.astype(bf16).astype(f32)
        out.append(head)
        value = value - head
    return out


def put(ref, row, value):
    for half in range(2):
        ref[half, row * GROUP : (row + 1) * GROUP, :] = value[:, half * 128 : (half + 1) * 128]


def get(ref, row):
    return jnp.concatenate([ref[half, row * GROUP : (row + 1) * GROUP, :] for half in range(2)], 1)


def split_parts(block):
    parts = [block[:, k * PANELS : (k + 1) * PANELS] for k in range(6)]
    return parts[:3], parts[3:]


def prepare_source(block, field, left):
    q, y = split_parts(block)
    one, zero = jnp.ones_like(q[0]), jnp.zeros_like(q[0])
    square = y[0] * y[0] + y[1] * y[1] + y[2] * y[2]
    along = y[0] * q[0] + y[1] * q[1] + y[2] * q[2]
    rows = list(q)
    for i in range(3):
        for j in range(3):
            rows += pieces(y[i] * q[j], 2)
    for i in range(3):
        rows += pieces(square * q[i] + y[i] * along, 3)
    rows += [zero] * (FIELD_ROWS - len(rows))
    for k, value in enumerate(rows):
        put(field, k, value)
    if left is None:
        return
    for k, value in enumerate([-2 * v for v in y] + pieces(square + EPS_SQ / 2, 3) + [one] * 3 + [zero] * 7):
        put(left, k, value)


def prepare_target(block, right):
    _, x = split_parts(block)
    one, zero = jnp.ones_like(x[0]), jnp.zeros_like(x[0])
    norm = pieces(x[0] * x[0] + x[1] * x[1] + x[2] * x[2] + EPS_SQ / 2, 3)
    for k, value in enumerate(x + [one] * 3 + norm + [zero] * 7):
        put(right, k, value)


def finish(block, sums):
    _, x = split_parts(block)
    mom = [get(sums, i) for i in range(3)]
    cross = [[get(sums, 3 + 2 * (3 * i + j)) + get(sums, 4 + 2 * (3 * i + j)) for j in range(3)] for i in range(3)]
    dot = x[0] * mom[0] + x[1] * mom[1] + x[2] * mom[2] - (cross[0][0] + cross[1][1] + cross[2][2])
    square = x[0] * x[0] + x[1] * x[1] + x[2] * x[2] + 2 * EPS_SQ
    out = []
    for i in range(3):
        mixed = sum(x[j] * (cross[i][j] + 2 * cross[j][i]) for j in range(3))
        tail = get(sums, 21 + 3 * i) + get(sums, 22 + 3 * i) + get(sums, 23 + 3 * i)
        out.append(((square * mom[i] + x[i] * dot - mixed) + tail) * STOKES_SCALE)
    return out


def near_kernel(ids_lane, first_ref, second_ref, near_first, out_hbm, to_second, sem, *scratch):
    own = first_ref.shape[0]
    near_first[...] = jnp.zeros_like(near_first)
    sets = [scratch[k : k + 6] for k in range(0, len(scratch), 6)]

    def load(ref, count, s):
        parts = [ref[half, pl.ds(s, count, stride=GROUP), :] for half in range(2)]
        return jnp.concatenate(parts, 1).astype(bf16)

    def apply(field, cube, dim, sums, s):
        total = lax.dot_general(
            load(field, FIELD_ROWS, s), cube, (((1,), (dim,)), ((), ())), preferred_element_type=f32
        )
        for half in range(2):
            sums[half, pl.ds(s, FIELD_ROWS, stride=GROUP), :] = total[:, half * 128 : (half + 1) * 128]

    def some_groups(g, carry):
        begun = []
        for k, (field_a, left, field_b, right, _, _) in enumerate(sets):
            rows = pl.ds(pl.multiple_of((len(sets) * g + k) * GROUP, GROUP), GROUP)
            ids = second_ref[rows, ids_lane : ids_lane + 128].astype(f32)[:, :own]
            chosen = (ids == lax.broadcasted_iota(jnp.int32, (GROUP, own), 1).astype(f32)).astype(bf16)
            first = jnp.dot(chosen, first_ref[...], preferred_element_type=f32)
            second = second_ref[rows, : 6 * PANELS].astype(f32)
            prepare_source(first, field_a, left)
            prepare_source(second, field_b, None)
            prepare_target(second, right)
            begun.append((rows, chosen, first, second))

        for field_a, left, field_b, right, sums_a, sums_b in sets:
            for start in range(0, GROUP, BATCH):
                batch = range(start, start + BATCH)
                shifted = [
                    lax.dot_general(
                        load(left, POINT_ROWS, s),
                        load(right, POINT_ROWS, s),
                        (((0,), (0,)), ((), ())),
                        preferred_element_type=f32,
                    )
                    for s in batch
                ]
                cubes = []
                for value in shifted:
                    inv = lax.rsqrt(value)
                    cubes.append((inv * inv * inv).astype(bf16))
                for s, cube in zip(batch, cubes):
                    apply(field_a, cube, 0, sums_b, s)
                for s, cube in zip(batch, cubes):
                    apply(field_b, cube, 1, sums_a, s)

        for (rows, chosen, first, second), (*_, sums_a, sums_b) in zip(begun, sets):
            for i, value in enumerate(finish(second, sums_b)):
                to_second[rows, i * PANELS : (i + 1) * PANELS] = value
            pltpu.make_async_copy(to_second.at[rows], out_hbm.at[rows, pl.ds(0, 3 * PANELS)], sem).start()
            for i, value in enumerate(finish(first, sums_a)):
                for piece in pieces(value, 3):
                    near_first[:, i * PANELS : (i + 1) * PANELS] += lax.dot_general(
                        chosen, piece.astype(bf16), (((0,), (0,)), ((), ())), preferred_element_type=f32
                    )
        return carry

    lax.fori_loop(0, second_ref.shape[0] // (len(sets) * GROUP), some_groups, 0)
    pltpu.make_async_copy(to_second, out_hbm.at[:, pl.ds(0, 3 * PANELS)], sem).wait()


def near_sums(first, second, ids_lane):
    slots = second.shape[0]
    vmem = pl.BlockSpec(memory_space=pltpu.VMEM)

    def rows(count):
        return pltpu.VMEM((2, count * GROUP, 128), f32)

    return pl.pallas_call(
        functools.partial(near_kernel, ids_lane),
        out_shape=[
            jax.ShapeDtypeStruct((first.shape[0], 3 * PANELS), f32),
            jax.ShapeDtypeStruct((slots, 3 * PANELS + 128), f32),
        ],
        in_specs=[vmem] * 2,
        out_specs=[vmem, pl.BlockSpec(memory_space=pltpu.HBM)],
        scratch_shapes=[pltpu.VMEM((slots, 3 * PANELS), f32), pltpu.SemaphoreType.DMA]
        + ([rows(FIELD_ROWS), rows(POINT_ROWS)] * 2 + [rows(FIELD_ROWS)] * 2) * GROUPS,
        compiler_params=pltpu.CompilerParams(vmem_limit_bytes=32 << 20),
        cost_estimate=pl.CostEstimate(
            flops=slots * 2 * 2 * 64 * PANELS * PANELS, bytes_accessed=slots * 9216, transcendentals=0
        ),
    )(first, second)


def hits_kernel(parents, ends, hits):
    count = ends.shape[1]
    for m in range(parents.shape[1]):
        hits[:, m * count : (m + 1) * count] = (parents[:, m : m + 1] == ends[...]).astype(f32).astype(bf16)


def far_kernel(start, recv, hits, factors, out_hbm, out, sems):
    count = factors.shape[2]
    parts = hits.shape[1] // count
    rank = 128 // parts
    slots = recv.shape[0]
    found = jnp.zeros((128, parts * count), f32)
    for r in range(hits.shape[0] // slots):
        found += lax.dot_general(
            recv[:, start + 128 * r : start + 128 * (r + 1)],
            hits[r * slots : (r + 1) * slots, :],
            (((0,), (0,)), ((), ())),
            preferred_element_type=f32,
        )
    at_ends = sum(found[m * rank : (m + 1) * rank, m * count : (m + 1) * count] for m in range(parts))
    sent = jnp.sum(factors[...] * at_ends[None], axis=1)
    sent = jnp.concatenate([sent[:, count // 2 :], sent[:, : count // 2]], axis=1)
    zero = jnp.zeros_like(sent)
    table = [
        jnp.concatenate([piece if m == k else zero for k in range(parts)], axis=1)
        for piece in pieces(sent, 2)
        for m in range(parts)
    ]
    table = jnp.concatenate(table, axis=0).astype(bf16)
    copies = []
    for k in range(0, out.shape[0], 256):
        rows = pl.ds(k, 256)
        both = lax.dot_general(hits[rows, :], table, (((1,), (1,)), ((), ())), preferred_element_type=f32)
        out[rows, :] = both[:, :128] + both[:, 128:]
        copies.append(pltpu.make_async_copy(out.at[rows], out_hbm.at[rows], sems.at[len(copies)]))
        copies[-1].start()
    for copy in copies:
        copy.wait()


def own_lanes(own, rank):
    shape = (own, own * rank)
    return lax.broadcasted_iota(jnp.int32, shape, 1) // rank == lax.broadcasted_iota(jnp.int32, shape, 0)


def join_kernel(density, coords, data):
    panels = density.shape[2]
    for k in range(3):
        data[:, k * panels : (k + 1) * panels] = density[k]
        data[:, (3 + k) * panels : (4 + k) * panels] = coords[k]


def join(density, coords):
    own, parts, panels = density.shape
    vmem = pl.BlockSpec(memory_space=pltpu.VMEM)
    return pl.pallas_call(
        join_kernel,
        out_shape=jax.ShapeDtypeStruct((own, 2 * parts * panels), density.dtype),
        in_specs=[vmem] * 2,
        out_specs=vmem,
        compiler_params=pltpu.CompilerParams(vmem_limit_bytes=8 << 20),
    )(density.transpose(1, 0, 2), coords.transpose(1, 0, 2))


def start_kernel(
    count_hbm, pairs_hbm, density_hbm, basis_hbm, transfer_hbm, message, count, pairs, density, basis, transfer, sems
):
    own, rank = density.shape[1], transfer.shape[1]
    step = 256
    chunks = [pl.ds(k, step) for k in range(0, own * rank, step)]
    sources = [density_hbm] + [basis_hbm.at[c] for c in chunks] + [transfer_hbm, count_hbm, pairs_hbm]
    targets = [density] + [basis.at[c] for c in chunks] + [transfer, count, pairs]
    copies = [pltpu.make_async_copy(a, b, sems.at[k]) for k, (a, b) in enumerate(zip(sources, targets))]
    for copy in copies:
        copy.start()
    mine = own_lanes(own, rank)
    across = (((1,), (1,)), ((), ()))
    copies[0].wait()
    flat = jnp.concatenate([density[i] for i in range(3)], axis=1)
    folded = jnp.zeros((own, 128), f32)
    for k, chunk in enumerate(chunks):
        copies[1 + k].wait()
        every = lax.dot_general(flat, basis[chunk, :], across, preferred_element_type=f32)
        every = jnp.where(mine[:, k * step : (k + 1) * step], every, 0.0)
        folded += sum(every[:, m : m + 128] for m in range(0, step, 128))
    moments = sum(folded[:, k : k + rank] for k in range(0, 128, rank))
    copies[-3].wait()
    wide = jnp.concatenate(pieces(moments, 3), axis=0).astype(bf16)
    lifted = sum(
        lax.dot_general(wide, piece.astype(bf16), across, preferred_element_type=f32)
        for piece in pieces(transfer[...], 2)
    )
    lifted = lifted[:own] + lifted[own : 2 * own] + lifted[2 * own :]
    lifted = jnp.sum(jnp.where(mine, lifted, 0.0), axis=0, keepdims=True)
    lifted = jnp.concatenate([lifted[:, k : k + 128] for k in range(0, own * rank, 128)], axis=0)
    copies[-2].wait()
    copies[-1].wait()
    ids = lax.rem(pairs[...], own)
    live = lax.broadcasted_iota(jnp.int32, ids.shape, 1) < count[0, 0]
    ids = jnp.where(live, ids, -1).astype(f32)
    rows = message.shape[0]
    block = ids.shape[1] // rows
    for k in range(rows):
        turned = jnp.concatenate([ids[:, k * block :], ids[:, : k * block]], axis=1) if k else ids
        message[k] = jnp.concatenate([lifted, turned], axis=0)


def start(near_count, near_pairs, density, basis, transfer, rows):
    own, rank, width = basis.shape
    vmem, hbm = pl.BlockSpec(memory_space=pltpu.VMEM), pl.BlockSpec(memory_space=pltpu.HBM)
    return pl.pallas_call(
        start_kernel,
        out_shape=jax.ShapeDtypeStruct((rows, own * rank // 128 + 2, near_pairs.shape[1]), f32),
        in_specs=[hbm] * 5,
        out_specs=vmem,
        scratch_shapes=[
            pltpu.SMEM((1, 1), jnp.int32),
            pltpu.VMEM(near_pairs.shape, jnp.int32),
            pltpu.VMEM((3, own, width // 3), density.dtype),
            pltpu.VMEM((own * rank, width), basis.dtype),
            pltpu.VMEM((own * rank, rank), f32),
            pltpu.SemaphoreType.DMA((own * rank // 256 + 4,)),
        ],
        compiler_params=pltpu.CompilerParams(vmem_limit_bytes=60 << 20),
    )(
        near_count.reshape(1, 1),
        near_pairs,
        density.transpose(1, 0, 2),
        basis.reshape(own * rank, width),
        transfer.reshape(own * rank, rank),
    )


def pick_kernel(orders, place, from_row, data, message_hbm, back, message, sems):
    rows, lift_rows = from_row.shape[0], from_row.shape[1] - 2
    own, wide = data.shape
    slots = message.shape[0]
    seats = len(orders[0])
    per_pair = slots // seats
    half = seats // rows

    def send(begin, stop):
        lanes = pl.ds(begin, stop - begin)
        copy = pltpu.make_async_copy(message.at[:, lanes], message_hbm.at[:, lanes], sems.at[min(begin, 1)])
        copy.start()
        return copy

    for r in range(rows):
        lifted = from_row[r, :lift_rows, :]
        lanes = slice(wide + 128 * (r + 1), wide + 128 * (r + 2))
        message[:, lanes] = jnp.concatenate([lifted] * (slots // lift_rows), axis=0).astype(bf16)
    copies = [send(wide + 128, message.shape[1])]
    lane = lax.broadcasted_iota(jnp.int32, (1, 128), 1)
    triples = []
    for r in range(rows):
        first, second = from_row[r, lift_rows : lift_rows + 1, :], from_row[r, lift_rows + 1 :, :]
        same = (place[0] == r) & (half * place[0] + lane // per_pair == place[1]) & (first == second)
        triples.append(jnp.concatenate([first, second, jnp.where(same, -1.0, second)], axis=0))
    even, odd = (
        jnp.concatenate([triples[r][:, h * per_pair : (h + 1) * per_pair] for r, h in order], axis=1)
        for order in orders
    )
    ids = jnp.where(place[0] % 2 == 0, even, odd)
    back[...] = ids[2:]
    down = (((0,), (0,)), ((), ()))
    cluster = lax.broadcasted_iota(jnp.int32, (own, slots), 0).astype(f32)
    first, second = ((ids[k : k + 1] == cluster).astype(f32).astype(bf16) for k in range(2))
    message[:, :wide] = lax.dot_general(second, data[...], down, preferred_element_type=f32).astype(bf16)
    names = (lax.broadcasted_iota(jnp.int32, (own, 128), 0) + 1).astype(f32).astype(bf16)
    names = lax.dot_general(first, names, down, preferred_element_type=f32) - 1.0
    message[:, wide : wide + 128] = names.astype(bf16)
    copies.append(send(0, wide + 128))
    for copy in copies:
        copy.wait()


def pick(place, from_row, data, slots, orders):
    vmem = pl.BlockSpec(memory_space=pltpu.VMEM)
    wide = data.shape[1] + 128 * (1 + from_row.shape[0])
    return pl.pallas_call(
        functools.partial(pick_kernel, orders),
        out_shape=[jax.ShapeDtypeStruct((slots, wide), bf16), jax.ShapeDtypeStruct((1, slots), f32)],
        in_specs=[pl.BlockSpec(memory_space=pltpu.SMEM)] + [vmem] * 2,
        out_specs=[pl.BlockSpec(memory_space=pltpu.HBM), vmem],
        scratch_shapes=[pltpu.VMEM((slots, wide), bf16), pltpu.SemaphoreType.DMA((2,))],
        compiler_params=pltpu.CompilerParams(vmem_limit_bytes=8 << 20),
    )(place, from_row, data)


def keep_kernel(joined, kept):
    kept[...] = joined[...]


def keep(joined, cost):
    vmem = pl.BlockSpec(memory_space=pltpu.VMEM)
    return pl.pallas_call(
        keep_kernel,
        out_shape=jax.ShapeDtypeStruct(joined.shape, joined.dtype),
        in_specs=[vmem],
        out_specs=vmem,
        compiler_params=pltpu.CompilerParams(vmem_limit_bytes=8 << 20),
        cost_estimate=pl.CostEstimate(flops=cost, bytes_accessed=1 << 18, transcendentals=0),
    )(joined)


def part_kernel(joined, parts):
    panels = parts.shape[2]
    for i in range(parts.shape[0]):
        parts[i] = joined[:, i * panels : (i + 1) * panels]


def part(joined):
    own, width = joined.shape
    vmem = pl.BlockSpec(memory_space=pltpu.VMEM)
    return pl.pallas_call(
        part_kernel,
        out_shape=jax.ShapeDtypeStruct((3, own, width // 3), joined.dtype),
        in_specs=[vmem],
        out_specs=vmem,
        compiler_params=pltpu.CompilerParams(vmem_limit_bytes=8 << 20),
        cost_estimate=pl.CostEstimate(flops=1 << 34, bytes_accessed=1 << 18, transcendentals=0),
    )(joined)


def end_kernel(back, returned, near_first, basis, transfer, out, velocity, sems):
    own, panels = velocity.shape[1:]
    rank = transfer.shape[1]
    mine = own_lanes(own, rank)
    lift_rows = own * rank // 128
    local = sum(returned[k : k + lift_rows, 3 * panels :] for k in range(0, returned.shape[0], lift_rows))
    local = jnp.concatenate([local[k : k + 1] for k in range(lift_rows)], axis=1)
    wide = jnp.concatenate(pieces(jnp.where(mine, local, 0.0), 3), axis=0).astype(bf16)
    coef = sum(
        jnp.dot(wide, piece.astype(bf16), preferred_element_type=f32) for piece in pieces(transfer[...], 3)
    )
    coef = coef[:own] + coef[own : 2 * own] + coef[2 * own :]
    coef = pieces(jnp.where(mine, jnp.concatenate([coef] * own, axis=1), 0.0), 3)
    coef = jnp.concatenate(coef, axis=0).astype(bf16)
    slot = lax.broadcasted_iota(jnp.int32, (own, back.shape[1]), 0).astype(f32)
    chosen = (back[...] == slot).astype(f32).astype(bf16)
    copies = []
    for i in range(3):
        lanes = slice(i * panels, (i + 1) * panels)
        far = jnp.dot(coef, basis[:, lanes], preferred_element_type=f32)
        total = far[:own] + far[own : 2 * own] + far[2 * own :]
        for piece in pieces(returned[:, lanes], 3):
            total += jnp.dot(chosen, piece.astype(bf16), preferred_element_type=f32)
        velocity[i] = near_first[i] + total
        copies.append(pltpu.make_async_copy(velocity.at[i], out.at[i], sems.at[i]))
        copies[-1].start()
    for copy in copies:
        copy.wait()


def end(back, returned, near_first, basis, transfer):
    own, rank, width = basis.shape
    shape = (3, own, width // 3)
    return pl.pallas_call(
        end_kernel,
        out_shape=jax.ShapeDtypeStruct(shape, f32),
        in_specs=[pl.BlockSpec(memory_space=pltpu.VMEM)] * 5,
        out_specs=pl.BlockSpec(memory_space=pltpu.HBM),
        scratch_shapes=[pltpu.VMEM(shape, f32), pltpu.SemaphoreType.DMA((3,))],
        compiler_params=pltpu.CompilerParams(vmem_limit_bytes=8 << 20),
    )(
        back,
        returned,
        near_first,
        basis.reshape(own * rank, width),
        transfer.reshape(own * rank, rank),
    ).transpose(1, 0, 2)


def seat(p, r, h, rows):
    hops = rows // 2
    near = (2 * (p % 2) + h, 2 * (p % 2) + (3 * h - 1))[r % 2] % hops
    return (r // 2 + hops // 2) % hops * hops + near


def shards(density, coords, basis, transfer, parent, near_pairs, near_count, far_pairs, coupling):
    own, _, panels = density.shape
    rank = basis.shape[1]
    rows, cols = lax.axis_size("row"), lax.axis_size("col")
    half = cols // rows
    slots = near_pairs.shape[1]
    vmem = pl.BlockSpec(memory_space=pltpu.VMEM)

    swap = [
        (r * cols + half * p + h, p * cols + seat(p, r, h, rows))
        for r in range(rows)
        for p in range(rows)
        for h in range(half)
    ]
    home = [(there, here) for here, there in swap]
    message = start(near_count, near_pairs, density, basis, transfer, rows)
    density, coords, message = lax.optimization_barrier((density, coords, message))
    from_row = lax.all_to_all(message, "row", 0, 0, tiled=True)
    data = join(density, coords)
    first_data = lax.ppermute(data, BOTH, swap)

    place = jnp.stack([lax.axis_index("row"), lax.axis_index("col")])
    orders = [sorted((seat(p, r, h, rows), r, h) for r in range(rows) for h in range(half)) for p in range(2)]
    orders = [[(r, h) for _, r, h in order] for order in orders]
    message, back_ids = pick(place, from_row, data, slots, orders)
    second = lax.all_to_all(message, "col", 0, 0, tiled=True)
    ids_lane = 6 * panels

    factors = jnp.concatenate([coupling.transpose(1, 2, 0), coupling.transpose(2, 1, 0)], axis=2)
    parents, from_row = lax.optimization_barrier((parent.reshape(-1, 128 // rank), from_row))
    hits = pl.pallas_call(
        hits_kernel,
        out_shape=jax.ShapeDtypeStruct((rows * slots, far_pairs.size * (128 // rank)), bf16),
        in_specs=[vmem] * 2,
        out_specs=vmem,
        compiler_params=pltpu.CompilerParams(vmem_limit_bytes=16 << 20),
    )(parents, far_pairs[::-1].reshape(1, -1))
    partial = pl.pallas_call(
        functools.partial(far_kernel, ids_lane + 128),
        out_shape=jax.ShapeDtypeStruct((rows * slots, 128), f32),
        in_specs=[vmem] * 3,
        out_specs=pl.BlockSpec(memory_space=pltpu.HBM),
        scratch_shapes=[pltpu.VMEM((rows * slots, 128), f32), pltpu.SemaphoreType.DMA((rows * slots // 256,))],
        compiler_params=pltpu.CompilerParams(vmem_limit_bytes=16 << 20),
    )(second, hits, factors)
    first_data = keep(first_data, 1 << 34)
    first_data, partial = lax.optimization_barrier((first_data, partial))
    row_locals = lax.all_to_all(partial.reshape(rows, slots, 128), "row", 0, 0, tiled=True)

    near_first, to_second = near_sums(first_data, second, ids_lane)
    near_first = lax.ppermute(near_first, BOTH, home)
    message = lax.dynamic_update_slice(to_second, row_locals.sum(axis=0), (0, 3 * panels))
    returned = lax.all_to_all(message, "col", 0, 0, tiled=True)
    return end(back_ids, returned, part(near_first), basis, transfer)


def solution(mesh):
    placed = (
        P(BOTH, None, None),
        P(BOTH, None, None),
        P(BOTH, None, None),
        P(BOTH, None, None),
        P(),
        P(None, BOTH),
        P(BOTH),
        P(None, BOTH),
        P(BOTH, None, None),
    )
    return jax.shard_map(
        shards, mesh=mesh, in_specs=placed, out_specs=P(BOTH, None, None), check_vma=False
    )
```

```python
import functools
import math

import jax
import jax.numpy as jnp
from jax import lax
from jax.experimental import pallas as pl
from jax.experimental.pallas import tpu as pltpu
from jax.sharding import PartitionSpec as P

REG_EPS = 0.02
EPS_SQ = REG_EPS * REG_EPS
STOKES_SCALE = 1.0 / (8.0 * math.pi)
BOTH = ("row", "col")
GROUP = 16
BATCH = 8
GROUPS = 8
PANELS = 256
FIELD_ROWS = 32
POINT_ROWS = 16
f32, bf16 = jnp.float32, jnp.bfloat16


def pieces(value, count):
    out = []
    for _ in range(count):
        head = value.astype(bf16).astype(f32)
        out.append(head)
        value = value - head
    return out


def put(ref, row, value):
    for half in range(2):
        ref[half, row * GROUP : (row + 1) * GROUP, :] = value[:, half * 128 : (half + 1) * 128]


def get(ref, row):
    return jnp.concatenate([ref[half, row * GROUP : (row + 1) * GROUP, :] for half in range(2)], 1)


def split_parts(block):
    parts = [block[:, k * PANELS : (k + 1) * PANELS] for k in range(6)]
    return parts[:3], parts[3:]


def prepare_source(block, field, left):
    q, y = split_parts(block)
    one, zero = jnp.ones_like(q[0]), jnp.zeros_like(q[0])
    square = y[0] * y[0] + y[1] * y[1] + y[2] * y[2]
    along = y[0] * q[0] + y[1] * q[1] + y[2] * q[2]
    rows = list(q)
    for i in range(3):
        for j in range(3):
            rows += pieces(y[i] * q[j], 2)
    for i in range(3):
        rows += pieces(square * q[i] + y[i] * along, 3)
    rows += [zero] * (FIELD_ROWS - len(rows))
    for k, value in enumerate(rows):
        put(field, k, value)
    if left is None:
        return
    for k, value in enumerate([-2 * v for v in y] + pieces(square + EPS_SQ / 2, 3) + [one] * 3 + [zero] * 7):
        put(left, k, value)


def prepare_target(block, right):
    _, x = split_parts(block)
    one, zero = jnp.ones_like(x[0]), jnp.zeros_like(x[0])
    norm = pieces(x[0] * x[0] + x[1] * x[1] + x[2] * x[2] + EPS_SQ / 2, 3)
    for k, value in enumerate(x + [one] * 3 + norm + [zero] * 7):
        put(right, k, value)


def finish(block, sums):
    _, x = split_parts(block)
    mom = [get(sums, i) for i in range(3)]
    cross = [[get(sums, 3 + 2 * (3 * i + j)) + get(sums, 4 + 2 * (3 * i + j)) for j in range(3)] for i in range(3)]
    dot = x[0] * mom[0] + x[1] * mom[1] + x[2] * mom[2] - (cross[0][0] + cross[1][1] + cross[2][2])
    square = x[0] * x[0] + x[1] * x[1] + x[2] * x[2] + 2 * EPS_SQ
    out = []
    for i in range(3):
        mixed = sum(x[j] * (cross[i][j] + 2 * cross[j][i]) for j in range(3))
        tail = get(sums, 21 + 3 * i) + get(sums, 22 + 3 * i) + get(sums, 23 + 3 * i)
        out.append(((square * mom[i] + x[i] * dot - mixed) + tail) * STOKES_SCALE)
    return out


def near_kernel(ids_lane, first_ref, second_ref, near_first, out_hbm, to_second, sem, *scratch):
    own = first_ref.shape[0]
    near_first[...] = jnp.zeros_like(near_first)
    sets = [scratch[k : k + 6] for k in range(0, len(scratch), 6)]

    def load(ref, count, s):
        parts = [ref[half, pl.ds(s, count, stride=GROUP), :] for half in range(2)]
        return jnp.concatenate(parts, 1).astype(bf16)

    def apply(field, cube, dim, sums, s):
        total = lax.dot_general(
            load(field, FIELD_ROWS, s), cube, (((1,), (dim,)), ((), ())), preferred_element_type=f32
        )
        for half in range(2):
            sums[half, pl.ds(s, FIELD_ROWS, stride=GROUP), :] = total[:, half * 128 : (half + 1) * 128]

    def some_groups(g, carry):
        begun = []
        for k, (field_a, left, field_b, right, _, _) in enumerate(sets):
            rows = pl.ds(pl.multiple_of((len(sets) * g + k) * GROUP, GROUP), GROUP)
            ids = second_ref[rows, ids_lane : ids_lane + 128].astype(f32)[:, :own]
            chosen = (ids == lax.broadcasted_iota(jnp.int32, (GROUP, own), 1).astype(f32)).astype(bf16)
            first = jnp.dot(chosen, first_ref[...], preferred_element_type=f32)
            second = second_ref[rows, : 6 * PANELS].astype(f32)
            prepare_source(first, field_a, left)
            prepare_source(second, field_b, None)
            prepare_target(second, right)
            begun.append((rows, chosen, first, second))

        for field_a, left, field_b, right, sums_a, sums_b in sets:
            for start in range(0, GROUP, BATCH):
                batch = range(start, start + BATCH)
                shifted = [
                    lax.dot_general(
                        load(left, POINT_ROWS, s),
                        load(right, POINT_ROWS, s),
                        (((0,), (0,)), ((), ())),
                        preferred_element_type=f32,
                    )
                    for s in batch
                ]
                cubes = []
                for value in shifted:
                    inv = lax.rsqrt(value)
                    cubes.append((inv * inv * inv).astype(bf16))
                for s, cube in zip(batch, cubes):
                    apply(field_a, cube, 0, sums_b, s)
                for s, cube in zip(batch, cubes):
                    apply(field_b, cube, 1, sums_a, s)

        for (rows, chosen, first, second), (*_, sums_a, sums_b) in zip(begun, sets):
            for i, value in enumerate(finish(second, sums_b)):
                to_second[rows, i * PANELS : (i + 1) * PANELS] = value
            pltpu.make_async_copy(to_second.at[rows], out_hbm.at[rows, pl.ds(0, 3 * PANELS)], sem).start()
            for i, value in enumerate(finish(first, sums_a)):
                for piece in pieces(value, 3):
                    near_first[:, i * PANELS : (i + 1) * PANELS] += lax.dot_general(
                        chosen, piece.astype(bf16), (((0,), (0,)), ((), ())), preferred_element_type=f32
                    )
        return carry

    lax.fori_loop(0, second_ref.shape[0] // (len(sets) * GROUP), some_groups, 0)
    pltpu.make_async_copy(to_second, out_hbm.at[:, pl.ds(0, 3 * PANELS)], sem).wait()


def near_sums(first, second, ids_lane):
    slots = second.shape[0]
    vmem = pl.BlockSpec(memory_space=pltpu.VMEM)

    def rows(count):
        return pltpu.VMEM((2, count * GROUP, 128), f32)

    return pl.pallas_call(
        functools.partial(near_kernel, ids_lane),
        out_shape=[
            jax.ShapeDtypeStruct((first.shape[0], 3 * PANELS), f32),
            jax.ShapeDtypeStruct((slots, 3 * PANELS + 128), f32),
        ],
        in_specs=[vmem] * 2,
        out_specs=[vmem, pl.BlockSpec(memory_space=pltpu.HBM)],
        scratch_shapes=[pltpu.VMEM((slots, 3 * PANELS), f32), pltpu.SemaphoreType.DMA]
        + ([rows(FIELD_ROWS), rows(POINT_ROWS)] * 2 + [rows(FIELD_ROWS)] * 2) * GROUPS,
        compiler_params=pltpu.CompilerParams(vmem_limit_bytes=32 << 20),
        cost_estimate=pl.CostEstimate(
            flops=slots * 2 * 2 * 64 * PANELS * PANELS, bytes_accessed=slots * 9216, transcendentals=0
        ),
    )(first, second)


def hits_kernel(parents, ends, hits):
    count = ends.shape[1]
    for m in range(parents.shape[1]):
        hits[:, m * count : (m + 1) * count] = (parents[:, m : m + 1] == ends[...]).astype(f32).astype(bf16)


def far_kernel(start, recv, hits, factors, out_hbm, out, sems):
    count = factors.shape[2]
    parts = hits.shape[1] // count
    rank = 128 // parts
    slots = recv.shape[0]
    found = jnp.zeros((128, parts * count), f32)
    for r in range(hits.shape[0] // slots):
        found += lax.dot_general(
            recv[:, start + 128 * r : start + 128 * (r + 1)],
            hits[r * slots : (r + 1) * slots, :],
            (((0,), (0,)), ((), ())),
            preferred_element_type=f32,
        )
    at_ends = sum(found[m * rank : (m + 1) * rank, m * count : (m + 1) * count] for m in range(parts))
    sent = jnp.sum(factors[...] * at_ends[None], axis=1)
    sent = jnp.concatenate([sent[:, count // 2 :], sent[:, : count // 2]], axis=1)
    zero = jnp.zeros_like(sent)
    table = [
        jnp.concatenate([piece if m == k else zero for k in range(parts)], axis=1)
        for piece in pieces(sent, 2)
        for m in range(parts)
    ]
    table = jnp.concatenate(table, axis=0).astype(bf16)
    copies = []
    for k in range(0, out.shape[0], 256):
        rows = pl.ds(k, 256)
        both = lax.dot_general(hits[rows, :], table, (((1,), (1,)), ((), ())), preferred_element_type=f32)
        out[rows, :] = both[:, :128] + both[:, 128:]
        copies.append(pltpu.make_async_copy(out.at[rows], out_hbm.at[rows], sems.at[len(copies)]))
        copies[-1].start()
    for copy in copies:
        copy.wait()


def own_lanes(own, rank):
    shape = (own, own * rank)
    return lax.broadcasted_iota(jnp.int32, shape, 1) // rank == lax.broadcasted_iota(jnp.int32, shape, 0)


def join_kernel(density, coords, data):
    panels = density.shape[2]
    for k in range(3):
        data[:, k * panels : (k + 1) * panels] = density[k]
        data[:, (3 + k) * panels : (4 + k) * panels] = coords[k]


def join(density, coords):
    own, parts, panels = density.shape
    vmem = pl.BlockSpec(memory_space=pltpu.VMEM)
    return pl.pallas_call(
        join_kernel,
        out_shape=jax.ShapeDtypeStruct((own, 2 * parts * panels), density.dtype),
        in_specs=[vmem] * 2,
        out_specs=vmem,
        compiler_params=pltpu.CompilerParams(vmem_limit_bytes=8 << 20),
    )(density.transpose(1, 0, 2), coords.transpose(1, 0, 2))


def start_kernel(
    count_hbm, pairs_hbm, density_hbm, basis_hbm, transfer_hbm, message, count, pairs, density, basis, transfer, sems
):
    own, rank = density.shape[1], transfer.shape[1]
    step = 256
    chunks = [pl.ds(k, step) for k in range(0, own * rank, step)]
    sources = [density_hbm] + [basis_hbm.at[c] for c in chunks] + [transfer_hbm, count_hbm, pairs_hbm]
    targets = [density] + [basis.at[c] for c in chunks] + [transfer, count, pairs]
    copies = [pltpu.make_async_copy(a, b, sems.at[k]) for k, (a, b) in enumerate(zip(sources, targets))]
    for copy in copies:
        copy.start()
    mine = own_lanes(own, rank)
    across = (((1,), (1,)), ((), ()))
    copies[0].wait()
    flat = jnp.concatenate([density[i] for i in range(3)], axis=1)
    folded = jnp.zeros((own, 128), f32)
    for k, chunk in enumerate(chunks):
        copies[1 + k].wait()
        every = lax.dot_general(flat, basis[chunk, :], across, preferred_element_type=f32)
        every = jnp.where(mine[:, k * step : (k + 1) * step], every, 0.0)
        folded += sum(every[:, m : m + 128] for m in range(0, step, 128))
    moments = sum(folded[:, k : k + rank] for k in range(0, 128, rank))
    copies[-3].wait()
    wide = jnp.concatenate(pieces(moments, 3), axis=0).astype(bf16)
    lifted = sum(
        lax.dot_general(wide, piece.astype(bf16), across, preferred_element_type=f32)
        for piece in pieces(transfer[...], 2)
    )
    lifted = lifted[:own] + lifted[own : 2 * own] + lifted[2 * own :]
    lifted = jnp.sum(jnp.where(mine, lifted, 0.0), axis=0, keepdims=True)
    lifted = jnp.concatenate([lifted[:, k : k + 128] for k in range(0, own * rank, 128)], axis=0)
    copies[-2].wait()
    copies[-1].wait()
    ids = lax.rem(pairs[...], own)
    live = lax.broadcasted_iota(jnp.int32, ids.shape, 1) < count[0, 0]
    ids = jnp.where(live, ids, -1).astype(f32)
    rows = message.shape[0]
    block = ids.shape[1] // rows
    for k in range(rows):
        turned = jnp.concatenate([ids[:, k * block :], ids[:, : k * block]], axis=1) if k else ids
        message[k] = jnp.concatenate([lifted, turned], axis=0)


def start(near_count, near_pairs, density, basis, transfer, rows):
    own, rank, width = basis.shape
    vmem, hbm = pl.BlockSpec(memory_space=pltpu.VMEM), pl.BlockSpec(memory_space=pltpu.HBM)
    return pl.pallas_call(
        start_kernel,
        out_shape=jax.ShapeDtypeStruct((rows, own * rank // 128 + 2, near_pairs.shape[1]), f32),
        in_specs=[hbm] * 5,
        out_specs=vmem,
        scratch_shapes=[
            pltpu.SMEM((1, 1), jnp.int32),
            pltpu.VMEM(near_pairs.shape, jnp.int32),
            pltpu.VMEM((3, own, width // 3), density.dtype),
            pltpu.VMEM((own * rank, width), basis.dtype),
            pltpu.VMEM((own * rank, rank), f32),
            pltpu.SemaphoreType.DMA((own * rank // 256 + 4,)),
        ],
        compiler_params=pltpu.CompilerParams(vmem_limit_bytes=60 << 20),
    )(
        near_count.reshape(1, 1),
        near_pairs,
        density.transpose(1, 0, 2),
        basis.reshape(own * rank, width),
        transfer.reshape(own * rank, rank),
    )


def pick_kernel(orders, place, from_row, data, message_hbm, back, message, sems):
    rows, lift_rows = from_row.shape[0], from_row.shape[1] - 2
    own, wide = data.shape
    slots = message.shape[0]
    seats = len(orders[0])
    per_pair = slots // seats
    half = seats // rows

    def send(begin, stop):
        lanes = pl.ds(begin, stop - begin)
        copy = pltpu.make_async_copy(message.at[:, lanes], message_hbm.at[:, lanes], sems.at[min(begin, 1)])
        copy.start()
        return copy

    for r in range(rows):
        lifted = from_row[r, :lift_rows, :]
        lanes = slice(wide + 128 * (r + 1), wide + 128 * (r + 2))
        message[:, lanes] = jnp.concatenate([lifted] * (slots // lift_rows), axis=0).astype(bf16)
    copies = [send(wide + 128, message.shape[1])]
    lane = lax.broadcasted_iota(jnp.int32, (1, 128), 1)
    triples = []
    for r in range(rows):
        first, second = from_row[r, lift_rows : lift_rows + 1, :], from_row[r, lift_rows + 1 :, :]
        same = (place[0] == r) & (half * place[0] + lane // per_pair == place[1]) & (first == second)
        triples.append(jnp.concatenate([first, second, jnp.where(same, -1.0, second)], axis=0))
    even, odd = (
        jnp.concatenate([triples[r][:, h * per_pair : (h + 1) * per_pair] for r, h in order], axis=1)
        for order in orders
    )
    ids = jnp.where(place[0] % 2 == 0, even, odd)
    back[...] = ids[2:]
    down = (((0,), (0,)), ((), ()))
    cluster = lax.broadcasted_iota(jnp.int32, (own, slots), 0).astype(f32)
    first, second = ((ids[k : k + 1] == cluster).astype(f32).astype(bf16) for k in range(2))
    message[:, :wide] = lax.dot_general(second, data[...], down, preferred_element_type=f32).astype(bf16)
    names = (lax.broadcasted_iota(jnp.int32, (own, 128), 0) + 1).astype(f32).astype(bf16)
    names = lax.dot_general(first, names, down, preferred_element_type=f32) - 1.0
    message[:, wide : wide + 128] = names.astype(bf16)
    copies.append(send(0, wide + 128))
    for copy in copies:
        copy.wait()


def pick(place, from_row, data, slots, orders):
    vmem = pl.BlockSpec(memory_space=pltpu.VMEM)
    wide = data.shape[1] + 128 * (1 + from_row.shape[0])
    return pl.pallas_call(
        functools.partial(pick_kernel, orders),
        out_shape=[jax.ShapeDtypeStruct((slots, wide), bf16), jax.ShapeDtypeStruct((1, slots), f32)],
        in_specs=[pl.BlockSpec(memory_space=pltpu.SMEM)] + [vmem] * 2,
        out_specs=[pl.BlockSpec(memory_space=pltpu.HBM), vmem],
        scratch_shapes=[pltpu.VMEM((slots, wide), bf16), pltpu.SemaphoreType.DMA((2,))],
        compiler_params=pltpu.CompilerParams(vmem_limit_bytes=8 << 20),
    )(place, from_row, data)


def keep_kernel(joined, kept):
    kept[...] = joined[...]


def keep(joined, cost):
    vmem = pl.BlockSpec(memory_space=pltpu.VMEM)
    return pl.pallas_call(
        keep_kernel,
        out_shape=jax.ShapeDtypeStruct(joined.shape, joined.dtype),
        in_specs=[vmem],
        out_specs=vmem,
        compiler_params=pltpu.CompilerParams(vmem_limit_bytes=8 << 20),
        cost_estimate=pl.CostEstimate(flops=cost, bytes_accessed=1 << 18, transcendentals=0),
    )(joined)


def part_kernel(joined, parts):
    panels = parts.shape[2]
    for i in range(parts.shape[0]):
        parts[i] = joined[:, i * panels : (i + 1) * panels]


def part(joined):
    own, width = joined.shape
    vmem = pl.BlockSpec(memory_space=pltpu.VMEM)
    return pl.pallas_call(
        part_kernel,
        out_shape=jax.ShapeDtypeStruct((3, own, width // 3), joined.dtype),
        in_specs=[vmem],
        out_specs=vmem,
        compiler_params=pltpu.CompilerParams(vmem_limit_bytes=8 << 20),
        cost_estimate=pl.CostEstimate(flops=1 << 34, bytes_accessed=1 << 18, transcendentals=0),
    )(joined)


def end_kernel(back, returned, near_first, basis, transfer, out, velocity, sems):
    own, panels = velocity.shape[1:]
    rank = transfer.shape[1]
    mine = own_lanes(own, rank)
    lift_rows = own * rank // 128
    local = sum(returned[k : k + lift_rows, 3 * panels :] for k in range(0, returned.shape[0], lift_rows))
    local = jnp.concatenate([local[k : k + 1] for k in range(lift_rows)], axis=1)
    wide = jnp.concatenate(pieces(jnp.where(mine, local, 0.0), 3), axis=0).astype(bf16)
    coef = sum(
        jnp.dot(wide, piece.astype(bf16), preferred_element_type=f32) for piece in pieces(transfer[...], 3)
    )
    coef = coef[:own] + coef[own : 2 * own] + coef[2 * own :]
    coef = pieces(jnp.where(mine, jnp.concatenate([coef] * own, axis=1), 0.0), 3)
    coef = jnp.concatenate(coef, axis=0).astype(bf16)
    slot = lax.broadcasted_iota(jnp.int32, (own, back.shape[1]), 0).astype(f32)
    chosen = (back[...] == slot).astype(f32).astype(bf16)
    copies = []
    for i in range(3):
        lanes = slice(i * panels, (i + 1) * panels)
        far = jnp.dot(coef, basis[:, lanes], preferred_element_type=f32)
        total = far[:own] + far[own : 2 * own] + far[2 * own :]
        for piece in pieces(returned[:, lanes], 3):
            total += jnp.dot(chosen, piece.astype(bf16), preferred_element_type=f32)
        velocity[i] = near_first[i] + total
        copies.append(pltpu.make_async_copy(velocity.at[i], out.at[i], sems.at[i]))
        copies[-1].start()
    for copy in copies:
        copy.wait()


def end(back, returned, near_first, basis, transfer):
    own, rank, width = basis.shape
    shape = (3, own, width // 3)
    return pl.pallas_call(
        end_kernel,
        out_shape=jax.ShapeDtypeStruct(shape, f32),
        in_specs=[pl.BlockSpec(memory_space=pltpu.VMEM)] * 5,
        out_specs=pl.BlockSpec(memory_space=pltpu.HBM),
        scratch_shapes=[pltpu.VMEM(shape, f32), pltpu.SemaphoreType.DMA((3,))],
        compiler_params=pltpu.CompilerParams(vmem_limit_bytes=8 << 20),
    )(
        back,
        returned,
        near_first,
        basis.reshape(own * rank, width),
        transfer.reshape(own * rank, rank),
    ).transpose(1, 0, 2)


def seat(p, r, h, rows):
    hops = rows // 2
    near = (2 * (p % 2) + h, 2 * (p % 2) + (3 * h - 1))[r % 2] % hops
    return (r // 2 + hops // 2) % hops * hops + near


def shards(density, coords, basis, transfer, parent, near_pairs, near_count, far_pairs, coupling):
    own, _, panels = density.shape
    rank = basis.shape[1]
    rows, cols = lax.axis_size("row"), lax.axis_size("col")
    half = cols // rows
    slots = near_pairs.shape[1]
    vmem = pl.BlockSpec(memory_space=pltpu.VMEM)

    swap = [
        (r * cols + half * p + h, p * cols + seat(p, r, h, rows))
        for r in range(rows)
        for p in range(rows)
        for h in range(half)
    ]
    home = [(there, here) for here, there in swap]
    message = start(near_count, near_pairs, density, basis, transfer, rows)
    density, coords, message = lax.optimization_barrier((density, coords, message))
    from_row = lax.all_to_all(message, "row", 0, 0, tiled=True)
    data = join(density, coords)
    first_data = lax.ppermute(data, BOTH, swap)

    place = jnp.stack([lax.axis_index("row"), lax.axis_index("col")])
    orders = [sorted((seat(p, r, h, rows), r, h) for r in range(rows) for h in range(half)) for p in range(2)]
    orders = [[(r, h) for _, r, h in order] for order in orders]
    message, back_ids = pick(place, from_row, data, slots, orders)
    second = lax.all_to_all(message, "col", 0, 0, tiled=True)
    ids_lane = 6 * panels

    factors = jnp.concatenate([coupling.transpose(1, 2, 0), coupling.transpose(2, 1, 0)], axis=2)
    parents, from_row = lax.optimization_barrier((parent.reshape(-1, 128 // rank), from_row))
    hits = pl.pallas_call(
        hits_kernel,
        out_shape=jax.ShapeDtypeStruct((rows * slots, far_pairs.size * (128 // rank)), bf16),
        in_specs=[vmem] * 2,
        out_specs=vmem,
        compiler_params=pltpu.CompilerParams(vmem_limit_bytes=16 << 20),
    )(parents, far_pairs[::-1].reshape(1, -1))
    partial = pl.pallas_call(
        functools.partial(far_kernel, ids_lane + 128),
        out_shape=jax.ShapeDtypeStruct((rows * slots, 128), f32),
        in_specs=[vmem] * 3,
        out_specs=pl.BlockSpec(memory_space=pltpu.HBM),
        scratch_shapes=[pltpu.VMEM((rows * slots, 128), f32), pltpu.SemaphoreType.DMA((rows * slots // 256,))],
        compiler_params=pltpu.CompilerParams(vmem_limit_bytes=16 << 20),
    )(second, hits, factors)
    first_data = keep(first_data, 1 << 34)
    first_data, partial = lax.optimization_barrier((first_data, partial))
    row_locals = lax.all_to_all(partial.reshape(rows, slots, 128), "row", 0, 0, tiled=True)

    near_first, to_second = near_sums(first_data, second, ids_lane)
    near_first = lax.ppermute(near_first, BOTH, home)
    message = lax.dynamic_update_slice(to_second, row_locals.sum(axis=0), (0, 3 * panels))
    returned = lax.all_to_all(message, "col", 0, 0, tiled=True)
    return end(back_ids, returned, part(near_first), basis, transfer)


def solution(mesh):
    placed = (
        P(BOTH, None, None),
        P(BOTH, None, None),
        P(BOTH, None, None),
        P(BOTH, None, None),
        P(),
        P(None, BOTH),
        P(BOTH),
        P(None, BOTH),
        P(BOTH, None, None),
    )
    return jax.shard_map(
        shards, mesh=mesh, in_specs=placed, out_specs=P(BOTH, None, None), check_vma=False
    )
```
